256 devices in a mesh: dp: 8 (over z), shard: 32 (over y, x, core).
Axes of the slice: x: 4, y: 4, z: 8, core: 2. Of those that a mesh axis runs over, the one named last changes fastest.
Arguments:
- latent: bfloat16 [65536, 512], P(('dp', 'shard')), may hold values from -24 to 24
- latent_grad: bfloat16 [65536, 8192], P(('dp', 'shard')), may hold values from -0.029907227 to 0.029907227
- row_counts: int32 [256], P(('dp', 'shard')), may hold values from 64 to 256, as said below
- momentum: float32 [512, 8192], P('shard'), may hold values from -1.8 to 1.8
Outputs:
- new_momentum: float32 [512, 8192], P('shard')
- update: bfloat16 [512, 8192], P('shard')
The draws below stay inside these ranges and needn't reach their ends.
Inputs may be any that keep to these rules, and one draw needn't show every extreme that they name: Live rows of one device are its first row_counts rows; some device has all 256 rows live.
All inputs are finite; a program needn't handle non-finite values.
Results may differ from the reference program's by a relative error of at most 0.0055.
Values may be sent and summed in bfloat16 or wider, within the bound.
No kernel may reach another device: no remote copies, remote signals or barrier semaphores. Data moves between devices by JAX's collectives and lax.ppermute only.
A program may use at most 128 MiB of HBM per device.

```python
import math
import jax
import jax.numpy as jnp
from jax import lax

HEADS = 32
KR = 512
SLOTS = 256
NS_STEPS = 5
HD = 256
TOKENS = 65536


def draw_row_counts(key, part):
    key = jax.random.fold_in(key, 3)
    first_key, second_key = jax.random.split(key)
    device_count = TOKENS // SLOTS
    counts = jax.random.randint(first_key, (device_count,), SLOTS // 4, SLOTS + 1)
    fullest = jax.random.randint(second_key, (), 0, device_count)
    return jnp.where(jnp.arange(device_count) == fullest, SLOTS, counts).astype(jnp.int32)


def raised(array, key, source, target, blocks, factor):
    def block_of(axis_at):
        return (jnp.arange(array.shape[axis_at]) // (array.shape[axis_at] // blocks)).reshape((-1,) + (1,) * (array.ndim - 1 - axis_at))

    first = jax.random.permutation(key, blocks)[block_of(target)]
    far = (block_of(target) + blocks // 2) % blocks
    return jnp.where((block_of(source) == first) | (block_of(source) == far), factor * array, array)


def block_scale(rng, dims, cuts, least, top_value):
    def one(axis_at, blocks):
        steps = jax.random.uniform(jax.random.fold_in(jax.random.fold_in(rng, 6), axis_at), (blocks,), jnp.float32, least / len(cuts), top_value / len(cuts))
        return jnp.repeat(jnp.exp(steps), dims[axis_at] // blocks).reshape((-1,) + (1,) * (len(dims) - axis_at - 1))

    level = one(*cuts[0])
    for cut in cuts[1:]:
        level = level * one(*cut)
    return level


def normal_values(rng, extent, deviation, bound, cuts=(), held_as=jnp.bfloat16):
    drawn = jax.random.normal(rng, extent, jnp.float32) * deviation
    if len(cuts) > 0:
        drawn = block_scale(rng, extent, cuts, -0.22, 0.18) * drawn
    return jnp.clip(drawn, min=-bound, max=bound).astype(held_as)


def gaussian_with(stream_key, dims, spread, bound, cuts, heavy, kind=jnp.bfloat16):
    values = spread * jax.random.normal(stream_key, dims, jnp.float32)
    if cuts:
        values = values * block_scale(stream_key, dims, cuts, -0.22, 0.18)
    return jnp.clip(raised(values, jax.random.fold_in(stream_key, 3), *heavy), -bound, bound).astype(kind)


def setup_inputs(seed: int = 0) -> dict:
    arg_keys = jax.random.split(jax.random.key(seed), 5)
    latent = gaussian_with(arg_keys[0], (TOKENS, KR), 1.0, 24.0, ((0, 256),), (0, 1, 256, 6.0))
    latent_grad = normal_values(arg_keys[1], (TOKENS, HEADS * HD), 0.005, 0.029907227, ((0, 256),))
    row_counts = draw_row_counts(jax.random.fold_in(arg_keys[4], 71), 0)
    momentum = normal_values(arg_keys[3], (KR, HEADS * HD), 0.3, 1.8, ((0, 32),), jnp.float32)
    return {"latent": latent, "latent_grad": latent_grad, "row_counts": row_counts, "momentum": momentum}


coef_a = 3.4445
coef_b = -4.775
coef_c = 2.0315
decay_rate = 0.95
highest = lax.Precision.HIGHEST

def orthogonal(matrices):
    frobenius = jnp.sqrt(lax.optimization_barrier(jnp.sum(matrices * matrices, axis=(1, 2), keepdims=True)))
    matrix = matrices / (frobenius + 1e-07)
    for iteration in range(NS_STEPS):
        gram_matrix = jnp.einsum('krc,krd->kcd', matrix, matrix, precision=highest)
        square = jnp.einsum('kcd,kde->kce', gram_matrix, gram_matrix, precision=highest)
        polynomial = coef_b * gram_matrix + coef_c * square
        matrix = coef_a * matrix + jnp.einsum('krc,kcd->krd', matrix, polynomial, precision=highest)
    return matrix

def reference(latent, latent_grad, row_counts, momentum):
    block_count = TOKENS // SLOTS
    blocked = latent.reshape(block_count, SLOTS, KR)
    grad_rows = latent_grad.reshape(block_count, SLOTS, HEADS * HD)
    live_rows = jnp.arange(SLOTS, dtype=jnp.int32)[None, :] < row_counts[:, None]
    masked = jnp.where(live_rows[:, :, None], blocked, jnp.zeros_like(blocked))

    def add_block(running, block_pair):
        rows_in, cotangent = block_pair
        product = lax.dot_general(rows_in, cotangent, (((0,), (0,)), ((), ())), preferred_element_type=jnp.float32)
        product = lax.optimization_barrier(product.astype(jnp.bfloat16))
        return (running + product.astype(jnp.float32), None)
    gradient, unused = lax.scan(add_block, jnp.zeros((KR, HEADS * HD), jnp.float32), (masked, grad_rows))
    renewed = decay_rate * momentum + gradient
    per_head = renewed.reshape(KR, HEADS, HD).transpose(1, 0, 2)

    def polish_one(single):
        return orthogonal(single[None])[0]
    polished = lax.map(polish_one, per_head)
    step_scale = 0.2 * math.sqrt(max(KR, HD))
    update = (step_scale * polished).astype(jnp.bfloat16).transpose(1, 0, 2).reshape(KR, HEADS * HD)
    return (renewed, update)
```

```python
import functools
import math

import jax
import jax.numpy as jnp
import numpy as np
from jax import lax
from jax.experimental import pallas as pl
from jax.experimental.pallas import tpu as pltpu
from jax.sharding import Mesh
from jax.sharding import PartitionSpec as P

HD = 256
NS_STEPS = 5
NZ, NY, NX, NC = 8, 4, 4, 2
AXES = ("z", "y", "x", "c")
PLANE = ("c", "y", "x")
COEF_A, COEF_B, COEF_C = 3.4445, -4.775, 2.0315
DECAY = 0.95
VMEM = 48 * 1024 * 1024
bf16, f32 = jnp.bfloat16, jnp.float32


SLOT_XOR = (0, 3, 1, 2)


def ring_place(coordinate, core):
    return (coordinate - core) % 4


def ring_coordinate(place, core):
    return (place + core) % 4


def pair_perm(axis, flip):
    pairs = []
    for z in range(NZ):
        for y in range(NY):
            for x in range(NX):
                for c in range(NC):
                    at = {"y": y, "x": x}
                    to = dict(at)
                    if axis == "c":
                        to_c = 1 - c
                    else:
                        to_c = c
                        to[axis] = ring_coordinate(ring_place(at[axis], c) ^ flip, c)
                    here = ((z * NY + y) * NX + x) * NC + c
                    there = ((z * NY + to["y"]) * NX + to["x"]) * NC + to_c
                    pairs.append((here, there))
    return pairs


def send(value, axis, flip=0):
    return lax.ppermute(value, AXES, pair_perm(axis, flip))


def partial_kernel(heads_x, heads_y, place, lat, mom, gx0, gx1, gy0, gy1, out_x, out_y, acc):
    half = acc.shape[0]
    row = place[1]
    for part, (g0, g1, out) in enumerate(((gx0, gx1, out_x), (gy0, gy1, out_y))):
        rows = slice(part * half, (part + 1) * half)
        p0 = jnp.dot(lat[0, rows, :], g0[...], preferred_element_type=f32)
        p1 = jnp.dot(lat[1, rows, :], g1[...], preferred_element_type=f32)
        acc[...] = p0.astype(bf16).astype(f32) + p1.astype(bf16).astype(f32)
        heads = heads_x if part == 0 else heads_y
        column = pl.multiple_of(heads[pl.program_id(0)] * HD, HD)

        @pl.when(row // half == part)
        def _():
            at = pl.ds(pl.multiple_of(row - part * half, 32), 32)
            acc[at, :] += (DECAY / NZ) * mom[:, pl.ds(column, HD)]

        out[0] = acc[...].astype(out.dtype)


def partial_tiles(heads_x, heads_y, place, lat, mom, grad_own, grad_other, dtype):
    tiles = heads_x.shape[0]
    tokens, features = lat.shape[2], lat.shape[1]
    half = features // 2

    def own(which):
        return lambda t, hx, hy, p: (0, p[0] * 16 + (hx if which == 0 else hy)[t])

    def other(which):
        return lambda t, hx, hy, p: (0, (hx if which == 0 else hy)[t])

    whole = lambda rank: lambda t, hx, hy, p: (0,) * rank
    block = pl.BlockSpec((1, half, HD), lambda t, hx, hy, p: (t, 0, 0))
    return pl.pallas_call(
        partial_kernel,
        out_shape=[jax.ShapeDtypeStruct((tiles, half, HD), dtype)] * 2,
        grid_spec=pltpu.PrefetchScalarGridSpec(
            num_scalar_prefetch=3,
            grid=(tiles,),
            in_specs=[
                pl.BlockSpec(lat.shape, whole(3)),
                pl.BlockSpec(mom.shape, whole(2)),
                pl.BlockSpec((tokens, HD), own(0)),
                pl.BlockSpec((tokens, HD), other(0)),
                pl.BlockSpec((tokens, HD), own(1)),
                pl.BlockSpec((tokens, HD), other(1)),
            ],
            out_specs=[block, block],
            scratch_shapes=[pltpu.VMEM((half, HD), f32)],
        ),
        compiler_params=pltpu.CompilerParams(vmem_limit_bytes=VMEM),
        cost_estimate=pl.CostEstimate(
            flops=2 * tiles * 2 * half * HD * 2 * tokens,
            bytes_accessed=tiles * 2 * (2 * tokens * HD * 2 + half * HD * 4),
            transcendentals=0,
        ),
    )(heads_x, heads_y, place, lat, mom, grad_own, grad_other, grad_own, grad_other)


def split(value):
    high = value.astype(bf16)
    return high, (value - high.astype(f32)).astype(bf16)


def product(a, b, dims):
    dot = functools.partial(
        lax.dot_general, dimension_numbers=(dims, ((), ())), preferred_element_type=f32
    )
    return dot(a[0], b[0]) + (dot(a[0], b[1]) + dot(a[1], b[0]))


def newton_schulz_kernel(moment_ref, out_ref):
    moment = moment_ref[...]
    rows, columns = moment.shape
    scale = 0.2 * math.sqrt(max(rows, columns))
    wide = moment.astype(f32).T
    norm = jnp.sqrt(jnp.sum(wide * wide))
    x = wide / (norm + 1e-7)
    for _ in range(NS_STEPS):
        pair = split(x)
        gram = product(pair, pair, ((1,), (1,)))
        gram_pair = split(gram)
        poly = COEF_B * gram + COEF_C * product(gram_pair, gram_pair, ((1,), (0,)))
        x = COEF_A * x + product(split(poly), pair, ((1,), (0,)))
    update = (scale * x).T.astype(bf16)
    moment = moment.astype(bf16)
    owners = out_ref.shape[0]
    depth = rows // owners
    for c in range(NC):
        for chip in range(owners // NC):
            at = slice((chip * NC + c) * depth, (chip * NC + c + 1) * depth)
            out_ref[c * (owners // NC) + chip, 0] = update[at, :]
            out_ref[c * (owners // NC) + chip, 1] = moment[at, :]


def newton_schulz(moment, owners):
    rows, columns = moment.shape
    return pl.pallas_call(
        newton_schulz_kernel,
        out_shape=jax.ShapeDtypeStruct((owners, 2, rows // owners, columns), bf16),
        compiler_params=pltpu.CompilerParams(vmem_limit_bytes=VMEM),
    )(moment)


def spread_kernel(returned, moment, update):
    for head in range(returned.shape[0]):
        at = slice(head * HD, (head + 1) * HD)
        update[:, at] = returned[head, 0]
        moment[:, at] = returned[head, 1].astype(f32)


def spread(returned):
    heads, _, rows, columns = returned.shape
    return pl.pallas_call(
        spread_kernel,
        out_shape=(
            jax.ShapeDtypeStruct((rows, heads * columns), f32),
            jax.ShapeDtypeStruct((rows, heads * columns), bf16),
        ),
        compiler_params=pltpu.CompilerParams(vmem_limit_bytes=VMEM),
    )(returned)


def body(latent, latent_grad, row_counts, momentum):
    z, y, x, c = (lax.axis_index(a) for a in AXES)
    slots, features = latent.shape
    columns = latent_grad.shape[1] // NC

    grad_other = send(lax.dynamic_slice_in_dim(latent_grad, (1 - c) * columns, columns, 1), "c")
    live = lax.broadcasted_iota(jnp.int32, (slots, 1), 0) < row_counts[0]
    masked = jnp.where(live, latent, jnp.zeros_like(latent)).T
    masked_other = send(masked, "c")
    lat = jnp.stack([masked, masked_other])
    mom_own = lax.dynamic_slice_in_dim(momentum, c * columns, columns, 1)
    mom_other = send(lax.dynamic_slice_in_dim(momentum, (1 - c) * columns, columns, 1), "c")
    mom = jnp.where(
        c == 0,
        jnp.concatenate([mom_own, mom_other], 0),
        jnp.concatenate([mom_other, mom_own], 0),
    )

    flips = jnp.array(SLOT_XOR, jnp.int32)
    x_at = ring_coordinate(ring_place(x, c) ^ flips, c)
    y_at = ring_coordinate(ring_place(y, c) ^ flips, c)
    heads_x = (x_at[:, None] + 4 * y_at[None, :]).reshape(-1).astype(jnp.int32)
    heads_y = (4 * y_at[:, None] + x_at[None, :]).reshape(-1).astype(jnp.int32)
    place = jnp.stack([c, (4 * y + x) * 32]).astype(jnp.int32)

    tiles = functools.partial(
        partial_tiles, place=place, lat=lat, mom=mom, grad_own=latent_grad, grad_other=grad_other
    )
    going = tiles(heads_x[8:], heads_y[8:], dtype=bf16)
    kept = tiles(heads_x[:8], heads_y[:8], dtype=f32)

    parts = []
    for first, second, out, keep in (("x", "y", going[0], kept[0]), ("y", "x", going[1], kept[1])):
        for axis in (first, second):
            width = keep.shape[0] // 2
            got = send(out, axis, 1)
            out = (keep[width:] + got[width:].astype(f32)).astype(bf16)
            keep = keep[:width] + got[:width].astype(f32)
            keep = keep + send(out, axis, 3).astype(f32)
            if axis == first:
                out = keep[2:].astype(bf16)
                keep = keep[:2]
        parts.append(keep[0])
    head = jnp.concatenate(parts, 0)

    pieces = head.astype(bf16).reshape(NZ, -1, HD)
    pieces = lax.all_to_all(pieces, "z", 0, 0, tiled=True)
    piece = jnp.sum(pieces.astype(f32), axis=0).astype(bf16)
    moment = lax.all_to_all(jnp.broadcast_to(piece, (NZ,) + piece.shape), "z", 0, 0, tiled=True)
    moment = moment.reshape(features, HD)

    outgoing = newton_schulz(moment, NC * NY * NX)
    returned = lax.all_to_all(outgoing, PLANE, 0, 0, tiled=True)
    return tuple(spread(returned))


def solution(mesh):
    fine = Mesh(mesh.devices.reshape(NZ, NY, NX, NC), AXES)
    shard = ("y", "x", "c")
    in_specs = (P(AXES, None), P(AXES, None), P(AXES), P(shard, None))
    out_specs = (P(shard, None), P(shard, None))
    return jax.shard_map(body, mesh=fine, in_specs=in_specs, out_specs=out_specs, check_vma=False)
```

```python
import functools
import math

import jax
import jax.numpy as jnp
import numpy as np
from jax import lax
from jax.experimental import pallas as pl
from jax.experimental.pallas import tpu as pltpu
from jax.sharding import Mesh
from jax.sharding import PartitionSpec as P

HD = 256
NS_STEPS = 5
NZ, NY, NX, NC = 8, 4, 4, 2
AXES = ("z", "y", "x", "c")
PLANE = ("c", "y", "x")
COEF_A, COEF_B, COEF_C = 3.4445, -4.775, 2.0315
DECAY = 0.95
VMEM = 16 * 1024 * 1024
bf16, f32 = jnp.bfloat16, jnp.float32


SLOT_XOR = (0, 3, 1, 2)


def ring_place(coordinate, core):
    return (coordinate - core) % 4


def ring_coordinate(place, core):
    return (place + core) % 4


def pair_perm(axis, flip):
    pairs = []
    for z in range(NZ):
        for y in range(NY):
            for x in range(NX):
                for c in range(NC):
                    at = {"y": y, "x": x}
                    to = dict(at)
                    if axis == "c":
                        to_c = 1 - c
                    else:
                        to_c = c
                        to[axis] = ring_coordinate(ring_place(at[axis], c) ^ flip, c)
                    here = ((z * NY + y) * NX + x) * NC + c
                    there = ((z * NY + to["y"]) * NX + to["x"]) * NC + to_c
                    pairs.append((here, there))
    return pairs


def send(value, axis, flip=0):
    return lax.ppermute(value, AXES, pair_perm(axis, flip))


def column_copy_kernel(place, grad, out, sems):
    width = out.shape[1] // sems.shape[0]
    copies = []
    for k in range(sems.shape[0]):
        start = pl.multiple_of((1 - place[0]) * out.shape[1] + k * width, width)
        copies.append(
            pltpu.make_async_copy(
                grad.at[:, pl.ds(start, width)], out.at[:, pl.ds(k * width, width)], sems.at[k]
            )
        )
    for copy in copies:
        copy.start()
    for copy in copies:
        copy.wait()


def column_copy(place, grad):
    rows, columns = grad.shape
    return pl.pallas_call(
        column_copy_kernel,
        out_shape=jax.ShapeDtypeStruct((rows, columns // NC), grad.dtype),
        in_specs=[pl.BlockSpec(memory_space=pltpu.SMEM), pl.BlockSpec(memory_space=pl.ANY)],
        out_specs=pl.BlockSpec(memory_space=pl.ANY),
        scratch_shapes=[pltpu.SemaphoreType.DMA((8,))],
        compiler_params=pltpu.CompilerParams(vmem_limit_bytes=VMEM),
    )(place, grad)


def partial_kernel(
    heads, place, lat_own, lat_other, mom_own, mom_other, grad_own, grad_other, out_x, out_y, acc, held, sems
):
    half = acc.shape[0]
    tiles = out_x.shape[0]
    core, row = place[0], place[1]

    def copies(part, tile):
        head = heads[part * tiles + tile]
        own = pl.multiple_of((core * 16 + head) * HD, HD)
        other = pl.multiple_of(head * HD, HD)
        at = part * tiles + tile
        return (
            pltpu.make_async_copy(grad_own.at[:, pl.ds(own, HD)], held.at[at, 0], sems.at[at, 0]),
            pltpu.make_async_copy(grad_other.at[:, pl.ds(other, HD)], held.at[at, 1], sems.at[at, 1]),
        )

    order = [(part, tile) for tile in range(tiles) for part in range(2)]
    for part, tile in order:
        for copy in copies(part, tile):
            copy.start()
    for part, tile in order:
        for copy in copies(part, tile):
            copy.wait()
        at = part * tiles + tile
        rows = slice(part * half, (part + 1) * half)
        p0 = jnp.dot(lat_own[rows, :], held[at, 0], preferred_element_type=f32)
        p1 = jnp.dot(lat_other[rows, :], held[at, 1], preferred_element_type=f32)
        acc[...] = p0.astype(bf16).astype(f32) + p1.astype(bf16).astype(f32)

        @pl.when(row // half == part)
        def _():
            column = pl.multiple_of(heads[at] * HD, HD)
            first = row - part * half
            depth = mom_own.shape[0]
            mine = pl.ds(pl.multiple_of(first + core * depth, depth), depth)
            theirs = pl.ds(pl.multiple_of(first + (1 - core) * depth, depth), depth)
            acc[mine, :] += (DECAY / NZ) * mom_own[:, pl.ds(column, HD)]
            acc[theirs, :] += (DECAY / NZ) * mom_other[:, pl.ds(column, HD)]

        out = out_x if part == 0 else out_y
        out[tile] = acc[...].astype(out.dtype)


def partial_tiles(heads, place, lat_own, lat_other, mom_own, mom_other, grad_own, grad_other, dtype):
    tiles = heads.shape[0] // 2
    features, tokens = lat_own.shape
    half = features // 2
    smem = pl.BlockSpec(memory_space=pltpu.SMEM)
    vmem = pl.BlockSpec(memory_space=pltpu.VMEM)
    hbm = pl.BlockSpec(memory_space=pl.ANY)
    return pl.pallas_call(
        partial_kernel,
        out_shape=[jax.ShapeDtypeStruct((tiles, half, HD), dtype)] * 2,
        in_specs=[smem, smem, vmem, vmem, vmem, vmem, hbm, hbm],
        out_specs=[vmem, vmem],
        scratch_shapes=[
            pltpu.VMEM((half, HD), f32),
            pltpu.VMEM((2 * tiles, 2, tokens, HD), bf16),
            pltpu.SemaphoreType.DMA((2 * tiles, 2)),
        ],
        compiler_params=pltpu.CompilerParams(vmem_limit_bytes=VMEM),
        cost_estimate=pl.CostEstimate(
            flops=2 * tiles * 2 * half * HD * 2 * tokens,
            bytes_accessed=tiles * 2 * (2 * tokens * HD * 2 + half * HD * 4),
            transcendentals=0,
        ),
    )(heads, place, lat_own, lat_other, mom_own, mom_other, grad_own, grad_other)


def split(value):
    high = value.astype(bf16)
    return high, (value - high.astype(f32)).astype(bf16)


def product(a, b, dims):
    dot = functools.partial(
        lax.dot_general, dimension_numbers=(dims, ((), ())), preferred_element_type=f32
    )
    return dot(a[0], b[0]) + (dot(a[0], b[1]) + dot(a[1], b[0]))


def newton_schulz_kernel(moment_ref, out_ref):
    moment = moment_ref[...]
    rows, columns = moment.shape
    scale = 0.2 * math.sqrt(max(rows, columns))
    wide = moment.astype(f32).T
    norm = jnp.sqrt(jnp.sum(wide * wide))
    x = wide / (norm + 1e-7)
    for _ in range(NS_STEPS):
        pair = split(x)
        gram = product(pair, pair, ((1,), (1,)))
        gram_pair = split(gram)
        poly = COEF_B * gram + COEF_C * product(gram_pair, gram_pair, ((1,), (0,)))
        x = COEF_A * x + product(split(poly), pair, ((1,), (0,)))
    update = (scale * x).T.astype(bf16)
    moment = moment.astype(bf16)
    owners = out_ref.shape[0]
    depth = rows // owners
    for c in range(NC):
        for chip in range(owners // NC):
            at = slice((chip * NC + c) * depth, (chip * NC + c + 1) * depth)
            out_ref[c * (owners // NC) + chip, 0] = update[at, :]
            out_ref[c * (owners // NC) + chip, 1] = moment[at, :]


def newton_schulz(moment, owners):
    rows, columns = moment.shape
    return pl.pallas_call(
        newton_schulz_kernel,
        out_shape=jax.ShapeDtypeStruct((owners, 2, rows // owners, columns), bf16),
        compiler_params=pltpu.CompilerParams(vmem_limit_bytes=VMEM),
    )(moment)


def spread_kernel(returned, moment, update):
    for head in range(returned.shape[0]):
        at = slice(head * HD, (head + 1) * HD)
        update[:, at] = returned[head, 0]
        moment[:, at] = returned[head, 1].astype(f32)


def spread(returned):
    heads, _, rows, columns = returned.shape
    return pl.pallas_call(
        spread_kernel,
        out_shape=(
            jax.ShapeDtypeStruct((rows, heads * columns), f32),
            jax.ShapeDtypeStruct((rows, heads * columns), bf16),
        ),
        compiler_params=pltpu.CompilerParams(vmem_limit_bytes=VMEM),
    )(returned)


def body(latent, latent_grad, row_counts, momentum):
    z, y, x, c = (lax.axis_index(a) for a in AXES)
    slots, features = latent.shape
    columns = latent_grad.shape[1] // NC
    place = jnp.stack([c, (4 * y + x) * 32]).astype(jnp.int32)

    grad_other = send(column_copy(place, latent_grad), "c")
    live = lax.broadcasted_iota(jnp.int32, (slots, 1), 0) < row_counts[0]
    lat_own = jnp.where(live, latent, jnp.zeros_like(latent)).T
    lat_other = send(lat_own, "c")
    mom_own = lax.dynamic_slice_in_dim(momentum, c * columns, columns, 1)
    mom_other = send(lax.dynamic_slice_in_dim(momentum, (1 - c) * columns, columns, 1), "c")

    flips = jnp.array(SLOT_XOR, jnp.int32)
    x_at = ring_coordinate(ring_place(x, c) ^ flips, c)
    y_at = ring_coordinate(ring_place(y, c) ^ flips, c)

    def tiles(first, second, dtype):
        heads = jnp.concatenate(
            [
                (x_at[first][:, None] + 4 * y_at[second][None, :]).reshape(-1),
                (4 * y_at[first][:, None] + x_at[second][None, :]).reshape(-1),
            ]
        ).astype(jnp.int32)
        return partial_tiles(
            heads, place, lat_own, lat_other, mom_own, mom_other, latent_grad, grad_other, dtype
        )

    near, far = slice(0, 2), slice(2, 4)
    far_going = tiles(far, far, bf16)
    near_going = tiles(far, near, bf16)
    far_kept = tiles(near, far, f32)
    near_kept = tiles(near, near, f32)

    def reduce_first(axis, going, kept):
        got = send(going, axis, 1).astype(f32)
        out = (kept[2:] + got[2:]).astype(bf16)
        return kept[:2] + got[:2] + send(out, axis, 3).astype(f32)

    parts = []
    for part, (first, second) in enumerate((("x", "y"), ("y", "x"))):
        out = reduce_first(first, far_going[part], far_kept[part]).astype(bf16)
        keep = reduce_first(first, near_going[part], near_kept[part])
        keep = keep + send(out, second, 1).astype(f32)
        parts.append(keep[0] + send(keep[1].astype(bf16), second, 3).astype(f32))
    head = jnp.concatenate(parts, 0)

    pieces = head.astype(bf16).reshape(NZ, -1, HD)
    pieces = lax.all_to_all(pieces, "z", 0, 0, tiled=True)
    piece = jnp.sum(pieces.astype(f32), axis=0).astype(bf16)
    moment = lax.all_to_all(jnp.broadcast_to(piece, (NZ,) + piece.shape), "z", 0, 0, tiled=True)
    moment = moment.reshape(features, HD)

    outgoing = newton_schulz(moment, NC * NY * NX)
    returned = lax.all_to_all(outgoing, PLANE, 0, 0, tiled=True)
    return tuple(spread(returned))


def solution(mesh):
    fine = Mesh(mesh.devices.reshape(NZ, NY, NX, NC), AXES)
    shard = ("y", "x", "c")
    in_specs = (P(AXES, None), P(AXES, None), P(AXES), P(shard, None))
    out_specs = (P(shard, None), P(shard, None))
    return jax.shard_map(body, mesh=fine, in_specs=in_specs, out_specs=out_specs, check_vma=False)
```

```python
import functools
import math

import jax
import jax.numpy as jnp
from jax import lax
from jax.experimental import pallas as pl
from jax.experimental.pallas import tpu as pltpu
from jax.sharding import Mesh
from jax.sharding import PartitionSpec as P

HD = 256
NS_STEPS = 5
NZ, NY, NX, NC = 8, 4, 4, 2
RING = 4
AXES = ("z", "y", "x", "c")
PLANE = ("c", "y", "x")
COEF_A, COEF_B, COEF_C = 3.4445, -4.775, 2.0315
DECAY = 0.95
VMEM = 16 * 1024 * 1024
bf16, f32 = jnp.bfloat16, jnp.float32


def device_at(z, y, x, c):
    return ((z * NY + y) * NX + x) * NC + c


def every_device():
    return [(z, y, x, c) for z in range(NZ) for y in range(NY) for x in range(NX) for c in range(NC)]


def partner(place, part, flip):
    return (((place - part) % RING) ^ flip) + part & (RING - 1)


def send(value, part, flip):
    pairs = []
    for z, y, x, c in every_device():
        to = (y, partner(x, part, flip)) if c == 0 else (partner(y, part, flip), x)
        pairs.append((device_at(z, y, x, c), device_at(z, *to, c)))
    return lax.ppermute(value, AXES, pairs)


def swap_cores(value):
    return lax.ppermute(
        value, AXES, [(device_at(z, y, x, c), device_at(z, y, x, 1 - c)) for z, y, x, c in every_device()]
    )


def second_axis_groups():
    groups = []
    for z in range(NZ):
        for place in range(RING):
            groups.append([device_at(z, other, place, 0) for other in range(RING)])
            groups.append([device_at(z, place, other, 1) for other in range(RING)])
    return groups


def first_place():
    core = lax.axis_index("c")
    return jnp.where(core == 0, lax.axis_index("x"), lax.axis_index("y"))


def column_copy_kernel(grad, out, sems):
    width = out.shape[1] // sems.shape[0]
    copies = []
    for k in range(sems.shape[0]):
        start = pl.multiple_of((1 - lax.axis_index("c")) * out.shape[1] + k * width, width)
        copies.append(
            pltpu.make_async_copy(
                grad.at[:, pl.ds(start, width)], out.at[:, pl.ds(k * width, width)], sems.at[k]
            )
        )
    for copy in copies:
        copy.start()
    for copy in copies:
        copy.wait()


def column_copy(grad):
    rows, columns = grad.shape
    return pl.pallas_call(
        column_copy_kernel,
        out_shape=jax.ShapeDtypeStruct((rows, columns // NC), grad.dtype),
        in_specs=[pl.BlockSpec(memory_space=pltpu.HBM)],
        out_specs=pl.BlockSpec(memory_space=pl.ANY),
        scratch_shapes=[pltpu.SemaphoreType.DMA((8,))],
        compiler_params=pltpu.CompilerParams(vmem_limit_bytes=VMEM),
    )(grad)


def partial_kernel(
    going, lat_own, lat_other, mom_own, mom_other, grad_own, grad_other, out_0, out_1, held, unit, sems
):
    features, tokens = lat_own.shape
    half = features // 2
    depth = mom_own.shape[0]
    width = RING * HD
    core, place = lax.axis_index("c"), first_place()
    here = lax.axis_index("y") * NX + lax.axis_index("x")

    def turned(part, flip):
        return lax.rem(lax.rem(place + RING - part, RING) ^ flip, RING) + part

    one = lax.rem(turned(0, 1), RING)
    two = lax.rem(turned(1, 1), RING)
    shared = lax.rem(place + (2 if going else 0), RING)
    blocks = (one, two, shared) if going else (two, one, shared)
    columns = grad_other.shape[1]

    def copies(k):
        other = pl.multiple_of(blocks[k] * width, width)
        own = pl.multiple_of(core * columns + blocks[k] * width, width)
        return (
            pltpu.make_async_copy(grad_own.at[:, pl.ds(own, width)], held.at[k, 0], sems.at[k, 0]),
            pltpu.make_async_copy(grad_other.at[:, pl.ds(other, width)], held.at[k, 1], sems.at[k, 1]),
        )

    for k in range(3):
        for copy in copies(k):
            copy.start()

    row = lax.broadcasted_iota(jnp.int32, (features, 4 * depth), 0)
    at = lax.broadcasted_iota(jnp.int32, (features, 4 * depth), 1)
    core_of = jnp.where((at // depth) % 2 == 0, core, 1 - core)
    unit[...] = (row == (here * NC + core_of) * depth + at % depth).astype(f32).astype(bf16)

    for k in range(3):
        for copy in copies(k):
            copy.wait()
        start = pl.multiple_of(blocks[k] * width, width)
        mom = []
        for ref in (mom_own, mom_other):
            value = (DECAY / NZ) * ref[:, pl.ds(start, width)]
            high = value.astype(bf16)
            mom.append((high, (value - high.astype(f32)).astype(bf16)))
        mom = jnp.concatenate([mom[0][0], mom[1][0], mom[0][1], mom[1][1]], axis=0)
        for part, out in ((0, out_0), (1, out_1)):
            if part == 1 - k:
                continue
            rows = slice(part * half, (part + 1) * half)
            slot = int(going) if k == 2 else 1 - int(going)
            for t in range(RING):
                at = slice(t * HD, (t + 1) * HD)
                p0 = jnp.dot(lat_own[rows, :], held[k, 0, :, at], preferred_element_type=f32)
                p1 = jnp.dot(lat_other[rows, :], held[k, 1, :, at], preferred_element_type=f32)
                p2 = jnp.dot(unit[rows, :], mom[:, at], preferred_element_type=f32)
                total = p0.astype(bf16).astype(f32) + p1.astype(bf16).astype(f32) + p2
                out[slot * RING + t] = total.astype(out.dtype)


def partial_tiles(going, lat_own, lat_other, mom_own, mom_other, grad_own, grad_other):
    features, tokens = lat_own.shape
    half = features // 2
    tiles = 2 * RING
    vmem = pl.BlockSpec(memory_space=pltpu.VMEM)
    hbm = pl.BlockSpec(memory_space=pl.ANY)
    return pl.pallas_call(
        functools.partial(partial_kernel, going),
        out_shape=[jax.ShapeDtypeStruct((tiles, half, HD), bf16 if going else f32)] * 2,
        in_specs=[vmem, vmem, vmem, vmem, hbm, hbm],
        out_specs=[vmem, vmem],
        scratch_shapes=[
            pltpu.VMEM((3, 2, tokens, RING * HD), bf16),
            pltpu.VMEM((features, 4 * mom_own.shape[0]), bf16),
            pltpu.SemaphoreType.DMA((3, 2)),
        ],
        compiler_params=pltpu.CompilerParams(vmem_limit_bytes=VMEM),
        cost_estimate=pl.CostEstimate(
            flops=2 * tiles * 2 * half * HD * 3 * tokens,
            bytes_accessed=tiles * 2 * (2 * tokens * HD * 2 + half * HD * 4),
            transcendentals=0,
        ),
    )(lat_own, lat_other, mom_own, mom_other, grad_own, grad_other)


def split(value):
    high = value.astype(bf16)
    return high, (value - high.astype(f32)).astype(bf16)


def product(a, b, dims):
    dot = functools.partial(
        lax.dot_general, dimension_numbers=(dims, ((), ())), preferred_element_type=f32
    )
    return dot(a[0], b[0]) + (dot(a[0], b[1]) + dot(a[1], b[0]))


def newton_schulz_kernel(moment_ref, out_ref):
    moment = moment_ref[...]
    rows, columns = moment.shape
    scale = 0.2 * math.sqrt(max(rows, columns))
    wide = moment.T
    gram = lax.dot_general(wide, wide, (((1,), (1,)), ((), ())), preferred_element_type=f32)
    wide = wide.astype(f32)
    inverse = 1.0 / (jnp.sqrt(jnp.sum(wide * wide)) + 1e-7)
    gram = (gram * inverse) * inverse
    x = wide * inverse
    for step in range(NS_STEPS):
        pair = split(x)
        if step > 0:
            gram = product(pair, pair, ((1,), (1,)))
        gram_pair = split(gram)
        poly = COEF_B * gram + COEF_C * product(gram_pair, gram_pair, ((1,), (0,)))
        x = COEF_A * x + product(split(poly), pair, ((1,), (0,)))
    update = (scale * x).T.astype(bf16)
    owners = out_ref.shape[0]
    depth = rows // owners
    for c in range(NC):
        for chip in range(owners // NC):
            at = slice((chip * NC + c) * depth, (chip * NC + c + 1) * depth)
            out_ref[c * (owners // NC) + chip, 0] = update[at, :]
            out_ref[c * (owners // NC) + chip, 1] = moment[at, :]


def newton_schulz(moment, owners):
    rows, columns = moment.shape
    return pl.pallas_call(
        newton_schulz_kernel,
        out_shape=jax.ShapeDtypeStruct((owners, 2, rows // owners, columns), bf16),
        compiler_params=pltpu.CompilerParams(vmem_limit_bytes=VMEM),
    )(moment)


def spread_kernel(returned, moment, update):
    for c in range(NC):
        for y in range(NY):
            for x in range(NX):
                source = (c * NY + y) * NX + x
                head = c * NY * NX + (RING * x + y if c == 0 else RING * y + x)
                at = slice(head * HD, (head + 1) * HD)
                update[:, at] = returned[source, 0]
                moment[:, at] = returned[source, 1].astype(f32)


def spread(returned):
    heads, _, rows, columns = returned.shape
    return pl.pallas_call(
        spread_kernel,
        out_shape=(
            jax.ShapeDtypeStruct((rows, heads * columns), f32),
            jax.ShapeDtypeStruct((rows, heads * columns), bf16),
        ),
        compiler_params=pltpu.CompilerParams(vmem_limit_bytes=VMEM),
    )(returned)


def body(latent, latent_grad, row_counts, momentum):
    c = lax.axis_index("c")
    slots, features = latent.shape
    columns = latent_grad.shape[1] // NC

    grad_other = swap_cores(column_copy(latent_grad))
    live = lax.broadcasted_iota(jnp.int32, (slots, 1), 0) < row_counts[0]
    lat_own = jnp.where(live, latent, jnp.zeros_like(latent)).T
    lat_other = swap_cores(lat_own)
    mom_own = lax.dynamic_slice_in_dim(momentum, c * columns, columns, 1)
    mom_other = swap_cores(lax.dynamic_slice_in_dim(momentum, (1 - c) * columns, columns, 1))

    operands = (lat_own, lat_other, mom_own, mom_other, latent_grad, grad_other)
    going = partial_tiles(True, *operands)
    kept = partial_tiles(False, *operands)

    parts = []
    for part in range(2):
        got = send(going[part], part, 1)
        out = (kept[part][RING:] + got[RING:].astype(f32)).astype(bf16)
        keep = kept[part][:RING] + got[:RING].astype(f32)
        parts.append((keep + send(out, part, 3).astype(f32)).astype(bf16))

    stack = jnp.concatenate(parts, axis=1)
    stack = lax.all_to_all(stack, AXES, 0, 0, axis_index_groups=second_axis_groups(), tiled=True)
    head = jnp.sum(stack.astype(f32), axis=0).astype(bf16)

    pieces = lax.all_to_all(head.reshape(NZ, -1, HD), "z", 0, 0, tiled=True)
    piece = jnp.sum(pieces.astype(f32), axis=0).astype(bf16)
    moment = lax.all_to_all(jnp.broadcast_to(piece, (NZ,) + piece.shape), "z", 0, 0, tiled=True)
    moment = moment.reshape(features, HD)

    outgoing = newton_schulz(moment, NC * NY * NX)
    returned = lax.all_to_all(outgoing, PLANE, 0, 0, tiled=True)
    return tuple(spread(returned))


def solution(mesh):
    fine = Mesh(mesh.devices.reshape(NZ, NY, NX, NC), AXES)
    shard = ("y", "x", "c")
    in_specs = (P(AXES, None), P(AXES, None), P(AXES), P(shard, None))
    out_specs = (P(shard, None), P(shard, None))
    return jax.shard_map(body, mesh=fine, in_specs=in_specs, out_specs=out_specs, check_vma=False)
```

```python
import functools
import math

import jax
import jax.numpy as jnp
from jax import lax
from jax.experimental import pallas as pl
from jax.experimental.pallas import tpu as pltpu
from jax.sharding import Mesh
from jax.sharding import PartitionSpec as P

HD = 256
NS_STEPS = 5
NZ, NY, NX, NC = 8, 4, 4, 2
RING = 4
AXES = ("z", "y", "x", "c")
PLANE = ("c", "y", "x")
COEF_A, COEF_B, COEF_C = 3.4445, -4.775, 2.0315
DECAY = 0.95
VMEM = 16 * 1024 * 1024
bf16, f32 = jnp.bfloat16, jnp.float32


def device_at(z, y, x, c):
    return ((z * NY + y) * NX + x) * NC + c


def every_device():
    return [(z, y, x, c) for z in range(NZ) for y in range(NY) for x in range(NX) for c in range(NC)]


def shift(value, axis, distance):
    pairs = []
    for z, y, x, c in every_device():
        if axis == c:
            to = (y, (x + distance) % NX)
        else:
            to = ((y + distance) % NY, x)
        pairs.append((device_at(z, y, x, c), device_at(z, *to, c)))
    return lax.ppermute(value, AXES, pairs)


def swap_cores(value):
    return lax.ppermute(
        value, AXES, [(device_at(z, y, x, c), device_at(z, y, x, 1 - c)) for z, y, x, c in every_device()]
    )


def places():
    core, y, x = lax.axis_index("c"), lax.axis_index("y"), lax.axis_index("x")
    return jnp.where(core == 0, x, y), jnp.where(core == 0, y, x)


def column_copy_kernel(grad, out, sems):
    width = out.shape[1] // sems.shape[0]
    copies = []
    for k in range(sems.shape[0]):
        start = pl.multiple_of((1 - lax.axis_index("c")) * out.shape[1] + k * width, width)
        copies.append(
            pltpu.make_async_copy(
                grad.at[:, pl.ds(start, width)], out.at[:, pl.ds(k * width, width)], sems.at[k]
            )
        )
    for copy in copies:
        copy.start()
    for copy in copies:
        copy.wait()


def column_copy(grad):
    rows, columns = grad.shape
    return pl.pallas_call(
        column_copy_kernel,
        out_shape=jax.ShapeDtypeStruct((rows, columns // NC), grad.dtype),
        in_specs=[pl.BlockSpec(memory_space=pl.ANY)],
        out_specs=pl.BlockSpec(memory_space=pl.ANY),
        scratch_shapes=[pltpu.SemaphoreType.DMA((8,))],
        compiler_params=pltpu.CompilerParams(vmem_limit_bytes=62 * 1024 * 1024),
    )(grad)


def head_columns(near, far):
    first, second = places()
    head = lax.rem(first + near, RING) * RING + lax.rem(second + far, RING)
    return pl.multiple_of(head * HD, HD)


def own_kernel(depth, lat, grad, *refs):
    outs, (unit, held, sems) = refs[:RING], refs[RING:]
    core = lax.axis_index("c")
    half = grad.shape[1] // NC
    copies = []
    for near in range(RING):
        for far in range(RING):
            start = pl.multiple_of(core * half + head_columns(near, far), HD)
            at = near * RING + far
            copies.append(
                pltpu.make_async_copy(grad.at[:, pl.ds(start, HD)], held.at[at], sems.at[at])
            )
    for copy in copies:
        copy.start()

    features = lat.shape[0]
    here = lax.axis_index("y") * NX + lax.axis_index("x")
    row = lax.broadcasted_iota(jnp.int32, (features, 4 * depth), 0)
    at = lax.broadcasted_iota(jnp.int32, (features, 4 * depth), 1)
    core_of = jnp.where((at // depth) % 2 == 0, core, 1 - core)
    unit[...] = (row == (here * NC + core_of) * depth + at % depth).astype(f32).astype(bf16)

    for copy in copies:
        copy.wait()
    for near in range(RING):
        for far in range(RING):
            product = jnp.dot(lat[...], held[near * RING + far], preferred_element_type=f32)
            outs[near][far] = product.astype(bf16)


def own_products(lat, grad, depth):
    features, tokens = lat.shape
    out = jax.ShapeDtypeStruct((RING, features, HD), bf16)
    vmem = pl.BlockSpec(memory_space=pltpu.VMEM)
    return pl.pallas_call(
        functools.partial(own_kernel, depth),
        out_shape=[out] * RING + [jax.ShapeDtypeStruct((features, 4 * depth), bf16)],
        in_specs=[vmem, pl.BlockSpec(memory_space=pl.ANY)],
        out_specs=[vmem] * (RING + 1),
        scratch_shapes=[
            pltpu.VMEM((RING * RING, tokens, HD), bf16),
            pltpu.SemaphoreType.DMA((RING * RING,)),
        ],
        compiler_params=pltpu.CompilerParams(vmem_limit_bytes=VMEM),
        cost_estimate=pl.CostEstimate(
            flops=2 * RING * RING * features * HD * tokens,
            bytes_accessed=RING * RING * (tokens + features) * HD * 2,
            transcendentals=0,
        ),
    )(lat, grad)


def block_kernel(near, own, unit, lat, mom_own, mom_other, grad, out):
    for far in range(RING):
        at = pl.ds(head_columns(near, far), HD)
        high, low = [], []
        for ref in (mom_own, mom_other):
            value = (DECAY / NZ) * ref[:, at]
            high.append(value.astype(bf16))
            low.append((value - high[-1].astype(f32)).astype(bf16))
        mom = jnp.concatenate(high + low, axis=0)
        other = jnp.dot(lat[...], grad[:, at], preferred_element_type=f32)
        added = jnp.dot(unit[...], mom, preferred_element_type=f32)
        total = own[far].astype(f32) + other.astype(bf16).astype(f32) + added
        out[far] = total.astype(out.dtype)


def block(near, own, unit, lat, mom_own, mom_other, grad):
    features, tokens = lat.shape
    dtype = f32 if near == 0 else bf16
    return pl.pallas_call(
        functools.partial(block_kernel, near),
        out_shape=jax.ShapeDtypeStruct(own.shape, dtype),
        compiler_params=pltpu.CompilerParams(vmem_limit_bytes=VMEM),
        cost_estimate=pl.CostEstimate(
            flops=2 * RING * features * HD * (tokens + unit.shape[1]),
            bytes_accessed=RING * (tokens + 2 * features) * HD * 2,
            transcendentals=0,
        ),
    )(own, unit, lat, mom_own, mom_other, grad)


def split(value):
    high = value.astype(bf16)
    return high, (value - high.astype(f32)).astype(bf16)


def product(a, b, dims):
    dot = functools.partial(
        lax.dot_general, dimension_numbers=(dims, ((), ())), preferred_element_type=f32
    )
    return dot(a[0], b[0]) + (dot(a[0], b[1]) + dot(a[1], b[0]))


def newton_schulz_kernel(moment_ref, out_ref):
    moment = moment_ref[...]
    rows, columns = moment.shape
    scale = 0.2 * math.sqrt(max(rows, columns))
    wide = moment.T
    gram = lax.dot_general(wide, wide, (((1,), (1,)), ((), ())), preferred_element_type=f32)
    wide = wide.astype(f32)
    inverse = 1.0 / (jnp.sqrt(jnp.sum(wide * wide)) + 1e-7)
    gram = (gram * inverse) * inverse
    x = wide * inverse
    for step in range(NS_STEPS):
        pair = split(x)
        if step > 0:
            gram = product(pair, pair, ((1,), (1,)))
        gram_pair = split(gram)
        poly = COEF_B * gram + COEF_C * product(gram_pair, gram_pair, ((1,), (0,)))
        x = COEF_A * x + product(split(poly), pair, ((1,), (0,)))
    update = (scale * x).T.astype(bf16)
    owners = out_ref.shape[0]
    depth = rows // owners
    for c in range(NC):
        for chip in range(owners // NC):
            at = slice((chip * NC + c) * depth, (chip * NC + c + 1) * depth)
            out_ref[c * (owners // NC) + chip, 0] = update[at, :]
            out_ref[c * (owners // NC) + chip, 1] = moment[at, :]


def newton_schulz(moment, owners):
    rows, columns = moment.shape
    return pl.pallas_call(
        newton_schulz_kernel,
        out_shape=jax.ShapeDtypeStruct((owners, 2, rows // owners, columns), bf16),
        compiler_params=pltpu.CompilerParams(vmem_limit_bytes=VMEM),
    )(moment)


def spread_kernel(returned, moment, update):
    for c in range(NC):
        for y in range(NY):
            for x in range(NX):
                source = (c * NY + y) * NX + x
                head = c * NY * NX + (RING * x + y if c == 0 else RING * y + x)
                at = slice(head * HD, (head + 1) * HD)
                update[:, at] = returned[source, 0]
                moment[:, at] = returned[source, 1].astype(f32)


def spread(returned):
    heads, _, rows, columns = returned.shape
    return pl.pallas_call(
        spread_kernel,
        out_shape=(
            jax.ShapeDtypeStruct((rows, heads * columns), f32),
            jax.ShapeDtypeStruct((rows, heads * columns), bf16),
        ),
        compiler_params=pltpu.CompilerParams(vmem_limit_bytes=VMEM),
    )(returned)


def body(latent, latent_grad, row_counts, momentum):
    c = lax.axis_index("c")
    slots, features = latent.shape
    columns = latent_grad.shape[1] // NC

    grad_other = swap_cores(column_copy(latent_grad))
    live = lax.broadcasted_iota(jnp.int32, (slots, 1), 0) < row_counts[0]
    lat_own = jnp.where(live, latent, jnp.zeros_like(latent)).T
    lat_other = swap_cores(lat_own)
    mom_own = lax.dynamic_slice_in_dim(momentum, c * columns, columns, 1)
    mom_other = swap_cores(lax.dynamic_slice_in_dim(momentum, (1 - c) * columns, columns, 1))

    *own, unit = own_products(lat_own, latent_grad, momentum.shape[0])
    blocks = [block(k, own[k], unit, lat_other, mom_own, mom_other, grad_other) for k in range(RING)]
    got = [shift(blocks[k], 0, k) for k in (2, 1, 3)]
    total = blocks[0] + sum(g.astype(f32) for g in got)

    got = [shift(total[k].astype(bf16), 1, k) for k in (2, 1, 3)]
    head = (total[0] + sum(g.astype(f32) for g in got)).astype(bf16)

    pieces = lax.all_to_all(head.reshape(NZ, -1, HD), "z", 0, 0, tiled=True)
    piece = jnp.sum(pieces.astype(f32), axis=0).astype(bf16)
    moment = lax.all_to_all(jnp.broadcast_to(piece, (NZ,) + piece.shape), "z", 0, 0, tiled=True)
    moment = moment.reshape(features, HD)

    outgoing = newton_schulz(moment, NC * NY * NX)
    returned = lax.all_to_all(outgoing, PLANE, 0, 0, tiled=True)
    return tuple(spread(returned))


def solution(mesh):
    fine = Mesh(mesh.devices.reshape(NZ, NY, NX, NC), AXES)
    shard = ("y", "x", "c")
    in_specs = (P(AXES, None), P(AXES, None), P(AXES), P(shard, None))
    out_specs = (P(shard, None), P(shard, None))
    return jax.shard_map(body, mesh=fine, in_specs=in_specs, out_specs=out_specs, check_vma=False)
```

```python
import functools
import math

import jax
import jax.numpy as jnp
from jax import lax
from jax.experimental import pallas as pl
from jax.experimental.pallas import tpu as pltpu
from jax.sharding import Mesh
from jax.sharding import PartitionSpec as P

HD = 256
NS_STEPS = 5
NZ, NY, NX, NC = 8, 4, 4, 2
RING = 4
AXES = ("z", "y", "x", "c")
PLANE = ("c", "y", "x")
COEF_A, COEF_B, COEF_C = 3.4445, -4.775, 2.0315
DECAY = 0.95
VMEM = 16 * 1024 * 1024
LARGE = 48 * 1024 * 1024
bf16, f32 = jnp.bfloat16, jnp.float32


def device_at(z, y, x, c):
    return ((z * NY + y) * NX + x) * NC + c


def every_device():
    return [(z, y, x, c) for z in range(NZ) for y in range(NY) for x in range(NX) for c in range(NC)]


def shift(value, axis, distance):
    pairs = []
    for z, y, x, c in every_device():
        if axis == c:
            to = (y, (x + distance) % NX)
        else:
            to = ((y + distance) % NY, x)
        pairs.append((device_at(z, y, x, c), device_at(z, *to, c)))
    return lax.ppermute(value, AXES, pairs)


def swap_cores(value):
    return lax.ppermute(
        value, AXES, [(device_at(z, y, x, c), device_at(z, y, x, 1 - c)) for z, y, x, c in every_device()]
    )


def places():
    core, y, x = lax.axis_index("c"), lax.axis_index("y"), lax.axis_index("x")
    return jnp.where(core == 0, x, y), jnp.where(core == 0, y, x)


def column_copy_kernel(grad, out, sems):
    width = out.shape[1] // sems.shape[0]
    copies = []
    for k in range(sems.shape[0]):
        start = pl.multiple_of((1 - lax.axis_index("c")) * out.shape[1] + k * width, width)
        copies.append(
            pltpu.make_async_copy(
                grad.at[:, pl.ds(start, width)], out.at[:, pl.ds(k * width, width)], sems.at[k]
            )
        )
    for copy in copies:
        copy.start()
    for copy in copies:
        copy.wait()


def column_copy(grad):
    rows, columns = grad.shape
    return pl.pallas_call(
        column_copy_kernel,
        out_shape=jax.ShapeDtypeStruct((rows, columns // NC), grad.dtype),
        in_specs=[pl.BlockSpec(memory_space=pl.ANY)],
        out_specs=pl.BlockSpec(memory_space=pltpu.VMEM),
        scratch_shapes=[pltpu.SemaphoreType.DMA((8,))],
        compiler_params=pltpu.CompilerParams(vmem_limit_bytes=LARGE),
    )(grad)


def head_columns(near, far):
    first, second = places()
    head = lax.rem(first + near, RING) * RING + lax.rem(second + far, RING)
    return pl.multiple_of(head * HD, HD)


def own_kernel(depth, lat, grad, *refs):
    outs, (unit, held, sems) = refs[:RING], refs[RING:]
    core = lax.axis_index("c")
    half = grad.shape[1] // NC
    copies = []
    for near in range(RING):
        for far in range(RING):
            start = pl.multiple_of(core * half + head_columns(near, far), HD)
            at = near * RING + far
            copies.append(
                pltpu.make_async_copy(grad.at[:, pl.ds(start, HD)], held.at[at], sems.at[at])
            )
    for copy in copies:
        copy.start()

    features = lat.shape[0]
    here = lax.axis_index("y") * NX + lax.axis_index("x")
    row = lax.broadcasted_iota(jnp.int32, (features, 4 * depth), 0)
    at = lax.broadcasted_iota(jnp.int32, (features, 4 * depth), 1)
    core_of = jnp.where((at // depth) % 2 == 0, core, 1 - core)
    unit[...] = (row == (here * NC + core_of) * depth + at % depth).astype(f32).astype(bf16)

    for copy in copies:
        copy.wait()
    for near in range(RING):
        for far in range(RING):
            product = jnp.dot(lat[...], held[near * RING + far], preferred_element_type=f32)
            outs[near][far] = product.astype(bf16)


def own_products(lat, grad, depth):
    features, tokens = lat.shape
    out = jax.ShapeDtypeStruct((RING, features, HD), bf16)
    vmem = pl.BlockSpec(memory_space=pltpu.VMEM)
    return pl.pallas_call(
        functools.partial(own_kernel, depth),
        out_shape=[out] * RING + [jax.ShapeDtypeStruct((features, 4 * depth), bf16)],
        in_specs=[vmem, pl.BlockSpec(memory_space=pl.ANY)],
        out_specs=[vmem] * (RING + 1),
        scratch_shapes=[
            pltpu.VMEM((RING * RING, tokens, HD), bf16),
            pltpu.SemaphoreType.DMA((RING * RING,)),
        ],
        compiler_params=pltpu.CompilerParams(vmem_limit_bytes=LARGE),
        cost_estimate=pl.CostEstimate(
            flops=2 * RING * RING * features * HD * tokens,
            bytes_accessed=RING * RING * (tokens + features) * HD * 2,
            transcendentals=0,
        ),
    )(lat, grad)


def block_kernel(tiles, unit, lat, mom_own, mom_other, grad, *refs):
    operands, outs = refs[: 1 + max(t[0] for t in tiles)], refs[1 + max(t[0] for t in tiles) :]
    for operand, result, near, fars in tiles:
        for place, far in enumerate(fars):
            at = pl.ds(head_columns(near, far), HD)
            high, low = [], []
            for ref in (mom_own, mom_other):
                value = (DECAY / NZ) * ref[:, at]
                high.append(value.astype(bf16))
                low.append((value - high[-1].astype(f32)).astype(bf16))
            mom = jnp.concatenate(high + low, axis=0)
            other = jnp.dot(lat[...], grad[:, at], preferred_element_type=f32)
            added = jnp.dot(unit[...], mom, preferred_element_type=f32)
            total = operands[operand][far].astype(f32) + other.astype(bf16).astype(f32) + added
            outs[result][place] = total.astype(outs[result].dtype)


def block(own, which, unit, lat, mom_own, mom_other, grad):
    features, tokens = lat.shape
    nears = sorted({near for near, _ in which})
    tiles = [(nears.index(near), k, near, fars) for k, (near, fars) in enumerate(which)]
    heads = sum(len(fars) for _, fars in which)
    return pl.pallas_call(
        functools.partial(block_kernel, tiles),
        out_shape=[
            jax.ShapeDtypeStruct((len(fars), features, HD), f32 if near == 0 else bf16)
            for near, fars in which
        ],
        compiler_params=pltpu.CompilerParams(vmem_limit_bytes=VMEM),
        cost_estimate=pl.CostEstimate(
            flops=2 * heads * features * HD * (tokens + unit.shape[1]),
            bytes_accessed=heads * (tokens + 2 * features) * HD * 2,
            transcendentals=0,
        ),
    )(unit, lat, mom_own, mom_other, grad, *[own[near] for near in nears])


def split(value):
    high = value.astype(bf16)
    return high, (value - high.astype(f32)).astype(bf16)


def product(a, b, dims):
    dot = functools.partial(
        lax.dot_general, dimension_numbers=(dims, ((), ())), preferred_element_type=f32
    )
    return dot(a[0], b[0]) + (dot(a[0], b[1]) + dot(a[1], b[0]))


def newton_schulz_kernel(moment_ref, out_ref):
    moment = moment_ref[...]
    rows, columns = moment.shape
    scale = 0.2 * math.sqrt(max(rows, columns))
    wide = moment.T
    gram = lax.dot_general(wide, wide, (((1,), (1,)), ((), ())), preferred_element_type=f32)
    wide = wide.astype(f32)
    inverse = 1.0 / (jnp.sqrt(jnp.sum(wide * wide)) + 1e-7)
    gram = (gram * inverse) * inverse
    x = wide * inverse
    for step in range(NS_STEPS):
        pair = split(x)
        if step > 0:
            gram = product(pair, pair, ((1,), (1,)))
        gram_pair = split(gram)
        poly = COEF_B * gram + COEF_C * product(gram_pair, gram_pair, ((1,), (0,)))
        x = COEF_A * x + product(split(poly), pair, ((1,), (0,)))
    update = (scale * x).T.astype(bf16)
    owners = out_ref.shape[0]
    depth = rows // owners
    for c in range(NC):
        for chip in range(owners // NC):
            at = slice((chip * NC + c) * depth, (chip * NC + c + 1) * depth)
            out_ref[c * (owners // NC) + chip, 0] = update[at, :]
            out_ref[c * (owners // NC) + chip, 1] = moment[at, :]


def newton_schulz(moment, owners):
    rows, columns = moment.shape
    return pl.pallas_call(
        newton_schulz_kernel,
        out_shape=jax.ShapeDtypeStruct((owners, 2, rows // owners, columns), bf16),
        compiler_params=pltpu.CompilerParams(vmem_limit_bytes=VMEM),
    )(moment)


def spread_kernel(returned, moment, update):
    for c in range(NC):
        for y in range(NY):
            for x in range(NX):
                source = (c * NY + y) * NX + x
                head = c * NY * NX + (RING * x + y if c == 0 else RING * y + x)
                at = slice(head * HD, (head + 1) * HD)
                update[:, at] = returned[source, 0]
                moment[:, at] = returned[source, 1].astype(f32)


def spread(returned):
    heads, _, rows, columns = returned.shape
    return pl.pallas_call(
        spread_kernel,
        out_shape=(
            jax.ShapeDtypeStruct((rows, heads * columns), f32),
            jax.ShapeDtypeStruct((rows, heads * columns), bf16),
        ),
        compiler_params=pltpu.CompilerParams(vmem_limit_bytes=VMEM),
    )(returned)


def body(latent, latent_grad, row_counts, momentum):
    c = lax.axis_index("c")
    slots, features = latent.shape
    columns = latent_grad.shape[1] // NC

    grad_other = swap_cores(column_copy(latent_grad))
    live = lax.broadcasted_iota(jnp.int32, (slots, 1), 0) < row_counts[0]
    lat_own = jnp.where(live, latent, jnp.zeros_like(latent)).T
    lat_other = swap_cores(lat_own)
    mom_own = lax.dynamic_slice_in_dim(momentum, c * columns, columns, 1)
    mom_other = swap_cores(lax.dynamic_slice_in_dim(momentum, (1 - c) * columns, columns, 1))

    *own, unit = own_products(lat_own, latent_grad, momentum.shape[0])
    operands = (unit, lat_other, mom_own, mom_other, grad_other)
    order, rest = (2, 1, 3), (1, 2, 3)
    on = [shift(block(own, [(k, rest)], *operands)[0], 0, k) for k in order]
    *stay, kept_stay, kept_on = block(
        own, [(k, (0,)) for k in order] + [(0, (0,)), (0, rest)], *operands
    )
    stay = [shift(value, 0, k) for value, k in zip(stay, order)]

    total = kept_on + sum(value.astype(f32) for value in on)
    got = [shift(total[k - 1].astype(bf16), 1, k) for k in order]
    head = kept_stay[0] + sum(value[0].astype(f32) for value in stay)
    head = (head + sum(value.astype(f32) for value in got)).astype(bf16)

    pieces = lax.all_to_all(head.reshape(NZ, -1, HD), "z", 0, 0, tiled=True)
    piece = jnp.sum(pieces.astype(f32), axis=0).astype(bf16)
    moment = lax.all_to_all(jnp.broadcast_to(piece, (NZ,) + piece.shape), "z", 0, 0, tiled=True)
    moment = moment.reshape(features, HD)

    outgoing = newton_schulz(moment, NC * NY * NX)
    returned = lax.all_to_all(outgoing, PLANE, 0, 0, tiled=True)
    return tuple(spread(returned))


def solution(mesh):
    fine = Mesh(mesh.devices.reshape(NZ, NY, NX, NC), AXES)
    shard = ("y", "x", "c")
    in_specs = (P(AXES, None), P(AXES, None), P(AXES), P(shard, None))
    out_specs = (P(shard, None), P(shard, None))
    return jax.shard_map(body, mesh=fine, in_specs=in_specs, out_specs=out_specs, check_vma=False)
```

```python
import functools
import math

import jax
import jax.numpy as jnp
from jax import lax
from jax.experimental import pallas as pl
from jax.experimental.pallas import tpu as pltpu
from jax.sharding import Mesh
from jax.sharding import PartitionSpec as P

HD = 256
NS_STEPS = 5
NZ, NY, NX, NC = 8, 4, 4, 2
RING = 4
AXES = ("z", "y", "x", "c")
PLANE = ("c", "y", "x")
COEF_A, COEF_B, COEF_C = 3.4445, -4.775, 2.0315
DECAY = 0.95
VMEM = 16 * 1024 * 1024
LARGE = 48 * 1024 * 1024
bf16, f32 = jnp.bfloat16, jnp.float32


def device_at(z, y, x, c):
    return ((z * NY + y) * NX + x) * NC + c


def every_device():
    return [(z, y, x, c) for z in range(NZ) for y in range(NY) for x in range(NX) for c in range(NC)]


def shift(value, axis, distance):
    pairs = []
    for z, y, x, c in every_device():
        if axis == c:
            to = (y, (x + distance) % NX)
        else:
            to = ((y + distance) % NY, x)
        pairs.append((device_at(z, y, x, c), device_at(z, *to, c)))
    return lax.ppermute(value, AXES, pairs)


def swap_cores(value):
    return lax.ppermute(
        value, AXES, [(device_at(z, y, x, c), device_at(z, y, x, 1 - c)) for z, y, x, c in every_device()]
    )


def places():
    core, y, x = lax.axis_index("c"), lax.axis_index("y"), lax.axis_index("x")
    return jnp.where(core == 0, x, y), jnp.where(core == 0, y, x)


def head_columns(near, far, other=False):
    first, second = places()
    if other:
        first, second = second, first
    head = lax.rem(first + near, RING) * RING + lax.rem(second + far, RING)
    return pl.multiple_of(head * HD, HD)


def gather(grad, held, sems, nears, other):
    core = lax.axis_index("c")
    half = grad.shape[1] // NC
    base = (1 - core if other else core) * half
    copies = []
    for near in nears:
        for far in range(RING):
            k = len(copies)
            start = pl.multiple_of(base + head_columns(near, far, other), HD)
            copies.append(
                pltpu.make_async_copy(
                    grad.at[:, pl.ds(start, HD)], held.at[:, pl.ds(k * HD, HD)], sems.at[k]
                )
            )
            copies[-1].start()
    return copies


def first_kernel(nears, counts, latent, momentum, grad, lat, mom_own, mom_other, unit, piece, sems):
    copies = gather(grad, piece, sems, nears, True)
    core = lax.axis_index("c")
    slots, features = latent.shape
    live = lax.broadcasted_iota(jnp.int32, (slots, features), 0) < counts[0]
    lat[...] = jnp.where(live, latent[...], jnp.zeros_like(latent)).T
    depth, half = momentum.shape[0], momentum.shape[1] // NC
    for out, which in ((mom_own, core), (mom_other, 1 - core)):
        value = (DECAY / NZ) * momentum[:, pl.ds(pl.multiple_of(which * half, half), half)]
        high = value.astype(bf16)
        out[:depth, :] = high
        out[depth:, :] = (value - high.astype(f32)).astype(bf16)
    here = lax.axis_index("y") * NX + lax.axis_index("x")
    row = lax.broadcasted_iota(jnp.int32, unit.shape, 0)
    at = lax.broadcasted_iota(jnp.int32, unit.shape, 1)
    core_of = jnp.where(at < 2 * depth, core, 1 - core)
    unit[...] = (row == (here * NC + core_of) * depth + at % depth).astype(f32).astype(bf16)
    for copy in copies:
        copy.wait()


def first(counts, latent, momentum, grad, nears):
    slots, features = latent.shape
    depth, columns = momentum.shape
    heads = RING * len(nears)
    vmem = pl.BlockSpec(memory_space=pltpu.VMEM)
    mom = jax.ShapeDtypeStruct((2 * depth, columns // NC), bf16)
    return pl.pallas_call(
        functools.partial(first_kernel, nears),
        out_shape=[
            jax.ShapeDtypeStruct((features, slots), bf16),
            mom,
            mom,
            jax.ShapeDtypeStruct((features, 4 * depth), bf16),
            jax.ShapeDtypeStruct((slots, heads * HD), bf16),
        ],
        in_specs=[pl.BlockSpec(memory_space=pltpu.SMEM), vmem, vmem, pl.BlockSpec(memory_space=pl.ANY)],
        out_specs=[vmem] * 5,
        scratch_shapes=[pltpu.SemaphoreType.DMA((heads,))],
        compiler_params=pltpu.CompilerParams(vmem_limit_bytes=LARGE),
    )(counts, latent, momentum, grad)


def piece_kernel(nears, grad, piece, sems):
    for copy in gather(grad, piece, sems, nears, True):
        copy.wait()


def later_piece(grad, nears):
    heads = RING * len(nears)
    return pl.pallas_call(
        functools.partial(piece_kernel, nears),
        out_shape=jax.ShapeDtypeStruct((grad.shape[0], heads * HD), bf16),
        in_specs=[pl.BlockSpec(memory_space=pl.ANY)],
        out_specs=pl.BlockSpec(memory_space=pltpu.VMEM),
        scratch_shapes=[pltpu.SemaphoreType.DMA((heads,))],
        compiler_params=pltpu.CompilerParams(vmem_limit_bytes=LARGE),
    )(grad)


def own_kernel(nears, lat, grad, *refs):
    outs, (held, sems) = refs[: len(nears)], refs[len(nears) :]
    for copy in gather(grad, held, sems, nears, False):
        copy.wait()
    for k in range(RING * len(nears)):
        product = jnp.dot(lat[...], held[:, k * HD : (k + 1) * HD], preferred_element_type=f32)
        outs[k // RING][k % RING] = product.astype(bf16)


def own_products(lat, grad, nears):
    features, tokens = lat.shape
    heads = RING * len(nears)
    vmem = pl.BlockSpec(memory_space=pltpu.VMEM)
    return pl.pallas_call(
        functools.partial(own_kernel, nears),
        out_shape=[jax.ShapeDtypeStruct((RING, features, HD), bf16)] * len(nears),
        in_specs=[vmem, pl.BlockSpec(memory_space=pl.ANY)],
        out_specs=[vmem] * len(nears),
        scratch_shapes=[
            pltpu.VMEM((tokens, heads * HD), bf16),
            pltpu.SemaphoreType.DMA((heads,)),
        ],
        compiler_params=pltpu.CompilerParams(vmem_limit_bytes=LARGE),
        cost_estimate=pl.CostEstimate(
            flops=2 * heads * features * HD * tokens,
            bytes_accessed=heads * (tokens + features) * HD * 2,
            transcendentals=0,
        ),
    )(lat, grad)


def block_kernel(tiles, unit, lat, mom_own, mom_other, grad, *refs):
    count = 1 + max(t[0] for t in tiles)
    operands, outs = refs[:count], refs[count:]
    for operand, at_piece, result, near, fars in tiles:
        for place, far in enumerate(fars):
            at = pl.ds(head_columns(near, far), HD)
            in_piece = (at_piece * RING + far) * HD
            mom = jnp.concatenate([mom_own[:, at], mom_other[:, at]], axis=0)
            other = jnp.dot(lat[...], grad[:, in_piece : in_piece + HD], preferred_element_type=f32)
            added = jnp.dot(unit[...], mom, preferred_element_type=f32)
            total = operands[operand][far].astype(f32) + other.astype(bf16).astype(f32) + added
            outs[result][place] = total.astype(outs[result].dtype)


def block(own, held, which, unit, lat, mom_own, mom_other, grad):
    features, tokens = lat.shape
    nears = sorted({near for near, _ in which})
    tiles = [
        (nears.index(near), held.index(near), k, near, fars) for k, (near, fars) in enumerate(which)
    ]
    heads = sum(len(fars) for _, fars in which)
    return pl.pallas_call(
        functools.partial(block_kernel, tiles),
        out_shape=[
            jax.ShapeDtypeStruct((len(fars), features, HD), f32 if near == 0 else bf16)
            for near, fars in which
        ],
        compiler_params=pltpu.CompilerParams(vmem_limit_bytes=VMEM),
        cost_estimate=pl.CostEstimate(
            flops=2 * heads * features * HD * (tokens + unit.shape[1]),
            bytes_accessed=heads * (tokens + 2 * features) * HD * 2,
            transcendentals=0,
        ),
    )(unit, lat, mom_own, mom_other, grad, *[own[near] for near in nears])


def split(value):
    high = value.astype(bf16)
    return high, (value - high.astype(f32)).astype(bf16)


def product(a, b, dims):
    (left,), (right,) = dims
    return lax.dot_general(
        jnp.concatenate([a[0], a[0], a[1]], axis=left),
        jnp.concatenate([b[0], b[1], b[0]], axis=right),
        (dims, ((), ())),
        preferred_element_type=f32,
    )


def newton_schulz_kernel(moment_ref, out_ref):
    moment = moment_ref[...]
    rows, columns = moment.shape
    scale = 0.2 * math.sqrt(max(rows, columns))
    wide = moment.T
    gram = lax.dot_general(wide, wide, (((1,), (1,)), ((), ())), preferred_element_type=f32)
    wide = wide.astype(f32)
    inverse = 1.0 / (jnp.sqrt(jnp.sum(wide * wide)) + 1e-7)
    gram = (gram * inverse) * inverse
    x = wide * inverse
    for step in range(NS_STEPS):
        pair = split(x)
        if step > 0:
            gram = product(pair, pair, ((1,), (1,)))
        gram_pair = split(gram)
        poly = COEF_B * gram + COEF_C * product(gram_pair, gram_pair, ((1,), (0,)))
        x = COEF_A * x + product(split(poly), pair, ((1,), (0,)))
    update = (scale * x).T.astype(bf16)
    owners = out_ref.shape[0]
    depth = rows // owners
    for c in range(NC):
        for chip in range(owners // NC):
            at = slice((chip * NC + c) * depth, (chip * NC + c + 1) * depth)
            out_ref[c * (owners // NC) + chip, 0] = update[at, :]
            out_ref[c * (owners // NC) + chip, 1] = moment[at, :]


def newton_schulz(moment, owners):
    rows, columns = moment.shape
    return pl.pallas_call(
        newton_schulz_kernel,
        out_shape=jax.ShapeDtypeStruct((owners, 2, rows // owners, columns), bf16),
        compiler_params=pltpu.CompilerParams(vmem_limit_bytes=VMEM),
    )(moment)


def spread_kernel(returned, moment, update):
    for c in range(NC):
        for y in range(NY):
            for x in range(NX):
                source = (c * NY + y) * NX + x
                head = c * NY * NX + (RING * x + y if c == 0 else RING * y + x)
                at = slice(head * HD, (head + 1) * HD)
                update[:, at] = returned[source, 0]
                moment[:, at] = returned[source, 1].astype(f32)


def spread(returned):
    heads, _, rows, columns = returned.shape
    return pl.pallas_call(
        spread_kernel,
        out_shape=(
            jax.ShapeDtypeStruct((rows, heads * columns), f32),
            jax.ShapeDtypeStruct((rows, heads * columns), bf16),
        ),
        compiler_params=pltpu.CompilerParams(vmem_limit_bytes=VMEM),
    )(returned)


def body(latent, latent_grad, row_counts, momentum):
    features = latent.shape[1]
    order, rest = (2, 1, 3), (1, 2, 3)

    early, late = (2,), (1, 3, 0)
    lat_own, mom_own, mom_other, unit, piece_early = first(
        row_counts, latent, momentum, latent_grad, early
    )
    grad_late, piece_early = lax.optimization_barrier((latent_grad, piece_early))
    piece_early, lat_other, mom_other = (
        swap_cores(piece_early), swap_cores(lat_own), swap_cores(mom_other)
    )
    piece_late = swap_cores(later_piece(grad_late, late))
    shared = (unit, lat_other, mom_own, mom_other)

    own = dict(zip(early, own_products(lat_own, grad_late, early)))
    on = list(block(own, early, [(early[0], rest)], *shared, piece_early))
    lat_late, on[0] = lax.optimization_barrier((lat_own, on[0]))
    own.update(zip(late, own_products(lat_late, grad_late, late)))
    on += [block(own, late, [(k, rest)], *shared, piece_late)[0] for k in order[1:]]
    on = [shift(value, 0, k) for value, k in zip(on, order)]
    stay_early = block(own, early, [(k, (0,)) for k in early], *shared, piece_early)
    *stay_late, kept_stay, kept_on = block(
        own, late, [(1, (0,)), (3, (0,)), (0, (0,)), (0, rest)], *shared, piece_late
    )
    *stay, on[0] = lax.optimization_barrier((*stay_early, *stay_late, on[0]))
    stay = [shift(value, 0, k) for value, k in zip(stay, order)]

    total = kept_on + sum(value.astype(f32) for value in on)
    got = [shift(total[k - 1].astype(bf16), 1, k) for k in order]
    head = kept_stay[0] + sum(value[0].astype(f32) for value in stay)
    head = (head + sum(value.astype(f32) for value in got)).astype(bf16)

    pieces = lax.all_to_all(head.reshape(NZ, -1, HD), "z", 0, 0, tiled=True)
    eighth = jnp.sum(pieces.astype(f32), axis=0).astype(bf16)
    moment = lax.all_to_all(jnp.broadcast_to(eighth, (NZ,) + eighth.shape), "z", 0, 0, tiled=True)
    moment = moment.reshape(features, HD)

    outgoing = newton_schulz(moment, NC * NY * NX)
    returned = lax.all_to_all(outgoing, PLANE, 0, 0, tiled=True)
    return tuple(spread(returned))


def solution(mesh):
    fine = Mesh(mesh.devices.reshape(NZ, NY, NX, NC), AXES)
    shard = ("y", "x", "c")
    in_specs = (P(AXES, None), P(AXES, None), P(AXES), P(shard, None))
    out_specs = (P(shard, None), P(shard, None))
    return jax.shard_map(body, mesh=fine, in_specs=in_specs, out_specs=out_specs, check_vma=False)
```

```python
import functools
import math

import jax
import jax.numpy as jnp
from jax import lax
from jax.experimental import pallas as pl
from jax.experimental.pallas import tpu as pltpu
from jax.sharding import Mesh
from jax.sharding import PartitionSpec as P

HD = 256
NS_STEPS = 5
NZ, NY, NX, NC = 8, 4, 4, 2
RING = 4
AXES = ("z", "y", "x", "c")
PLANE = ("c", "y", "x")
COEF_A, COEF_B, COEF_C = 3.4445, -4.775, 2.0315
DECAY = 0.95
VMEM = 16 * 1024 * 1024
LARGE = 48 * 1024 * 1024
bf16, f32 = jnp.bfloat16, jnp.float32


def device_at(z, y, x, c):
    return ((z * NY + y) * NX + x) * NC + c


def every_device():
    return [(z, y, x, c) for z in range(NZ) for y in range(NY) for x in range(NX) for c in range(NC)]


def shift(value, axis, distance):
    pairs = []
    for z, y, x, c in every_device():
        if axis == c:
            to = (y, (x + distance) % NX)
        else:
            to = ((y + distance) % NY, x)
        pairs.append((device_at(z, y, x, c), device_at(z, *to, c)))
    return lax.ppermute(value, AXES, pairs)


def swap_cores(value):
    return lax.ppermute(
        value, AXES, [(device_at(z, y, x, c), device_at(z, y, x, 1 - c)) for z, y, x, c in every_device()]
    )


def places():
    core, y, x = lax.axis_index("c"), lax.axis_index("y"), lax.axis_index("x")
    return jnp.where(core == 0, x, y), jnp.where(core == 0, y, x)


def head_columns(near, far, other=False):
    first, second = places()
    if other:
        first, second = second, first
    head = lax.rem(first + near, RING) * RING + lax.rem(second + far, RING)
    return pl.multiple_of(head * HD, HD)


def pieces_kernel(groups, grad, *refs):
    outs, (held, sems) = refs[: len(groups)], refs[len(groups) :]
    base = (1 - lax.axis_index("c")) * (grad.shape[1] // NC)
    into, onto = [], []
    for nears, out in zip(groups, outs):
        for place, near in enumerate(nears):
            for far in range(RING):
                k = len(into)
                start = pl.multiple_of(base + head_columns(near, far, True), HD)
                target = (place * RING + far) * HD
                into.append(
                    pltpu.make_async_copy(grad.at[:, pl.ds(start, HD)], held.at[k], sems.at[0, k])
                )
                onto.append(
                    pltpu.make_async_copy(held.at[k], out.at[:, pl.ds(target, HD)], sems.at[1, k])
                )
    for copy in into:
        copy.start()
    for k in range(len(into)):
        into[k].wait()
        onto[k].start()
    for copy in onto:
        copy.wait()


def column_pieces(grad, groups):
    rows = grad.shape[0]
    count = RING * RING
    hbm = pl.BlockSpec(memory_space=pl.ANY)
    return pl.pallas_call(
        functools.partial(pieces_kernel, groups),
        out_shape=[jax.ShapeDtypeStruct((rows, len(g) * RING * HD), grad.dtype) for g in groups],
        in_specs=[hbm],
        out_specs=[hbm] * len(groups),
        scratch_shapes=[
            pltpu.VMEM((count, rows, HD), grad.dtype),
            pltpu.SemaphoreType.DMA((2, count)),
        ],
        compiler_params=pltpu.CompilerParams(vmem_limit_bytes=LARGE),
    )(grad)


def own_kernel(nears, depth, lat, grad, *refs):
    outs, (unit, held, sems) = refs[: len(nears)], refs[len(nears) :]
    base = lax.axis_index("c") * (grad.shape[1] // NC)
    copies = []
    for near in nears:
        for far in range(RING):
            k = len(copies)
            start = pl.multiple_of(base + head_columns(near, far), HD)
            copies.append(
                pltpu.make_async_copy(grad.at[:, pl.ds(start, HD)], held.at[k], sems.at[k])
            )
            copies[k].start()

    core = lax.axis_index("c")
    here = lax.axis_index("y") * NX + lax.axis_index("x")
    row = lax.broadcasted_iota(jnp.int32, unit.shape, 0)
    at = lax.broadcasted_iota(jnp.int32, unit.shape, 1)
    core_of = jnp.where((at // depth) % 2 == 0, core, 1 - core)
    unit[...] = (row == (here * NC + core_of) * depth + at % depth).astype(f32).astype(bf16)

    for copy in copies:
        copy.wait()
    for k in range(len(copies)):
        value = jnp.dot(lat[...], held[k], preferred_element_type=f32)
        outs[k // RING][k % RING] = value.astype(bf16)


def own_products(lat, grad, depth, nears):
    features, tokens = lat.shape
    count = RING * len(nears)
    vmem = pl.BlockSpec(memory_space=pltpu.VMEM)
    return pl.pallas_call(
        functools.partial(own_kernel, nears, depth),
        out_shape=[jax.ShapeDtypeStruct((RING, features, HD), bf16)] * len(nears)
        + [jax.ShapeDtypeStruct((features, 4 * depth), bf16)],
        in_specs=[vmem, pl.BlockSpec(memory_space=pl.ANY)],
        out_specs=[vmem] * (len(nears) + 1),
        scratch_shapes=[
            pltpu.VMEM((count, tokens, HD), bf16),
            pltpu.SemaphoreType.DMA((count,)),
        ],
        compiler_params=pltpu.CompilerParams(vmem_limit_bytes=LARGE),
        cost_estimate=pl.CostEstimate(
            flops=2 * count * features * HD * tokens,
            bytes_accessed=count * (tokens + features) * HD * 2,
            transcendentals=0,
        ),
    )(lat, grad)


def block_kernel(tiles, unit, lat, mom_own, mom_other, grad, *refs):
    count = 1 + max(t[0] for t in tiles)
    operands, outs = refs[:count], refs[count:]
    for operand, at_piece, result, near, fars in tiles:
        for place, far in enumerate(fars):
            at = pl.ds(head_columns(near, far), HD)
            in_piece = (at_piece * RING + far) * HD
            high, low = [], []
            for ref in (mom_own, mom_other):
                value = (DECAY / NZ) * ref[:, at]
                high.append(value.astype(bf16))
                low.append((value - high[-1].astype(f32)).astype(bf16))
            mom = jnp.concatenate(high + low, axis=0)
            other = jnp.dot(lat[...], grad[:, in_piece : in_piece + HD], preferred_element_type=f32)
            added = jnp.dot(unit[...], mom, preferred_element_type=f32)
            total = operands[operand][far].astype(f32) + other.astype(bf16).astype(f32) + added
            outs[result][place] = total.astype(outs[result].dtype)


def block(own, held, which, unit, lat, mom_own, mom_other, grad):
    features, tokens = lat.shape
    nears = sorted({near for near, _ in which})
    tiles = [
        (nears.index(near), held.index(near), k, near, fars) for k, (near, fars) in enumerate(which)
    ]
    heads = sum(len(fars) for _, fars in which)
    return pl.pallas_call(
        functools.partial(block_kernel, tiles),
        out_shape=[
            jax.ShapeDtypeStruct((len(fars), features, HD), f32 if near == 0 else bf16)
            for near, fars in which
        ],
        compiler_params=pltpu.CompilerParams(vmem_limit_bytes=VMEM),
        cost_estimate=pl.CostEstimate(
            flops=2 * heads * features * HD * (tokens + unit.shape[1]),
            bytes_accessed=heads * (tokens + 2 * features) * HD * 2,
            transcendentals=0,
        ),
    )(unit, lat, mom_own, mom_other, grad, *[own[near] for near in nears])


def split(value):
    high = value.astype(bf16)
    return high, (value - high.astype(f32)).astype(bf16)


def product(a, b, dims):
    (left,), (right,) = dims
    return lax.dot_general(
        jnp.concatenate([a[0], a[0], a[1]], axis=left),
        jnp.concatenate([b[0], b[1], b[0]], axis=right),
        (dims, ((), ())),
        preferred_element_type=f32,
    )


def newton_schulz_kernel(moment_ref, out_ref):
    moment = moment_ref[...]
    rows, columns = moment.shape
    scale = 0.2 * math.sqrt(max(rows, columns))
    wide = moment.T
    gram = lax.dot_general(wide, wide, (((1,), (1,)), ((), ())), preferred_element_type=f32)
    wide = wide.astype(f32)
    inverse = 1.0 / (jnp.sqrt(jnp.sum(wide * wide)) + 1e-7)
    gram = (gram * inverse) * inverse
    x = wide * inverse
    for step in range(NS_STEPS):
        pair = split(x)
        if step > 0:
            gram = product(pair, pair, ((1,), (1,)))
        gram_pair = split(gram)
        poly = COEF_B * gram + COEF_C * product(gram_pair, gram_pair, ((1,), (0,)))
        x = COEF_A * x + product(split(poly), pair, ((1,), (0,)))
    update = (scale * x).T.astype(bf16)
    owners = out_ref.shape[0]
    depth = rows // owners
    for c in range(NC):
        for chip in range(owners // NC):
            at = slice((chip * NC + c) * depth, (chip * NC + c + 1) * depth)
            out_ref[c * (owners // NC) + chip, 0] = update[at, :]
            out_ref[c * (owners // NC) + chip, 1] = moment[at, :]


def newton_schulz(moment, owners):
    rows, columns = moment.shape
    return pl.pallas_call(
        newton_schulz_kernel,
        out_shape=jax.ShapeDtypeStruct((owners, 2, rows // owners, columns), bf16),
        compiler_params=pltpu.CompilerParams(vmem_limit_bytes=VMEM),
    )(moment)


def spread_kernel(returned, moment, update):
    for c in range(NC):
        for y in range(NY):
            for x in range(NX):
                source = (c * NY + y) * NX + x
                head = c * NY * NX + (RING * x + y if c == 0 else RING * y + x)
                at = slice(head * HD, (head + 1) * HD)
                update[:, at] = returned[source, 0]
                moment[:, at] = returned[source, 1].astype(f32)


def spread(returned):
    heads, _, rows, columns = returned.shape
    return pl.pallas_call(
        spread_kernel,
        out_shape=(
            jax.ShapeDtypeStruct((rows, heads * columns), f32),
            jax.ShapeDtypeStruct((rows, heads * columns), bf16),
        ),
        compiler_params=pltpu.CompilerParams(vmem_limit_bytes=VMEM),
    )(returned)


def body(latent, latent_grad, row_counts, momentum):
    c = lax.axis_index("c")
    slots, features = latent.shape
    depth, columns = momentum.shape[0], momentum.shape[1] // NC
    order, rest = (2, 1, 3), (1, 2, 3)
    tie = lax.optimization_barrier

    early, late = (2,), (1, 3, 0)
    piece_early, piece_late = column_pieces(latent_grad, (early, late))
    piece_early = swap_cores(piece_early)
    live = lax.broadcasted_iota(jnp.int32, (slots, 1), 0) < row_counts[0]
    lat_own = jnp.where(live, latent, jnp.zeros_like(latent)).T
    lat_other = swap_cores(lat_own)
    mom_own = lax.dynamic_slice_in_dim(momentum, c * columns, columns, 1)
    mom_other = swap_cores(lax.dynamic_slice_in_dim(momentum, (1 - c) * columns, columns, 1))
    own_early, unit = own_products(lat_own, latent_grad, depth, early)
    piece_late, piece_early, lat_other, mom_other, own_early = tie(
        (piece_late, piece_early, lat_other, mom_other, own_early)
    )
    piece_late = swap_cores(piece_late)
    shared = (unit, lat_other, mom_own, mom_other)

    own = {2: own_early}
    (first_on,) = block(own, early, [(2, rest)], *shared, piece_early)
    lat_late, first_on = tie((lat_own, first_on))
    own[1], own[3], own[0], _ = own_products(lat_late, latent_grad, depth, late)
    on = [first_on] + [block(own, late, [(k, rest)], *shared, piece_late)[0] for k in order[1:]]
    on = [shift(value, 0, k) for value, k in zip(on, order)]
    (stay,) = block(own, early, [(2, (0,))], *shared, piece_early)
    *stays, kept_stay, kept_on = block(
        own, late, [(1, (0,)), (3, (0,)), (0, (0,)), (0, rest)], *shared, piece_late
    )
    stay = [shift(value, 0, k) for value, k in zip([stay] + stays, order)]

    total = kept_on + sum(value.astype(f32) for value in on)
    got = [shift(total[k - 1].astype(bf16), 1, k) for k in order]
    head = kept_stay[0] + sum(value[0].astype(f32) for value in stay)
    head = (head + sum(value.astype(f32) for value in got)).astype(bf16)

    pieces = lax.all_to_all(head.reshape(NZ, -1, HD), "z", 0, 0, tiled=True)
    piece = jnp.sum(pieces.astype(f32), axis=0).astype(bf16)
    moment = lax.all_to_all(jnp.broadcast_to(piece, (NZ,) + piece.shape), "z", 0, 0, tiled=True)
    moment = moment.reshape(features, HD)

    outgoing = newton_schulz(moment, NC * NY * NX)
    returned = lax.all_to_all(outgoing, PLANE, 0, 0, tiled=True)
    return tuple(spread(returned))


def solution(mesh):
    fine = Mesh(mesh.devices.reshape(NZ, NY, NX, NC), AXES)
    shard = ("y", "x", "c")
    in_specs = (P(AXES, None), P(AXES, None), P(AXES), P(shard, None))
    out_specs = (P(shard, None), P(shard, None))
    return jax.shard_map(body, mesh=fine, in_specs=in_specs, out_specs=out_specs, check_vma=False)
```

```python
import functools
import math

import jax
import jax.numpy as jnp
from jax import lax
from jax.experimental import pallas as pl
from jax.experimental.pallas import tpu as pltpu
from jax.sharding import Mesh
from jax.sharding import PartitionSpec as P

HD = 256
NS_STEPS = 5
NZ, NY, NX, NC = 8, 4, 4, 2
RING = 4
AXES = ("z", "y", "x", "c")
PLANE = ("c", "y", "x")
COEF_A, COEF_B, COEF_C = 3.4445, -4.775, 2.0315
DECAY = 0.95
VMEM = 16 * 1024 * 1024
LARGE = 48 * 1024 * 1024
bf16, f32 = jnp.bfloat16, jnp.float32


def device_at(z, y, x, c):
    return ((z * NY + y) * NX + x) * NC + c


def every_device():
    return [(z, y, x, c) for z in range(NZ) for y in range(NY) for x in range(NX) for c in range(NC)]


def shift(value, axis, distance):
    pairs = []
    for z, y, x, c in every_device():
        if axis == c:
            to = (y, (x + distance) % NX)
        else:
            to = ((y + distance) % NY, x)
        pairs.append((device_at(z, y, x, c), device_at(z, *to, c)))
    return lax.ppermute(value, AXES, pairs)


def swap_cores(value):
    return lax.ppermute(
        value, AXES, [(device_at(z, y, x, c), device_at(z, y, x, 1 - c)) for z, y, x, c in every_device()]
    )


def places():
    core, y, x = lax.axis_index("c"), lax.axis_index("y"), lax.axis_index("x")
    return jnp.where(core == 0, x, y), jnp.where(core == 0, y, x)


def head_columns(near, far, other=False):
    first, second = places()
    if other:
        first, second = second, first
    head = lax.rem(first + near, RING) * RING + lax.rem(second + far, RING)
    return pl.multiple_of(head * HD, HD)


def gather(grad, held, sems, nears, other):
    core = lax.axis_index("c")
    base = (1 - core if other else core) * (grad.shape[1] // NC)
    copies = []
    for near in nears:
        for far in range(RING):
            k = len(copies)
            start = pl.multiple_of(base + head_columns(near, far, other), HD)
            copies.append(
                pltpu.make_async_copy(grad.at[:, pl.ds(start, HD)], held.at[k], sems.at[k])
            )
    return copies


def pieces_kernel(groups, grad, early, late, mine, held, sems_in, sems_out):
    lists = [(groups[0], True), (groups[1], True), (groups[0], False)]
    into, onto = [], []
    for (nears, other), out in zip(lists, (early, late, mine)):
        at = len(into)
        count = RING * len(nears)
        into += gather(grad, held.at[pl.ds(at, count)], sems_in.at[pl.ds(at, count)], nears, other)
        for k in range(count):
            onto.append(
                pltpu.make_async_copy(
                    held.at[at + k], out.at[:, k * HD : (k + 1) * HD], sems_out.at[at + k]
                )
            )
    for copy in into:
        copy.start()
    for k in range(len(into)):
        into[k].wait()
        onto[k].start()
    for copy in onto:
        copy.wait()


def column_pieces(grad, groups):
    slots = grad.shape[0]
    widths = [RING * len(nears) for nears in (groups[0], groups[1], groups[0])]
    hbm = pl.BlockSpec(memory_space=pl.ANY)
    return pl.pallas_call(
        functools.partial(pieces_kernel, groups),
        out_shape=[jax.ShapeDtypeStruct((slots, width * HD), bf16) for width in widths],
        in_specs=[hbm],
        out_specs=[hbm] * 3,
        scratch_shapes=[
            pltpu.VMEM((sum(widths), slots, HD), bf16),
            pltpu.SemaphoreType.DMA((sum(widths),)),
            pltpu.SemaphoreType.DMA((sum(widths),)),
        ],
        compiler_params=pltpu.CompilerParams(vmem_limit_bytes=LARGE),
    )(grad)


def first_kernel(counts, latent, momentum, mine, lat, mom_own, mom_other, unit, own):
    core = lax.axis_index("c")
    slots, features = latent.shape
    depth, half = momentum.shape[0], momentum.shape[1] // NC
    live = lax.broadcasted_iota(jnp.int32, (slots, features), 0) < counts[0]
    lat[...] = jnp.where(live, latent[...], jnp.zeros_like(latent)).T
    for out, which in ((mom_own, core), (mom_other, 1 - core)):
        value = (DECAY / NZ) * momentum[:, pl.ds(pl.multiple_of(which * half, half), half)]
        high = value.astype(bf16)
        out[:depth, :] = high
        out[depth:, :] = (value - high.astype(f32)).astype(bf16)
    here = lax.axis_index("y") * NX + lax.axis_index("x")
    row = lax.broadcasted_iota(jnp.int32, unit.shape, 0)
    at = lax.broadcasted_iota(jnp.int32, unit.shape, 1)
    core_of = jnp.where(at < 2 * depth, core, 1 - core)
    unit[...] = (row == (here * NC + core_of) * depth + at % depth).astype(f32).astype(bf16)
    for far in range(RING):
        columns = mine[:, far * HD : (far + 1) * HD]
        own[far] = jnp.dot(lat[...], columns, preferred_element_type=f32).astype(bf16)


def first(counts, latent, momentum, mine):
    slots, features = latent.shape
    depth, columns = momentum.shape
    vmem = pl.BlockSpec(memory_space=pltpu.VMEM)
    mom = jax.ShapeDtypeStruct((2 * depth, columns // NC), bf16)
    return pl.pallas_call(
        first_kernel,
        out_shape=[
            jax.ShapeDtypeStruct((features, slots), bf16),
            mom,
            mom,
            jax.ShapeDtypeStruct((features, 4 * depth), bf16),
            jax.ShapeDtypeStruct((RING, features, HD), bf16),
        ],
        in_specs=[pl.BlockSpec(memory_space=pltpu.SMEM), vmem, vmem, vmem],
        compiler_params=pltpu.CompilerParams(vmem_limit_bytes=VMEM),
    )(counts, latent, momentum, mine)


def own_kernel(nears, lat, grad, *refs):
    outs, (held, sems) = refs[: len(nears)], refs[len(nears) :]
    copies = gather(grad, held, sems, nears, False)
    for copy in copies:
        copy.start()
    for near in range(len(nears)):
        for far in range(RING):
            copies[near * RING + far].wait()
        for far in range(RING):
            value = jnp.dot(lat[...], held[near * RING + far], preferred_element_type=f32)
            outs[near][far] = value.astype(bf16)


def own_products(lat, grad, nears):
    features, tokens = lat.shape
    count = RING * len(nears)
    vmem = pl.BlockSpec(memory_space=pltpu.VMEM)
    return pl.pallas_call(
        functools.partial(own_kernel, nears),
        out_shape=[jax.ShapeDtypeStruct((RING, features, HD), bf16)] * len(nears),
        in_specs=[vmem, pl.BlockSpec(memory_space=pl.ANY)],
        out_specs=[vmem] * len(nears),
        scratch_shapes=[
            pltpu.VMEM((count, tokens, HD), bf16),
            pltpu.SemaphoreType.DMA((count,)),
        ],
        compiler_params=pltpu.CompilerParams(vmem_limit_bytes=LARGE),
        cost_estimate=pl.CostEstimate(
            flops=2 * count * features * HD * tokens,
            bytes_accessed=count * (tokens + features) * HD * 2,
            transcendentals=0,
        ),
    )(lat, grad)


def block_kernel(tiles, unit, lat, mom_own, mom_other, grad, *refs):
    count = 1 + max(t[0] for t in tiles)
    operands, outs = refs[:count], refs[count:]
    for operand, at_piece, result, near, fars in tiles:
        for place, far in enumerate(fars):
            at = pl.ds(head_columns(near, far), HD)
            in_piece = (at_piece * RING + far) * HD
            mom = jnp.concatenate([mom_own[:, at], mom_other[:, at]], axis=0)
            other = jnp.dot(lat[...], grad[:, in_piece : in_piece + HD], preferred_element_type=f32)
            added = jnp.dot(unit[...], mom, preferred_element_type=f32)
            total = operands[operand][far].astype(f32) + other.astype(bf16).astype(f32) + added
            outs[result][place] = total.astype(outs[result].dtype)


def block(own, held, which, unit, lat, mom_own, mom_other, grad):
    features, tokens = lat.shape
    nears = sorted({near for near, _ in which})
    tiles = [
        (nears.index(near), held.index(near), k, near, fars) for k, (near, fars) in enumerate(which)
    ]
    heads = sum(len(fars) for _, fars in which)
    return pl.pallas_call(
        functools.partial(block_kernel, tiles),
        out_shape=[
            jax.ShapeDtypeStruct((len(fars), features, HD), f32 if near == 0 else bf16)
            for near, fars in which
        ],
        compiler_params=pltpu.CompilerParams(vmem_limit_bytes=VMEM),
        cost_estimate=pl.CostEstimate(
            flops=2 * heads * features * HD * (tokens + unit.shape[1]),
            bytes_accessed=heads * (tokens + 2 * features) * HD * 2,
            transcendentals=0,
        ),
    )(unit, lat, mom_own, mom_other, grad, *[own[near] for near in nears])


def split(value):
    high = value.astype(bf16)
    return high, (value - high.astype(f32)).astype(bf16)


def product(a, b, dims):
    (left,), (right,) = dims
    return lax.dot_general(
        jnp.concatenate([a[0], a[0], a[1]], axis=left),
        jnp.concatenate([b[0], b[1], b[0]], axis=right),
        (dims, ((), ())),
        preferred_element_type=f32,
    )


def newton_schulz_kernel(moment_ref, out_ref):
    moment = moment_ref[...]
    rows, columns = moment.shape
    scale = 0.2 * math.sqrt(max(rows, columns))
    wide = moment.T
    gram = lax.dot_general(wide, wide, (((1,), (1,)), ((), ())), preferred_element_type=f32)
    wide = wide.astype(f32)
    inverse = 1.0 / (jnp.sqrt(jnp.sum(wide * wide)) + 1e-7)
    gram = (gram * inverse) * inverse
    x = wide * inverse
    for step in range(NS_STEPS):
        pair = split(x)
        if step > 0:
            gram = product(pair, pair, ((1,), (1,)))
        gram_pair = split(gram)
        poly = COEF_B * gram + COEF_C * product(gram_pair, gram_pair, ((1,), (0,)))
        x = COEF_A * x + product(split(poly), pair, ((1,), (0,)))
    update = (scale * x).T.astype(bf16)
    owners = out_ref.shape[0]
    depth = rows // owners
    for c in range(NC):
        for chip in range(owners // NC):
            at = slice((chip * NC + c) * depth, (chip * NC + c + 1) * depth)
            out_ref[c * (owners // NC) + chip, 0] = update[at, :]
            out_ref[c * (owners // NC) + chip, 1] = moment[at, :]


def newton_schulz(moment, owners):
    rows, columns = moment.shape
    return pl.pallas_call(
        newton_schulz_kernel,
        out_shape=jax.ShapeDtypeStruct((owners, 2, rows // owners, columns), bf16),
        compiler_params=pltpu.CompilerParams(vmem_limit_bytes=VMEM),
    )(moment)


def spread_kernel(returned, moment, update):
    for c in range(NC):
        for y in range(NY):
            for x in range(NX):
                source = (c * NY + y) * NX + x
                head = c * NY * NX + (RING * x + y if c == 0 else RING * y + x)
                at = slice(head * HD, (head + 1) * HD)
                update[:, at] = returned[source, 0]
                moment[:, at] = returned[source, 1].astype(f32)


def spread(returned):
    heads, _, rows, columns = returned.shape
    return pl.pallas_call(
        spread_kernel,
        out_shape=(
            jax.ShapeDtypeStruct((rows, heads * columns), f32),
            jax.ShapeDtypeStruct((rows, heads * columns), bf16),
        ),
        compiler_params=pltpu.CompilerParams(vmem_limit_bytes=VMEM),
    )(returned)


def body(latent, latent_grad, row_counts, momentum):
    features = latent.shape[1]
    order, rest = (2, 1, 3), (1, 2, 3)
    tie = lax.optimization_barrier

    early, late = (2,), (1, 3, 0)
    piece_early, piece_late, mine = column_pieces(latent_grad, (early, late))
    lat_own, mom_own, mom_other, unit, own_early = first(row_counts, latent, momentum, mine)
    piece_early, lat_other, mom_other = (
        swap_cores(piece_early), swap_cores(lat_own), swap_cores(mom_other)
    )
    piece_late, piece_early, lat_other, mom_other = tie(
        (piece_late, piece_early, lat_other, mom_other)
    )
    piece_late = swap_cores(piece_late)
    shared = (unit, lat_other, mom_own, mom_other)

    own = {2: own_early}
    (first_on,) = block(own, early, [(2, rest)], *shared, piece_early)
    lat_late, first_on = tie((lat_own, first_on))
    own[1], own[3], own[0] = own_products(lat_late, latent_grad, late)
    on = [first_on] + [block(own, late, [(k, rest)], *shared, piece_late)[0] for k in order[1:]]
    on = [shift(value, 0, k) for value, k in zip(on, order)]
    (stay,) = block(own, early, [(2, (0,))], *shared, piece_early)
    *stays, kept_stay, kept_on = block(
        own, late, [(1, (0,)), (3, (0,)), (0, (0,)), (0, rest)], *shared, piece_late
    )
    stay = [shift(value, 0, k) for value, k in zip([stay] + stays, order)]

    total = kept_on + sum(value.astype(f32) for value in on)
    got = [shift(total[k - 1].astype(bf16), 1, k) for k in order]
    head = kept_stay[0] + sum(value[0].astype(f32) for value in stay)
    head = (head + sum(value.astype(f32) for value in got)).astype(bf16)

    pieces = lax.all_to_all(head.reshape(NZ, -1, HD), "z", 0, 0, tiled=True)
    piece = jnp.sum(pieces.astype(f32), axis=0).astype(bf16)
    moment = lax.all_to_all(jnp.broadcast_to(piece, (NZ,) + piece.shape), "z", 0, 0, tiled=True)
    moment = moment.reshape(features, HD)

    outgoing = newton_schulz(moment, NC * NY * NX)
    returned = lax.all_to_all(outgoing, PLANE, 0, 0, tiled=True)
    return tuple(spread(returned))


def solution(mesh):
    fine = Mesh(mesh.devices.reshape(NZ, NY, NX, NC), AXES)
    shard = ("y", "x", "c")
    in_specs = (P(AXES, None), P(AXES, None), P(AXES), P(shard, None))
    out_specs = (P(shard, None), P(shard, None))
    return jax.shard_map(body, mesh=fine, in_specs=in_specs, out_specs=out_specs, check_vma=False)
```

```python
import functools
import math

import jax
import jax.numpy as jnp
from jax import lax
from jax.experimental import pallas as pl
from jax.experimental.pallas import tpu as pltpu
from jax.sharding import Mesh
from jax.sharding import PartitionSpec as P

HD = 256
NS_STEPS = 5
NZ, NY, NX, NC = 8, 4, 4, 2
RING = 4
AXES = ("z", "y", "x", "c")
PLANE = ("c", "y", "x")
COEF_A, COEF_B, COEF_C = 3.4445, -4.775, 2.0315
DECAY = 0.95
VMEM = 16 * 1024 * 1024
MIDDLE = 5 * 10**9
LARGE = 48 * 1024 * 1024
bf16, f32 = jnp.bfloat16, jnp.float32


def device_at(z, y, x, c):
    return ((z * NY + y) * NX + x) * NC + c


def every_device():
    return [(z, y, x, c) for z in range(NZ) for y in range(NY) for x in range(NX) for c in range(NC)]


def shift(value, axis, distance):
    pairs = []
    for z, y, x, c in every_device():
        if axis == c:
            to = (y, (x + distance) % NX)
        else:
            to = ((y + distance) % NY, x)
        pairs.append((device_at(z, y, x, c), device_at(z, *to, c)))
    return lax.ppermute(value, AXES, pairs)


def swap_cores(value):
    return lax.ppermute(
        value, AXES, [(device_at(z, y, x, c), device_at(z, y, x, 1 - c)) for z, y, x, c in every_device()]
    )


def places():
    core, y, x = lax.axis_index("c"), lax.axis_index("y"), lax.axis_index("x")
    return jnp.where(core == 0, x, y), jnp.where(core == 0, y, x)


def head_columns(near, far, other=False):
    first, second = places()
    if other:
        first, second = second, first
    head = lax.rem(first + near, RING) * RING + lax.rem(second + far, RING)
    return pl.multiple_of(head * HD, HD)


def gather(grad, held, sems, nears, other):
    core = lax.axis_index("c")
    base = (1 - core if other else core) * (grad.shape[1] // NC)
    copies = []
    for near in nears:
        for far in range(RING):
            k = len(copies)
            start = pl.multiple_of(base + head_columns(near, far, other), HD)
            copies.append(
                pltpu.make_async_copy(grad.at[:, pl.ds(start, HD)], held.at[k], sems.at[k])
            )
    return copies


def pieces_kernel(groups, grad, early, late, mine, held, sems_in, sems_out):
    lists = [(groups[0], True), (groups[1], True), (groups[0], False)]
    into, onto = [], []
    for (nears, other), out in zip(lists, (early, late, mine)):
        at = len(into)
        count = RING * len(nears)
        into += gather(grad, held.at[pl.ds(at, count)], sems_in.at[pl.ds(at, count)], nears, other)
        for k in range(count):
            onto.append(
                pltpu.make_async_copy(
                    held.at[at + k], out.at[:, k * HD : (k + 1) * HD], sems_out.at[at + k]
                )
            )
    for copy in into:
        copy.start()
    for k in range(len(into)):
        into[k].wait()
        onto[k].start()
    for copy in onto:
        copy.wait()


def column_pieces(grad, groups):
    slots = grad.shape[0]
    widths = [RING * len(nears) for nears in (groups[0], groups[1], groups[0])]
    hbm = pl.BlockSpec(memory_space=pl.ANY)
    return pl.pallas_call(
        functools.partial(pieces_kernel, groups),
        out_shape=[jax.ShapeDtypeStruct((slots, width * HD), bf16) for width in widths],
        in_specs=[hbm],
        out_specs=[hbm] * 3,
        scratch_shapes=[
            pltpu.VMEM((sum(widths), slots, HD), bf16),
            pltpu.SemaphoreType.DMA((sum(widths),)),
            pltpu.SemaphoreType.DMA((sum(widths),)),
        ],
        compiler_params=pltpu.CompilerParams(vmem_limit_bytes=LARGE),
    )(grad)


def first_kernel(counts, latent, momentum, mine, lat, mom_own, mom_other, unit, own):
    core = lax.axis_index("c")
    slots, features = latent.shape
    depth, half = momentum.shape[0], momentum.shape[1] // NC
    live = lax.broadcasted_iota(jnp.int32, (slots, features), 0) < counts[0]
    lat[...] = jnp.where(live, latent[...], jnp.zeros_like(latent)).T
    for out, which in ((mom_own, core), (mom_other, 1 - core)):
        value = (DECAY / NZ) * momentum[:, pl.ds(pl.multiple_of(which * half, half), half)]
        high = value.astype(bf16)
        out[:depth, :] = high
        out[depth:, :] = (value - high.astype(f32)).astype(bf16)
    here = lax.axis_index("y") * NX + lax.axis_index("x")
    row = lax.broadcasted_iota(jnp.int32, unit.shape, 0)
    at = lax.broadcasted_iota(jnp.int32, unit.shape, 1)
    core_of = jnp.where(at < 2 * depth, core, 1 - core)
    unit[...] = (row == (here * NC + core_of) * depth + at % depth).astype(f32).astype(bf16)
    for far in range(RING):
        columns = mine[:, far * HD : (far + 1) * HD]
        own[far] = jnp.dot(lat[...], columns, preferred_element_type=f32).astype(bf16)


def first(counts, latent, momentum, mine):
    slots, features = latent.shape
    depth, columns = momentum.shape
    vmem = pl.BlockSpec(memory_space=pltpu.VMEM)
    mom = jax.ShapeDtypeStruct((2 * depth, columns // NC), bf16)
    return pl.pallas_call(
        first_kernel,
        out_shape=[
            jax.ShapeDtypeStruct((features, slots), bf16),
            mom,
            mom,
            jax.ShapeDtypeStruct((features, 4 * depth), bf16),
            jax.ShapeDtypeStruct((RING, features, HD), bf16),
        ],
        in_specs=[pl.BlockSpec(memory_space=pltpu.SMEM), vmem, vmem, vmem],
        compiler_params=pltpu.CompilerParams(vmem_limit_bytes=VMEM),
    )(counts, latent, momentum, mine)


def own_kernel(nears, lat, grad, *refs):
    outs, (held, sems) = refs[: len(nears)], refs[len(nears) :]
    copies = gather(grad, held, sems, nears, False)
    for copy in copies:
        copy.start()
    for near in range(len(nears)):
        for far in range(RING):
            copies[near * RING + far].wait()
        for far in range(RING):
            value = jnp.dot(lat[...], held[near * RING + far], preferred_element_type=f32)
            outs[near][far] = value.astype(bf16)


def own_products(lat, grad, nears):
    features, tokens = lat.shape
    count = RING * len(nears)
    vmem = pl.BlockSpec(memory_space=pltpu.VMEM)
    return pl.pallas_call(
        functools.partial(own_kernel, nears),
        out_shape=[jax.ShapeDtypeStruct((RING, features, HD), bf16)] * len(nears),
        in_specs=[vmem, pl.BlockSpec(memory_space=pl.ANY)],
        out_specs=[vmem] * len(nears),
        scratch_shapes=[
            pltpu.VMEM((count, tokens, HD), bf16),
            pltpu.SemaphoreType.DMA((count,)),
        ],
        compiler_params=pltpu.CompilerParams(vmem_limit_bytes=LARGE),
        cost_estimate=pl.CostEstimate(
            flops=2 * count * features * HD * tokens,
            bytes_accessed=count * (tokens + features) * HD * 2,
            transcendentals=0,
        ),
    )(lat, grad)


def block_kernel(tiles, unit, lat, mom_own, mom_other, grad, *refs):
    count = 1 + max(t[0] for t in tiles)
    operands, outs = refs[:count], refs[count:]
    for (operand, at_piece, near, fars, row), out in zip(tiles, outs):
        rows = slice(row, row + out.shape[1])
        for place, far in enumerate(fars):
            at = pl.ds(head_columns(near, far), HD)
            in_piece = (at_piece * RING + far) * HD
            mom = jnp.concatenate([mom_own[:, at], mom_other[:, at]], axis=0)
            other = jnp.dot(
                lat[rows, :], grad[:, in_piece : in_piece + HD], preferred_element_type=f32
            )
            added = jnp.dot(unit[rows, :], mom, preferred_element_type=f32)
            total = operands[operand][far, rows].astype(f32) + other.astype(bf16).astype(f32) + added
            out[place] = total.astype(out.dtype)


def block(own, held, which, unit, lat, mom_own, mom_other, grad):
    tokens = lat.shape[1]
    nears = sorted({w[0] for w in which})
    tiles = [(nears.index(w[0]), held.index(w[0]), *w[:3]) for w in which]
    work = sum(len(w[1]) * w[3] for w in which)
    return pl.pallas_call(
        functools.partial(block_kernel, tiles),
        out_shape=[jax.ShapeDtypeStruct((len(w[1]), w[3], HD), w[4]) for w in which],
        compiler_params=pltpu.CompilerParams(vmem_limit_bytes=VMEM),
        cost_estimate=pl.CostEstimate(
            flops=2 * work * HD * (tokens + unit.shape[1]),
            bytes_accessed=work * HD * 4 + len(which) * RING * tokens * HD * 2,
            transcendentals=0,
        ),
    )(unit, lat, mom_own, mom_other, grad, *[own[near] for near in nears])


def middle_kernel(kept, upper, lower, one, three, two_a, two_b, kept_out, one_out, three_out):
    half = upper.shape[1]
    for k in range(kept.shape[0]):
        kept_out[k, :half] = kept[k, :half] + upper[k].astype(f32)
        kept_out[k, half:] = kept[k, half:] + lower[k].astype(f32)
    one_out[:half, :] = (one[0, :half] + two_a[0].astype(f32)).astype(bf16)
    one_out[half:, :] = one[0, half:].astype(bf16)
    three_out[:half, :] = three[0, :half].astype(bf16)
    three_out[half:, :] = (three[0, half:] + two_b[0].astype(f32)).astype(bf16)


def middle(kept, *parts):
    stay = jax.ShapeDtypeStruct(kept.shape[1:], bf16)
    return pl.pallas_call(
        middle_kernel,
        out_shape=[jax.ShapeDtypeStruct(kept.shape, f32), stay, stay],
        compiler_params=pltpu.CompilerParams(vmem_limit_bytes=VMEM),
        cost_estimate=pl.CostEstimate(flops=MIDDLE, bytes_accessed=0, transcendentals=0),
    )(kept, *parts)


def stay_kernel(kept, one, three, out):
    out[...] = kept[0] + one[...].astype(f32) + three[...].astype(f32)


def stay_sum(kept, one, three):
    return pl.pallas_call(
        stay_kernel,
        out_shape=jax.ShapeDtypeStruct(kept.shape[1:], f32),
        compiler_params=pltpu.CompilerParams(vmem_limit_bytes=VMEM),
        cost_estimate=pl.CostEstimate(flops=MIDDLE, bytes_accessed=0, transcendentals=0),
    )(kept, one, three)


def add_kernel(kept, upper, lower, *outs):
    half = upper.shape[1]
    for k, out in enumerate(outs):
        out[:half, :] = (kept[k, :half] + upper[k].astype(f32)).astype(out.dtype)
        out[half:, :] = (kept[k, half:] + lower[k].astype(f32)).astype(out.dtype)


def add_up(kept, *parts):
    heads, rows, columns = kept.shape
    return pl.pallas_call(
        add_kernel,
        out_shape=[jax.ShapeDtypeStruct((rows, columns), bf16)] * heads,
        compiler_params=pltpu.CompilerParams(vmem_limit_bytes=VMEM),
    )(kept, *parts)


def split(value):
    high = value.astype(bf16)
    return high, (value - high.astype(f32)).astype(bf16)


def product(a, b, dims):
    (left,), (right,) = dims
    return lax.dot_general(
        jnp.concatenate([a[0], a[0], a[1]], axis=left),
        jnp.concatenate([b[0], b[1], b[0]], axis=right),
        (dims, ((), ())),
        preferred_element_type=f32,
    )


def newton_schulz_kernel(moment_ref, out_ref):
    moment = moment_ref[...]
    rows, columns = moment.shape
    scale = 0.2 * math.sqrt(max(rows, columns))
    wide = moment.T
    gram = lax.dot_general(wide, wide, (((1,), (1,)), ((), ())), preferred_element_type=f32)
    wide = wide.astype(f32)
    inverse = 1.0 / (jnp.sqrt(jnp.sum(wide * wide)) + 1e-7)
    gram = (gram * inverse) * inverse
    x = wide * inverse
    for step in range(NS_STEPS):
        pair = split(x)
        if step > 0:
            gram = product(pair, pair, ((1,), (1,)))
        gram_pair = split(gram)
        poly = COEF_B * gram + COEF_C * product(gram_pair, gram_pair, ((1,), (0,)))
        x = COEF_A * x + product(split(poly), pair, ((1,), (0,)))
    update = (scale * x).T.astype(bf16)
    owners = out_ref.shape[0]
    depth = rows // owners
    for c in range(NC):
        for chip in range(owners // NC):
            at = slice((chip * NC + c) * depth, (chip * NC + c + 1) * depth)
            out_ref[c * (owners // NC) + chip, 0] = update[at, :]
            out_ref[c * (owners // NC) + chip, 1] = moment[at, :]


def newton_schulz(moment, owners):
    rows, columns = moment.shape
    return pl.pallas_call(
        newton_schulz_kernel,
        out_shape=jax.ShapeDtypeStruct((owners, 2, rows // owners, columns), bf16),
        compiler_params=pltpu.CompilerParams(vmem_limit_bytes=VMEM),
    )(moment)


def spread_kernel(returned, moment, update, moment_held, update_held, sems):
    half = moment_held.shape[1] // NC
    copies = []
    for c in range(NC):
        for y in range(NY):
            for x in range(NX):
                source = (c * NY + y) * NX + x
                head = c * NY * NX + (RING * x + y if c == 0 else RING * y + x)
                at = slice(head * HD, (head + 1) * HD)
                update_held[:, at] = returned[source, 0]
                moment_held[:, at] = returned[source, 1].astype(f32)
        done = pl.ds(c * half, half)
        for k, (held, out) in enumerate(((moment_held, moment), (update_held, update))):
            copies.append(pltpu.make_async_copy(held.at[:, done], out.at[:, done], sems.at[c, k]))
            copies[-1].start()
    for copy in copies:
        copy.wait()


def spread(returned):
    heads, _, rows, columns = returned.shape
    moment = jax.ShapeDtypeStruct((rows, heads * columns), f32)
    update = jax.ShapeDtypeStruct((rows, heads * columns), bf16)
    hbm = pl.BlockSpec(memory_space=pl.ANY)
    return pl.pallas_call(
        spread_kernel,
        out_shape=(moment, update),
        in_specs=[pl.BlockSpec(memory_space=pltpu.VMEM)],
        out_specs=(hbm, hbm),
        scratch_shapes=[
            pltpu.VMEM(moment.shape, f32),
            pltpu.VMEM(update.shape, bf16),
            pltpu.SemaphoreType.DMA((NC, 2)),
        ],
        compiler_params=pltpu.CompilerParams(vmem_limit_bytes=VMEM),
    )(returned)


def body(latent, latent_grad, row_counts, momentum):
    features = latent.shape[1]
    order = (2, 1, 3)
    tie = lax.optimization_barrier

    early, late = (2,), (1, 3, 0)
    piece_early, piece_late, mine = column_pieces(latent_grad, (early, late))
    lat_own, mom_own, mom_other, unit, own_early = first(row_counts, latent, momentum, mine)
    piece_early, lat_other, mom_other = (
        swap_cores(piece_early), swap_cores(lat_own), swap_cores(mom_other)
    )
    piece_late, piece_early, lat_other, mom_other = tie((piece_late, piece_early, lat_other, mom_other))
    piece_late = swap_cores(piece_late)
    shared = (unit, lat_other, mom_own, mom_other)

    half = features // 2
    upper, lower, whole = (0, half), (half, half), (0, features)
    every, rest, stay = (0, 1, 2, 3), (1, 2, 3), (0,)
    own = {2: own_early}
    two_a, two_b = block(
        own, early, [(2, every, *upper, bf16), (2, every, *lower, bf16)], *shared, piece_early
    )
    lat_late, two_a, two_b = tie((lat_own, two_a, two_b))
    own[1], own[3], own[0] = own_products(lat_late, latent_grad, late)
    (one_b,) = block(own, late, [(1, rest, *lower, bf16)], *shared, piece_late)
    (three_a,) = block(own, late, [(3, rest, *upper, bf16)], *shared, piece_late)
    own[0], one_b, three_a = tie((own[0], one_b, three_a))
    one_a, three_b, one_stay, three_stay, kept_on, kept_stay = block(
        own,
        late,
        [
            (1, rest, *upper, f32),
            (3, rest, *lower, f32),
            (1, stay, *whole, f32),
            (3, stay, *whole, f32),
            (0, rest, *whole, f32),
            (0, stay, *whole, f32),
        ],
        *shared,
        piece_late,
    )
    two_a, two_b = shift(two_a, 0, 1), shift(two_b, 0, 3)
    one_b, three_a = shift(one_b, 0, 1), shift(three_a, 0, 3)
    one_a = shift((one_a + two_a[1:].astype(f32)).astype(bf16), 0, 1)
    three_b = shift((three_b + two_b[1:].astype(f32)).astype(bf16), 0, 3)
    kept_on, one_stay, three_stay = middle(
        kept_on, three_a, one_b, one_stay, three_stay, two_a, two_b
    )
    one_stay, three_stay = shift(one_stay, 0, 1), shift(three_stay, 0, 3)

    sums = add_up(kept_on, one_a, three_b)
    got = [shift(sums[k - 1], 1, k) for k in order]
    head = stay_sum(kept_stay, one_stay, three_stay)
    head = (head + sum(value.astype(f32) for value in got)).astype(bf16)

    pieces = lax.all_to_all(head.reshape(NZ, -1, HD), "z", 0, 0, tiled=True)
    piece = jnp.sum(pieces.astype(f32), axis=0).astype(bf16)
    moment = lax.all_to_all(jnp.broadcast_to(piece, (NZ,) + piece.shape), "z", 0, 0, tiled=True)
    moment = moment.reshape(features, HD)

    outgoing = newton_schulz(moment, NC * NY * NX)
    returned = lax.all_to_all(outgoing, PLANE, 0, 0, tiled=True)
    return tuple(spread(returned))


def solution(mesh):
    fine = Mesh(mesh.devices.reshape(NZ, NY, NX, NC), AXES)
    shard = ("y", "x", "c")
    in_specs = (P(AXES, None), P(AXES, None), P(AXES), P(shard, None))
    out_specs = (P(shard, None), P(shard, None))
    return jax.shard_map(body, mesh=fine, in_specs=in_specs, out_specs=out_specs, check_vma=False)
```

```python
import functools
import math

import jax
import jax.numpy as jnp
from jax import lax
from jax.experimental import pallas as pl
from jax.experimental.pallas import tpu as pltpu
from jax.sharding import Mesh
from jax.sharding import PartitionSpec as P

HD = 256
NS_STEPS = 5
NZ, NY, NX, NC = 8, 4, 4, 2
RING = 4
AXES = ("z", "y", "x", "c")
PLANE = ("c", "y", "x")
COEF_A, COEF_B, COEF_C = 3.4445, -4.775, 2.0315
DECAY = 0.95
VMEM = 16 * 1024 * 1024
LARGE = 48 * 1024 * 1024
bf16, f32 = jnp.bfloat16, jnp.float32


def device_at(z, y, x, c):
    return ((z * NY + y) * NX + x) * NC + c


def every_device():
    return [(z, y, x, c) for z in range(NZ) for y in range(NY) for x in range(NX) for c in range(NC)]


def exchange(value, axis, distance):
    pairs = []
    for z, y, x, c in every_device():
        if axis == c:
            to = (y, x ^ distance)
        else:
            to = (y ^ distance, x)
        pairs.append((device_at(z, y, x, c), device_at(z, *to, c)))
    return lax.ppermute(value, AXES, pairs)


def swap_cores(value):
    return lax.ppermute(
        value, AXES, [(device_at(z, y, x, c), device_at(z, y, x, 1 - c)) for z, y, x, c in every_device()]
    )


def places():
    core, y, x = lax.axis_index("c"), lax.axis_index("y"), lax.axis_index("x")
    return jnp.where(core == 0, x, y), jnp.where(core == 0, y, x)


def head_columns(near, far, other=False):
    first, second = places()
    if other:
        first, second = second, first
    head = (first ^ near) * RING + (second ^ far)
    return pl.multiple_of(head * HD, HD)


def gather(grad, held, sems, nears, other):
    core = lax.axis_index("c")
    base = (1 - core if other else core) * (grad.shape[1] // NC)
    copies = []
    for near in nears:
        for far in range(RING):
            k = len(copies)
            start = pl.multiple_of(base + head_columns(near, far, other), HD)
            copies.append(
                pltpu.make_async_copy(grad.at[:, pl.ds(start, HD)], held.at[k], sems.at[k])
            )
    return copies


def pieces_kernel(groups, grad, early, late, mine, held, sems_in, sems_out):
    lists = [(groups[0], True), (groups[1], True), (groups[0], False)]
    into, onto = [], []
    for (nears, other), out in zip(lists, (early, late, mine)):
        at = len(into)
        count = RING * len(nears)
        into += gather(grad, held.at[pl.ds(at, count)], sems_in.at[pl.ds(at, count)], nears, other)
        for k in range(count):
            onto.append(
                pltpu.make_async_copy(
                    held.at[at + k], out.at[:, k * HD : (k + 1) * HD], sems_out.at[at + k]
                )
            )
    for copy in into:
        copy.start()
    for k in range(len(into)):
        into[k].wait()
        onto[k].start()
    for copy in onto:
        copy.wait()


def column_pieces(grad, groups):
    slots = grad.shape[0]
    widths = [RING * len(nears) for nears in (groups[0], groups[1], groups[0])]
    hbm = pl.BlockSpec(memory_space=pl.ANY)
    return pl.pallas_call(
        functools.partial(pieces_kernel, groups),
        out_shape=[jax.ShapeDtypeStruct((slots, width * HD), bf16) for width in widths],
        in_specs=[hbm],
        out_specs=[hbm] * 3,
        scratch_shapes=[
            pltpu.VMEM((sum(widths), slots, HD), bf16),
            pltpu.SemaphoreType.DMA((sum(widths),)),
            pltpu.SemaphoreType.DMA((sum(widths),)),
        ],
        compiler_params=pltpu.CompilerParams(vmem_limit_bytes=LARGE),
    )(grad)


def first_kernel(counts, latent, momentum, mine, lat, mom_own, mom_other, unit, own):
    core = lax.axis_index("c")
    slots, features = latent.shape
    depth, half = momentum.shape[0], momentum.shape[1] // NC
    live = lax.broadcasted_iota(jnp.int32, (slots, features), 0) < counts[0]
    lat[...] = jnp.where(live, latent[...], jnp.zeros_like(latent)).T
    for out, which in ((mom_own, core), (mom_other, 1 - core)):
        value = (DECAY / NZ) * momentum[:, pl.ds(pl.multiple_of(which * half, half), half)]
        high = value.astype(bf16)
        out[:depth, :] = high
        out[depth:, :] = (value - high.astype(f32)).astype(bf16)
    here = lax.axis_index("y") * NX + lax.axis_index("x")
    row = lax.broadcasted_iota(jnp.int32, unit.shape, 0)
    at = lax.broadcasted_iota(jnp.int32, unit.shape, 1)
    core_of = jnp.where(at < 2 * depth, core, 1 - core)
    unit[...] = (row == (here * NC + core_of) * depth + at % depth).astype(f32).astype(bf16)
    for far in range(RING):
        columns = mine[:, far * HD : (far + 1) * HD]
        own[far] = jnp.dot(lat[...], columns, preferred_element_type=f32).astype(bf16)


def first(counts, latent, momentum, mine):
    slots, features = latent.shape
    depth, columns = momentum.shape
    vmem = pl.BlockSpec(memory_space=pltpu.VMEM)
    mom = jax.ShapeDtypeStruct((2 * depth, columns // NC), bf16)
    return pl.pallas_call(
        first_kernel,
        out_shape=[
            jax.ShapeDtypeStruct((features, slots), bf16),
            mom,
            mom,
            jax.ShapeDtypeStruct((features, 4 * depth), bf16),
            jax.ShapeDtypeStruct((RING, features, HD), bf16),
        ],
        in_specs=[pl.BlockSpec(memory_space=pltpu.SMEM), vmem, vmem, vmem],
        compiler_params=pltpu.CompilerParams(vmem_limit_bytes=VMEM),
    )(counts, latent, momentum, mine)


def own_kernel(nears, lat, grad, *refs):
    outs, (held, sems) = refs[: len(nears)], refs[len(nears) :]
    copies = gather(grad, held, sems, nears, False)
    for copy in copies:
        copy.start()
    for near in range(len(nears)):
        for far in range(RING):
            copies[near * RING + far].wait()
        for far in range(RING):
            value = jnp.dot(lat[...], held[near * RING + far], preferred_element_type=f32)
            outs[near][far] = value.astype(bf16)


def own_products(lat, grad, nears):
    features, tokens = lat.shape
    count = RING * len(nears)
    vmem = pl.BlockSpec(memory_space=pltpu.VMEM)
    return pl.pallas_call(
        functools.partial(own_kernel, nears),
        out_shape=[jax.ShapeDtypeStruct((RING, features, HD), bf16)] * len(nears),
        in_specs=[vmem, pl.BlockSpec(memory_space=pl.ANY)],
        out_specs=[vmem] * len(nears),
        scratch_shapes=[
            pltpu.VMEM((count, tokens, HD), bf16),
            pltpu.SemaphoreType.DMA((count,)),
        ],
        compiler_params=pltpu.CompilerParams(vmem_limit_bytes=LARGE),
        cost_estimate=pl.CostEstimate(
            flops=2 * count * features * HD * tokens,
            bytes_accessed=count * (tokens + features) * HD * 2,
            transcendentals=0,
        ),
    )(lat, grad)


def block_kernel(tiles, unit, lat, mom_own, mom_other, grad, *refs):
    count = 1 + max(t[0] for t in tiles)
    operands, outs = refs[:count], refs[count:]
    for operand, at_piece, result, near, fars in tiles:
        for place, far in enumerate(fars):
            at = pl.ds(head_columns(near, far), HD)
            in_piece = (at_piece * RING + far) * HD
            mom = jnp.concatenate([mom_own[:, at], mom_other[:, at]], axis=0)
            other = jnp.dot(lat[...], grad[:, in_piece : in_piece + HD], preferred_element_type=f32)
            added = jnp.dot(unit[...], mom, preferred_element_type=f32)
            total = operands[operand][far].astype(f32) + other.astype(bf16).astype(f32) + added
            outs[result][place] = total.astype(outs[result].dtype)


def block(own, held, which, unit, lat, mom_own, mom_other, grad):
    features, tokens = lat.shape
    nears = sorted({near for near, _ in which})
    tiles = [
        (nears.index(near), held.index(near), k, near, fars) for k, (near, fars) in enumerate(which)
    ]
    heads = sum(len(fars) for _, fars in which)
    return pl.pallas_call(
        functools.partial(block_kernel, tiles),
        out_shape=[
            jax.ShapeDtypeStruct((len(fars), features, HD), f32 if near == 0 else bf16)
            for near, fars in which
        ],
        compiler_params=pltpu.CompilerParams(vmem_limit_bytes=VMEM),
        cost_estimate=pl.CostEstimate(
            flops=2 * heads * features * HD * (tokens + unit.shape[1]),
            bytes_accessed=heads * (tokens + 2 * features) * HD * 2,
            transcendentals=0,
        ),
    )(unit, lat, mom_own, mom_other, grad, *[own[near] for near in nears])


def split(value):
    high = value.astype(bf16)
    return high, (value - high.astype(f32)).astype(bf16)


def product(a, b, dims):
    (left,), (right,) = dims
    return lax.dot_general(
        jnp.concatenate([a[0], a[0], a[1]], axis=left),
        jnp.concatenate([b[0], b[1], b[0]], axis=right),
        (dims, ((), ())),
        preferred_element_type=f32,
    )


def newton_schulz_kernel(moment_ref, out_ref):
    moment = moment_ref[...]
    rows, columns = moment.shape
    scale = 0.2 * math.sqrt(max(rows, columns))
    wide = moment.T
    gram = lax.dot_general(wide, wide, (((1,), (1,)), ((), ())), preferred_element_type=f32)
    wide = wide.astype(f32)
    inverse = 1.0 / (jnp.sqrt(jnp.sum(wide * wide)) + 1e-7)
    gram = (gram * inverse) * inverse
    x = wide * inverse
    for step in range(NS_STEPS):
        pair = split(x)
        if step > 0:
            gram = product(pair, pair, ((1,), (1,)))
        gram_pair = split(gram)
        poly = COEF_B * gram + COEF_C * product(gram_pair, gram_pair, ((1,), (0,)))
        x = COEF_A * x + product(split(poly), pair, ((1,), (0,)))
    update = (scale * x).T.astype(bf16)
    owners = out_ref.shape[0]
    depth = rows // owners
    for c in range(NC):
        for chip in range(owners // NC):
            at = slice((chip * NC + c) * depth, (chip * NC + c + 1) * depth)
            out_ref[c * (owners // NC) + chip, 0] = update[at, :]
            out_ref[c * (owners // NC) + chip, 1] = moment[at, :]


def newton_schulz(moment, owners):
    rows, columns = moment.shape
    return pl.pallas_call(
        newton_schulz_kernel,
        out_shape=jax.ShapeDtypeStruct((owners, 2, rows // owners, columns), bf16),
        compiler_params=pltpu.CompilerParams(vmem_limit_bytes=VMEM),
    )(moment)


def spread_kernel(returned, moment, update, moment_held, update_held, sems):
    half = moment_held.shape[1] // NC
    copies = []
    for c in range(NC):
        for y in range(NY):
            for x in range(NX):
                source = (c * NY + y) * NX + x
                head = c * NY * NX + (RING * x + y if c == 0 else RING * y + x)
                at = slice(head * HD, (head + 1) * HD)
                update_held[:, at] = returned[source, 0]
                moment_held[:, at] = returned[source, 1].astype(f32)
        done = pl.ds(c * half, half)
        for k, (held, out) in enumerate(((moment_held, moment), (update_held, update))):
            copies.append(pltpu.make_async_copy(held.at[:, done], out.at[:, done], sems.at[c, k]))
            copies[-1].start()
    for copy in copies:
        copy.wait()


def spread(returned):
    heads, _, rows, columns = returned.shape
    moment = jax.ShapeDtypeStruct((rows, heads * columns), f32)
    update = jax.ShapeDtypeStruct((rows, heads * columns), bf16)
    hbm = pl.BlockSpec(memory_space=pl.ANY)
    return pl.pallas_call(
        spread_kernel,
        out_shape=(moment, update),
        in_specs=[pl.BlockSpec(memory_space=pltpu.VMEM)],
        out_specs=(hbm, hbm),
        scratch_shapes=[
            pltpu.VMEM(moment.shape, f32),
            pltpu.VMEM(update.shape, bf16),
            pltpu.SemaphoreType.DMA((NC, 2)),
        ],
        compiler_params=pltpu.CompilerParams(vmem_limit_bytes=VMEM),
    )(returned)


def body(latent, latent_grad, row_counts, momentum):
    features = latent.shape[1]
    order, rest = (2, 1, 3), (1, 2, 3)
    tie = lax.optimization_barrier

    early, late = (2,), (1, 3, 0)
    piece_early, piece_late, mine = column_pieces(latent_grad, (early, late))
    lat_own, mom_own, mom_other, unit, own_early = first(row_counts, latent, momentum, mine)
    piece_early, lat_other, mom_other = (
        swap_cores(piece_early), swap_cores(lat_own), swap_cores(mom_other)
    )
    piece_late, piece_early, lat_other, mom_other = tie((piece_late, piece_early, lat_other, mom_other))
    piece_late = swap_cores(piece_late)
    shared = (unit, lat_other, mom_own, mom_other)

    own = {2: own_early}
    (first_on,) = block(own, early, [(2, rest)], *shared, piece_early)
    lat_late, first_on = tie((lat_own, first_on))
    own[1], own[3], own[0] = own_products(lat_late, latent_grad, late)
    on = [first_on] + [block(own, late, [(k, rest)], *shared, piece_late)[0] for k in order[1:]]
    on = [exchange(value, 0, k) for value, k in zip(on, order)]
    (stay,) = block(own, early, [(2, (0,))], *shared, piece_early)
    *stays, kept_stay, kept_on = block(
        own, late, [(1, (0,)), (3, (0,)), (0, (0,)), (0, rest)], *shared, piece_late
    )
    stay = [exchange(value, 0, k) for value, k in zip([stay] + stays, order)]

    total = kept_on + sum(value.astype(f32) for value in on)
    got = [exchange(total[k - 1].astype(bf16), 1, k) for k in order]
    head = kept_stay[0] + sum(value[0].astype(f32) for value in stay)
    head = (head + sum(value.astype(f32) for value in got)).astype(bf16)

    pieces = lax.all_to_all(head.reshape(NZ, -1, HD), "z", 0, 0, tiled=True)
    piece = jnp.sum(pieces.astype(f32), axis=0).astype(bf16)
    moment = lax.all_to_all(jnp.broadcast_to(piece, (NZ,) + piece.shape), "z", 0, 0, tiled=True)
    moment = moment.reshape(features, HD)

    outgoing = newton_schulz(moment, NC * NY * NX)
    returned = lax.all_to_all(outgoing, PLANE, 0, 0, tiled=True)
    return tuple(spread(returned))


def solution(mesh):
    fine = Mesh(mesh.devices.reshape(NZ, NY, NX, NC), AXES)
    shard = ("y", "x", "c")
    in_specs = (P(AXES, None), P(AXES, None), P(AXES), P(shard, None))
    out_specs = (P(shard, None), P(shard, None))
    return jax.shard_map(body, mesh=fine, in_specs=in_specs, out_specs=out_specs, check_vma=False)
```

```python
import functools
import math

import jax
import jax.numpy as jnp
from jax import lax
from jax.experimental import pallas as pl
from jax.experimental.pallas import tpu as pltpu
from jax.sharding import Mesh
from jax.sharding import PartitionSpec as P

HD = 256
NS_STEPS = 5
NZ, NY, NX, NC = 8, 4, 4, 2
RING = 4
AXES = ("z", "y", "x", "c")
PLANE = ("c", "y", "x")
COEF_A, COEF_B, COEF_C = 3.4445, -4.775, 2.0315
DECAY = 0.95
VMEM = 16 * 1024 * 1024
MIDDLE = 5 * 10**9
LARGE = 48 * 1024 * 1024
bf16, f32 = jnp.bfloat16, jnp.float32


def device_at(z, y, x, c):
    return ((z * NY + y) * NX + x) * NC + c


def every_device():
    return [(z, y, x, c) for z in range(NZ) for y in range(NY) for x in range(NX) for c in range(NC)]


def exchange(value, axis, distance):
    pairs = []
    for z, y, x, c in every_device():
        if axis == c:
            to = (y, x ^ distance)
        else:
            to = (y ^ distance, x)
        pairs.append((device_at(z, y, x, c), device_at(z, *to, c)))
    return lax.ppermute(value, AXES, pairs)


def swap_cores(value):
    return lax.ppermute(
        value, AXES, [(device_at(z, y, x, c), device_at(z, y, x, 1 - c)) for z, y, x, c in every_device()]
    )


def places():
    core, y, x = lax.axis_index("c"), lax.axis_index("y"), lax.axis_index("x")
    return jnp.where(core == 0, x, y), jnp.where(core == 0, y, x)


def head_columns(near, far, other=False):
    first, second = places()
    if other:
        first, second = second, first
    head = (first ^ near) * RING + (second ^ far)
    return pl.multiple_of(head * HD, HD)


def gather(grad, held, sems, nears, other):
    core = lax.axis_index("c")
    base = (1 - core if other else core) * (grad.shape[1] // NC)
    copies = []
    for near in nears:
        for far in range(RING):
            k = len(copies)
            start = pl.multiple_of(base + head_columns(near, far, other), HD)
            copies.append(
                pltpu.make_async_copy(grad.at[:, pl.ds(start, HD)], held.at[k], sems.at[k])
            )
    return copies


def pieces_kernel(groups, grad, early, late, mine, held, sems_in, sems_out):
    lists = [(groups[0], True), (groups[1], True), (groups[0], False)]
    into, onto = [], []
    for (nears, other), out in zip(lists, (early, late, mine)):
        at = len(into)
        count = RING * len(nears)
        into += gather(grad, held.at[pl.ds(at, count)], sems_in.at[pl.ds(at, count)], nears, other)
        for k in range(count):
            onto.append(
                pltpu.make_async_copy(
                    held.at[at + k], out.at[:, k * HD : (k + 1) * HD], sems_out.at[at + k]
                )
            )
    for copy in into:
        copy.start()
    for k in range(len(into)):
        into[k].wait()
        onto[k].start()
    for copy in onto:
        copy.wait()


def column_pieces(grad, groups):
    slots = grad.shape[0]
    widths = [RING * len(nears) for nears in (groups[0], groups[1], groups[0])]
    hbm = pl.BlockSpec(memory_space=pl.ANY)
    return pl.pallas_call(
        functools.partial(pieces_kernel, groups),
        out_shape=[jax.ShapeDtypeStruct((slots, width * HD), bf16) for width in widths],
        in_specs=[hbm],
        out_specs=[hbm] * 3,
        scratch_shapes=[
            pltpu.VMEM((sum(widths), slots, HD), bf16),
            pltpu.SemaphoreType.DMA((sum(widths),)),
            pltpu.SemaphoreType.DMA((sum(widths),)),
        ],
        compiler_params=pltpu.CompilerParams(vmem_limit_bytes=LARGE),
    )(grad)


def first_kernel(counts, latent, momentum, mine, lat, mom_own, mom_other, unit, own):
    core = lax.axis_index("c")
    slots, features = latent.shape
    depth, half = momentum.shape[0], momentum.shape[1] // NC
    live = lax.broadcasted_iota(jnp.int32, (slots, features), 0) < counts[0]
    lat[...] = jnp.where(live, latent[...], jnp.zeros_like(latent)).T
    for out, which in ((mom_own, core), (mom_other, 1 - core)):
        value = (DECAY / NZ) * momentum[:, pl.ds(pl.multiple_of(which * half, half), half)]
        high = value.astype(bf16)
        out[:depth, :] = high
        out[depth:, :] = (value - high.astype(f32)).astype(bf16)
    here = lax.axis_index("y") * NX + lax.axis_index("x")
    row = lax.broadcasted_iota(jnp.int32, unit.shape, 0)
    at = lax.broadcasted_iota(jnp.int32, unit.shape, 1)
    core_of = jnp.where(at < 2 * depth, core, 1 - core)
    unit[...] = (row == (here * NC + core_of) * depth + at % depth).astype(f32).astype(bf16)
    for far in range(RING):
        columns = mine[:, far * HD : (far + 1) * HD]
        own[far] = jnp.dot(lat[...], columns, preferred_element_type=f32).astype(bf16)


def first(counts, latent, momentum, mine):
    slots, features = latent.shape
    depth, columns = momentum.shape
    vmem = pl.BlockSpec(memory_space=pltpu.VMEM)
    mom = jax.ShapeDtypeStruct((2 * depth, columns // NC), bf16)
    return pl.pallas_call(
        first_kernel,
        out_shape=[
            jax.ShapeDtypeStruct((features, slots), bf16),
            mom,
            mom,
            jax.ShapeDtypeStruct((features, 4 * depth), bf16),
            jax.ShapeDtypeStruct((RING, features, HD), bf16),
        ],
        in_specs=[pl.BlockSpec(memory_space=pltpu.SMEM), vmem, vmem, vmem],
        compiler_params=pltpu.CompilerParams(vmem_limit_bytes=VMEM),
    )(counts, latent, momentum, mine)


def own_kernel(nears, lat, grad, *refs):
    outs, (held, sems) = refs[: len(nears)], refs[len(nears) :]
    copies = gather(grad, held, sems, nears, False)
    for copy in copies:
        copy.start()
    for near in range(len(nears)):
        for far in range(RING):
            copies[near * RING + far].wait()
        for far in range(RING):
            value = jnp.dot(lat[...], held[near * RING + far], preferred_element_type=f32)
            outs[near][far] = value.astype(bf16)


def own_products(lat, grad, nears):
    features, tokens = lat.shape
    count = RING * len(nears)
    vmem = pl.BlockSpec(memory_space=pltpu.VMEM)
    return pl.pallas_call(
        functools.partial(own_kernel, nears),
        out_shape=[jax.ShapeDtypeStruct((RING, features, HD), bf16)] * len(nears),
        in_specs=[vmem, pl.BlockSpec(memory_space=pl.ANY)],
        out_specs=[vmem] * len(nears),
        scratch_shapes=[
            pltpu.VMEM((count, tokens, HD), bf16),
            pltpu.SemaphoreType.DMA((count,)),
        ],
        compiler_params=pltpu.CompilerParams(vmem_limit_bytes=LARGE),
        cost_estimate=pl.CostEstimate(
            flops=2 * count * features * HD * tokens,
            bytes_accessed=count * (tokens + features) * HD * 2,
            transcendentals=0,
        ),
    )(lat, grad)


def block_kernel(tiles, unit, lat, mom_own, mom_other, grad, *refs):
    count = 1 + max(t[0] for t in tiles)
    operands, outs = refs[:count], refs[count:]
    for (operand, at_piece, near, fars, row), out in zip(tiles, outs):
        rows = slice(row, row + out.shape[1])
        for place, far in enumerate(fars):
            at = pl.ds(head_columns(near, far), HD)
            in_piece = (at_piece * RING + far) * HD
            mom = jnp.concatenate([mom_own[:, at], mom_other[:, at]], axis=0)
            other = jnp.dot(
                lat[rows, :], grad[:, in_piece : in_piece + HD], preferred_element_type=f32
            )
            added = jnp.dot(unit[rows, :], mom, preferred_element_type=f32)
            total = operands[operand][far, rows].astype(f32) + other.astype(bf16).astype(f32) + added
            out[place] = total.astype(out.dtype)


def block(own, held, which, unit, lat, mom_own, mom_other, grad):
    tokens = lat.shape[1]
    nears = sorted({w[0] for w in which})
    tiles = [(nears.index(w[0]), held.index(w[0]), *w[:3]) for w in which]
    work = sum(len(w[1]) * w[3] for w in which)
    return pl.pallas_call(
        functools.partial(block_kernel, tiles),
        out_shape=[jax.ShapeDtypeStruct((len(w[1]), w[3], HD), w[4]) for w in which],
        compiler_params=pltpu.CompilerParams(vmem_limit_bytes=VMEM),
        cost_estimate=pl.CostEstimate(
            flops=2 * work * HD * (tokens + unit.shape[1]),
            bytes_accessed=work * HD * 4 + len(which) * RING * tokens * HD * 2,
            transcendentals=0,
        ),
    )(unit, lat, mom_own, mom_other, grad, *[own[near] for near in nears])


def middle_kernel(kept, upper, lower, one, three, two_a, two_b, kept_out, one_out, three_out):
    half = upper.shape[1]
    for k in range(kept.shape[0]):
        kept_out[k, :half] = kept[k, :half] + upper[k].astype(f32)
        kept_out[k, half:] = kept[k, half:] + lower[k].astype(f32)
    one_out[:half, :] = one[0, :half].astype(bf16)
    one_out[half:, :] = (one[0, half:] + two_b[0].astype(f32)).astype(bf16)
    three_out[:half, :] = (three[0, :half] + two_a[0].astype(f32)).astype(bf16)
    three_out[half:, :] = three[0, half:].astype(bf16)


def middle(kept, *parts):
    stay = jax.ShapeDtypeStruct(kept.shape[1:], bf16)
    return pl.pallas_call(
        middle_kernel,
        out_shape=[jax.ShapeDtypeStruct(kept.shape, f32), stay, stay],
        compiler_params=pltpu.CompilerParams(vmem_limit_bytes=VMEM),
        cost_estimate=pl.CostEstimate(flops=MIDDLE, bytes_accessed=0, transcendentals=0),
    )(kept, *parts)


def stay_kernel(kept, one, three, out):
    out[...] = kept[0] + one[...].astype(f32) + three[...].astype(f32)


def stay_sum(kept, one, three):
    return pl.pallas_call(
        stay_kernel,
        out_shape=jax.ShapeDtypeStruct(kept.shape[1:], f32),
        compiler_params=pltpu.CompilerParams(vmem_limit_bytes=VMEM),
        cost_estimate=pl.CostEstimate(flops=MIDDLE, bytes_accessed=0, transcendentals=0),
    )(kept, one, three)


def add_kernel(kept, upper, lower, *outs):
    half = upper.shape[1]
    for k, out in enumerate(outs):
        out[:half, :] = (kept[k, :half] + upper[k].astype(f32)).astype(out.dtype)
        out[half:, :] = (kept[k, half:] + lower[k].astype(f32)).astype(out.dtype)


def add_up(kept, *parts):
    heads, rows, columns = kept.shape
    return pl.pallas_call(
        add_kernel,
        out_shape=[jax.ShapeDtypeStruct((rows, columns), bf16)] * heads,
        compiler_params=pltpu.CompilerParams(vmem_limit_bytes=VMEM),
    )(kept, *parts)


def split(value):
    high = value.astype(bf16)
    return high, (value - high.astype(f32)).astype(bf16)


def product(a, b, dims):
    (left,), (right,) = dims
    return lax.dot_general(
        jnp.concatenate([a[0], a[0], a[1]], axis=left),
        jnp.concatenate([b[0], b[1], b[0]], axis=right),
        (dims, ((), ())),
        preferred_element_type=f32,
    )


def newton_schulz_kernel(moment_ref, out_ref):
    moment = moment_ref[...]
    rows, columns = moment.shape
    scale = 0.2 * math.sqrt(max(rows, columns))
    wide = moment.T
    gram = lax.dot_general(wide, wide, (((1,), (1,)), ((), ())), preferred_element_type=f32)
    wide = wide.astype(f32)
    inverse = 1.0 / (jnp.sqrt(jnp.sum(wide * wide)) + 1e-7)
    gram = (gram * inverse) * inverse
    x = wide * inverse
    for step in range(NS_STEPS):
        pair = split(x)
        if step > 0:
            gram = product(pair, pair, ((1,), (1,)))
        gram_pair = split(gram)
        poly = COEF_B * gram + COEF_C * product(gram_pair, gram_pair, ((1,), (0,)))
        x = COEF_A * x + product(split(poly), pair, ((1,), (0,)))
    update = (scale * x).T.astype(bf16)
    owners = out_ref.shape[0]
    depth = rows // owners
    for c in range(NC):
        for chip in range(owners // NC):
            at = slice((chip * NC + c) * depth, (chip * NC + c + 1) * depth)
            out_ref[c * (owners // NC) + chip, 0] = update[at, :]
            out_ref[c * (owners // NC) + chip, 1] = moment[at, :]


def newton_schulz(moment, owners):
    rows, columns = moment.shape
    return pl.pallas_call(
        newton_schulz_kernel,
        out_shape=jax.ShapeDtypeStruct((owners, 2, rows // owners, columns), bf16),
        compiler_params=pltpu.CompilerParams(vmem_limit_bytes=VMEM),
    )(moment)


def spread_kernel(returned, moment, update, moment_held, update_held, sems):
    half = moment_held.shape[1] // NC
    copies = []
    for c in range(NC):
        for y in range(NY):
            for x in range(NX):
                source = (c * NY + y) * NX + x
                head = c * NY * NX + (RING * x + y if c == 0 else RING * y + x)
                at = slice(head * HD, (head + 1) * HD)
                update_held[:, at] = returned[source, 0]
                moment_held[:, at] = returned[source, 1].astype(f32)
        done = pl.ds(c * half, half)
        for k, (held, out) in enumerate(((moment_held, moment), (update_held, update))):
            copies.append(pltpu.make_async_copy(held.at[:, done], out.at[:, done], sems.at[c, k]))
            copies[-1].start()
    for copy in copies:
        copy.wait()


def spread(returned):
    heads, _, rows, columns = returned.shape
    moment = jax.ShapeDtypeStruct((rows, heads * columns), f32)
    update = jax.ShapeDtypeStruct((rows, heads * columns), bf16)
    hbm = pl.BlockSpec(memory_space=pl.ANY)
    return pl.pallas_call(
        spread_kernel,
        out_shape=(moment, update),
        in_specs=[pl.BlockSpec(memory_space=pltpu.VMEM)],
        out_specs=(hbm, hbm),
        scratch_shapes=[
            pltpu.VMEM(moment.shape, f32),
            pltpu.VMEM(update.shape, bf16),
            pltpu.SemaphoreType.DMA((NC, 2)),
        ],
        compiler_params=pltpu.CompilerParams(vmem_limit_bytes=VMEM),
    )(returned)


def body(latent, latent_grad, row_counts, momentum):
    features = latent.shape[1]
    order = (2, 1, 3)
    tie = lax.optimization_barrier

    early, late = (2,), (1, 3, 0)
    piece_early, piece_late, mine = column_pieces(latent_grad, (early, late))
    lat_own, mom_own, mom_other, unit, own_early = first(row_counts, latent, momentum, mine)
    piece_early, lat_other, mom_other = (
        swap_cores(piece_early), swap_cores(lat_own), swap_cores(mom_other)
    )
    piece_late, piece_early, lat_other, mom_other = tie((piece_late, piece_early, lat_other, mom_other))
    piece_late = swap_cores(piece_late)
    shared = (unit, lat_other, mom_own, mom_other)

    half = features // 2
    upper, lower, whole = (0, half), (half, half), (0, features)
    every, rest, stay = (0, 1, 2, 3), (1, 2, 3), (0,)
    own = {2: own_early}
    two_a, two_b = block(
        own, early, [(2, every, *upper, bf16), (2, every, *lower, bf16)], *shared, piece_early
    )
    lat_late, two_a, two_b = tie((lat_own, two_a, two_b))
    own[1], own[3], own[0] = own_products(lat_late, latent_grad, late)
    (one_a,) = block(own, late, [(1, rest, *upper, bf16)], *shared, piece_late)
    (three_b,) = block(own, late, [(3, rest, *lower, bf16)], *shared, piece_late)
    own[0], one_a, three_b = tie((own[0], one_a, three_b))
    one_b, three_a, one_stay, three_stay, kept_on, kept_stay = block(
        own,
        late,
        [
            (1, rest, *lower, f32),
            (3, rest, *upper, f32),
            (1, stay, *whole, f32),
            (3, stay, *whole, f32),
            (0, rest, *whole, f32),
            (0, stay, *whole, f32),
        ],
        *shared,
        piece_late,
    )
    two_a, two_b = exchange(two_a, 0, 1), exchange(two_b, 0, 3)
    one_a, three_b = exchange(one_a, 0, 1), exchange(three_b, 0, 3)
    three_a = exchange((three_a + two_a[1:].astype(f32)).astype(bf16), 0, 3)
    one_b = exchange((one_b + two_b[1:].astype(f32)).astype(bf16), 0, 1)
    kept_on, one_stay, three_stay = middle(
        kept_on, one_a, three_b, one_stay, three_stay, two_a, two_b
    )
    one_stay, three_stay = exchange(one_stay, 0, 1), exchange(three_stay, 0, 3)

    sums = add_up(kept_on, three_a, one_b)
    got = [exchange(sums[k - 1], 1, k) for k in order]
    head = stay_sum(kept_stay, one_stay, three_stay)
    head = (head + sum(value.astype(f32) for value in got)).astype(bf16)

    pieces = lax.all_to_all(head.reshape(NZ, -1, HD), "z", 0, 0, tiled=True)
    piece = jnp.sum(pieces.astype(f32), axis=0).astype(bf16)
    moment = lax.all_to_all(jnp.broadcast_to(piece, (NZ,) + piece.shape), "z", 0, 0, tiled=True)
    moment = moment.reshape(features, HD)

    outgoing = newton_schulz(moment, NC * NY * NX)
    returned = lax.all_to_all(outgoing, PLANE, 0, 0, tiled=True)
    return tuple(spread(returned))


def solution(mesh):
    fine = Mesh(mesh.devices.reshape(NZ, NY, NX, NC), AXES)
    shard = ("y", "x", "c")
    in_specs = (P(AXES, None), P(AXES, None), P(AXES), P(shard, None))
    out_specs = (P(shard, None), P(shard, None))
    return jax.shard_map(body, mesh=fine, in_specs=in_specs, out_specs=out_specs, check_vma=False)
```

```python
import functools
import math

import jax
import jax.numpy as jnp
from jax import lax
from jax.experimental import pallas as pl
from jax.experimental.pallas import tpu as pltpu
from jax.sharding import Mesh
from jax.sharding import PartitionSpec as P

HD = 256
NS_STEPS = 5
NZ, NY, NX, NC = 8, 4, 4, 2
RING = 4
AXES = ("z", "y", "x", "c")
PLANE = ("c", "y", "x")
COEF_A, COEF_B, COEF_C = 3.4445, -4.775, 2.0315
DECAY = 0.95
VMEM = 16 * 1024 * 1024
MIDDLE = 5 * 10**9
LARGE = 48 * 1024 * 1024
LARGER = 52 * 1024 * 1024
bf16, f32 = jnp.bfloat16, jnp.float32


def device_at(z, y, x, c):
    return ((z * NY + y) * NX + x) * NC + c


def every_device():
    return [(z, y, x, c) for z in range(NZ) for y in range(NY) for x in range(NX) for c in range(NC)]


def exchange(value, axis, distance):
    pairs = []
    for z, y, x, c in every_device():
        if axis == c:
            to = (y, x ^ distance)
        else:
            to = (y ^ distance, x)
        pairs.append((device_at(z, y, x, c), device_at(z, *to, c)))
    return lax.ppermute(value, AXES, pairs)


def swap_cores(value):
    return lax.ppermute(
        value, AXES, [(device_at(z, y, x, c), device_at(z, y, x, 1 - c)) for z, y, x, c in every_device()]
    )


def places():
    core, y, x = lax.axis_index("c"), lax.axis_index("y"), lax.axis_index("x")
    return jnp.where(core == 0, x, y), jnp.where(core == 0, y, x)


def head_columns(near, far, other=False):
    first, second = places()
    if other:
        first, second = second, first
    head = (first ^ near) * RING + (second ^ far)
    return pl.multiple_of(head * HD, HD)


def gather(grad, held, sems, nears, other):
    core = lax.axis_index("c")
    base = (1 - core if other else core) * (grad.shape[1] // NC)
    copies = []
    for near in nears:
        for far in range(RING):
            k = len(copies)
            start = pl.multiple_of(base + head_columns(near, far, other), HD)
            copies.append(
                pltpu.make_async_copy(grad.at[:, pl.ds(start, HD)], held.at[k], sems.at[k])
            )
    return copies


def pieces_kernel(lists, grad, *refs):
    outs, (held, sems_in, sems_out) = refs[: len(lists)], refs[len(lists) :]
    into, onto = [], []
    for (nears, other), out in zip(lists, outs):
        at = len(into)
        count = RING * len(nears)
        into += gather(grad, held.at[pl.ds(at, count)], sems_in.at[pl.ds(at, count)], nears, other)
        for k in range(count):
            onto.append(
                pltpu.make_async_copy(
                    held.at[at + k], out.at[:, k * HD : (k + 1) * HD], sems_out.at[at + k]
                )
            )
    for copy in into:
        copy.start()
    for k in range(len(into)):
        into[k].wait()
        onto[k].start()
    for copy in onto:
        copy.wait()


def column_pieces(grad, lists):
    slots = grad.shape[0]
    widths = [RING * len(nears) for nears, _ in lists]
    hbm = pl.BlockSpec(memory_space=pl.ANY)
    return pl.pallas_call(
        functools.partial(pieces_kernel, lists),
        out_shape=[jax.ShapeDtypeStruct((slots, width * HD), bf16) for width in widths],
        in_specs=[hbm],
        out_specs=[hbm] * len(lists),
        scratch_shapes=[
            pltpu.VMEM((sum(widths), slots, HD), bf16),
            pltpu.SemaphoreType.DMA((sum(widths),)),
            pltpu.SemaphoreType.DMA((sum(widths),)),
        ],
        compiler_params=pltpu.CompilerParams(vmem_limit_bytes=LARGER),
    )(grad)


def first_kernel(counts, latent, momentum, mine, lat, mom_own, mom_other, unit, own):
    core = lax.axis_index("c")
    slots, features = latent.shape
    depth, half = momentum.shape[0], momentum.shape[1] // NC
    live = lax.broadcasted_iota(jnp.int32, (slots, features), 0) < counts[0]
    lat[...] = jnp.where(live, latent[...], jnp.zeros_like(latent)).T
    for out, which in ((mom_own, core), (mom_other, 1 - core)):
        value = (DECAY / NZ) * momentum[:, pl.ds(pl.multiple_of(which * half, half), half)]
        high = value.astype(bf16)
        out[:depth, :] = high
        out[depth:, :] = (value - high.astype(f32)).astype(bf16)
    here = lax.axis_index("y") * NX + lax.axis_index("x")
    row = lax.broadcasted_iota(jnp.int32, unit.shape, 0)
    at = lax.broadcasted_iota(jnp.int32, unit.shape, 1)
    core_of = jnp.where(at < 2 * depth, core, 1 - core)
    unit[...] = (row == (here * NC + core_of) * depth + at % depth).astype(f32).astype(bf16)
    for far in range(RING):
        columns = mine[:, far * HD : (far + 1) * HD]
        own[far] = jnp.dot(lat[...], columns, preferred_element_type=f32).astype(bf16)


def first(counts, latent, momentum, mine):
    slots, features = latent.shape
    depth, columns = momentum.shape
    vmem = pl.BlockSpec(memory_space=pltpu.VMEM)
    mom = jax.ShapeDtypeStruct((2 * depth, columns // NC), bf16)
    return pl.pallas_call(
        first_kernel,
        out_shape=[
            jax.ShapeDtypeStruct((features, slots), bf16),
            mom,
            mom,
            jax.ShapeDtypeStruct((features, 4 * depth), bf16),
            jax.ShapeDtypeStruct((RING, features, HD), bf16),
        ],
        in_specs=[pl.BlockSpec(memory_space=pltpu.SMEM), vmem, vmem, vmem],
        compiler_params=pltpu.CompilerParams(vmem_limit_bytes=VMEM),
    )(counts, latent, momentum, mine)


def own_kernel(nears, lat, grad, *refs):
    outs, (held, sems) = refs[: len(nears)], refs[len(nears) :]
    copies = gather(grad, held, sems, nears, False)
    for copy in copies:
        copy.start()
    for near in range(len(nears)):
        for far in range(RING):
            copies[near * RING + far].wait()
        for far in range(RING):
            value = jnp.dot(lat[...], held[near * RING + far], preferred_element_type=f32)
            outs[near][far] = value.astype(bf16)


def own_products(lat, grad, nears):
    features, tokens = lat.shape
    count = RING * len(nears)
    vmem = pl.BlockSpec(memory_space=pltpu.VMEM)
    return pl.pallas_call(
        functools.partial(own_kernel, nears),
        out_shape=[jax.ShapeDtypeStruct((RING, features, HD), bf16)] * len(nears),
        in_specs=[vmem, pl.BlockSpec(memory_space=pl.ANY)],
        out_specs=[vmem] * len(nears),
        scratch_shapes=[
            pltpu.VMEM((count, tokens, HD), bf16),
            pltpu.SemaphoreType.DMA((count,)),
        ],
        compiler_params=pltpu.CompilerParams(vmem_limit_bytes=LARGE),
        cost_estimate=pl.CostEstimate(
            flops=2 * count * features * HD * tokens,
            bytes_accessed=count * (tokens + features) * HD * 2,
            transcendentals=0,
        ),
    )(lat, grad)


def block_kernel(tiles, unit, lat, mom_own, mom_other, grad, *refs):
    count = 1 + max(t[0] for t in tiles)
    operands, outs = refs[:count], refs[count:]
    for (operand, at_piece, near, fars, row), out in zip(tiles, outs):
        rows = slice(row, row + out.shape[1])
        for place, far in enumerate(fars):
            at = pl.ds(head_columns(near, far), HD)
            in_piece = (at_piece * RING + far) * HD
            mom = jnp.concatenate([mom_own[:, at], mom_other[:, at]], axis=0)
            other = jnp.dot(
                lat[rows, :], grad[:, in_piece : in_piece + HD], preferred_element_type=f32
            )
            added = jnp.dot(unit[rows, :], mom, preferred_element_type=f32)
            total = operands[operand][far, rows].astype(f32) + other.astype(bf16).astype(f32) + added
            out[place] = total.astype(out.dtype)


def block(own, held, which, unit, lat, mom_own, mom_other, grad):
    tokens = lat.shape[1]
    nears = sorted({w[0] for w in which})
    tiles = [(nears.index(w[0]), held.index(w[0]), *w[:3]) for w in which]
    work = sum(len(w[1]) * w[3] for w in which)
    return pl.pallas_call(
        functools.partial(block_kernel, tiles),
        out_shape=[jax.ShapeDtypeStruct((len(w[1]), w[3], HD), w[4]) for w in which],
        compiler_params=pltpu.CompilerParams(vmem_limit_bytes=VMEM),
        cost_estimate=pl.CostEstimate(
            flops=2 * work * HD * (tokens + unit.shape[1]),
            bytes_accessed=work * HD * 4 + len(which) * RING * tokens * HD * 2,
            transcendentals=0,
        ),
    )(unit, lat, mom_own, mom_other, grad, *[own[near] for near in nears])


def middle_kernel(kept, upper, lower, one, three, two_a, two_b, kept_out, one_out, three_out):
    half = upper.shape[1]
    for k in range(kept.shape[0]):
        kept_out[k, :half] = kept[k, :half] + upper[k].astype(f32)
        kept_out[k, half:] = kept[k, half:] + lower[k].astype(f32)
    one_out[:half, :] = one[0, :half].astype(bf16)
    one_out[half:, :] = (one[0, half:] + two_b[0].astype(f32)).astype(bf16)
    three_out[:half, :] = (three[0, :half] + two_a[0].astype(f32)).astype(bf16)
    three_out[half:, :] = three[0, half:].astype(bf16)


def middle(kept, *parts):
    stay = jax.ShapeDtypeStruct(kept.shape[1:], bf16)
    return pl.pallas_call(
        middle_kernel,
        out_shape=[jax.ShapeDtypeStruct(kept.shape, f32), stay, stay],
        compiler_params=pltpu.CompilerParams(vmem_limit_bytes=VMEM),
        cost_estimate=pl.CostEstimate(flops=MIDDLE, bytes_accessed=0, transcendentals=0),
    )(kept, *parts)


def stay_kernel(kept, one, three, out):
    out[...] = kept[0] + one[...].astype(f32) + three[...].astype(f32)


def stay_sum(kept, one, three):
    return pl.pallas_call(
        stay_kernel,
        out_shape=jax.ShapeDtypeStruct(kept.shape[1:], f32),
        compiler_params=pltpu.CompilerParams(vmem_limit_bytes=VMEM),
        cost_estimate=pl.CostEstimate(flops=MIDDLE, bytes_accessed=0, transcendentals=0),
    )(kept, one, three)


def add_kernel(kept, upper, lower, *outs):
    half = upper.shape[1]
    for k, out in enumerate(outs):
        out[:half, :] = (kept[k, :half] + upper[k].astype(f32)).astype(out.dtype)
        out[half:, :] = (kept[k, half:] + lower[k].astype(f32)).astype(out.dtype)


def add_up(kept, *parts):
    heads, rows, columns = kept.shape
    return pl.pallas_call(
        add_kernel,
        out_shape=[jax.ShapeDtypeStruct((rows, columns), bf16)] * heads,
        compiler_params=pltpu.CompilerParams(vmem_limit_bytes=VMEM),
    )(kept, *parts)


def split(value):
    high = value.astype(bf16)
    return high, (value - high.astype(f32)).astype(bf16)


def product(a, b, dims):
    (left,), (right,) = dims
    return lax.dot_general(
        jnp.concatenate([a[0], a[0], a[1]], axis=left),
        jnp.concatenate([b[0], b[1], b[0]], axis=right),
        (dims, ((), ())),
        preferred_element_type=f32,
    )


def newton_schulz_kernel(moment_ref, out_ref):
    moment = moment_ref[...]
    rows, columns = moment.shape
    scale = 0.2 * math.sqrt(max(rows, columns))
    wide = moment.T
    gram = lax.dot_general(wide, wide, (((1,), (1,)), ((), ())), preferred_element_type=f32)
    wide = wide.astype(f32)
    inverse = 1.0 / (jnp.sqrt(jnp.sum(wide * wide)) + 1e-7)
    gram = (gram * inverse) * inverse
    x = wide * inverse
    for step in range(NS_STEPS):
        pair = split(x)
        if step > 0:
            gram = product(pair, pair, ((1,), (1,)))
        gram_pair = split(gram)
        poly = COEF_B * gram + COEF_C * product(gram_pair, gram_pair, ((1,), (0,)))
        x = COEF_A * x + product(split(poly), pair, ((1,), (0,)))
    update = (scale * x).T.astype(bf16)
    owners = out_ref.shape[0]
    depth = rows // owners
    for c in range(NC):
        for chip in range(owners // NC):
            at = slice((chip * NC + c) * depth, (chip * NC + c + 1) * depth)
            out_ref[c * (owners // NC) + chip, 0] = update[at, :]
            out_ref[c * (owners // NC) + chip, 1] = moment[at, :]


def newton_schulz(moment, owners):
    rows, columns = moment.shape
    return pl.pallas_call(
        newton_schulz_kernel,
        out_shape=jax.ShapeDtypeStruct((owners, 2, rows // owners, columns), bf16),
        compiler_params=pltpu.CompilerParams(vmem_limit_bytes=VMEM),
    )(moment)


def spread_kernel(returned, moment, update, moment_held, update_held, sems):
    half = moment_held.shape[1] // NC
    copies = []
    for c in range(NC):
        for y in range(NY):
            for x in range(NX):
                source = (c * NY + y) * NX + x
                head = c * NY * NX + (RING * x + y if c == 0 else RING * y + x)
                at = slice(head * HD, (head + 1) * HD)
                update_held[:, at] = returned[source, 0]
                moment_held[:, at] = returned[source, 1].astype(f32)
        done = pl.ds(c * half, half)
        for k, (held, out) in enumerate(((moment_held, moment), (update_held, update))):
            copies.append(pltpu.make_async_copy(held.at[:, done], out.at[:, done], sems.at[c, k]))
            copies[-1].start()
    for copy in copies:
        copy.wait()


def spread(returned):
    heads, _, rows, columns = returned.shape
    moment = jax.ShapeDtypeStruct((rows, heads * columns), f32)
    update = jax.ShapeDtypeStruct((rows, heads * columns), bf16)
    hbm = pl.BlockSpec(memory_space=pl.ANY)
    return pl.pallas_call(
        spread_kernel,
        out_shape=(moment, update),
        in_specs=[pl.BlockSpec(memory_space=pltpu.VMEM)],
        out_specs=(hbm, hbm),
        scratch_shapes=[
            pltpu.VMEM(moment.shape, f32),
            pltpu.VMEM(update.shape, bf16),
            pltpu.SemaphoreType.DMA((NC, 2)),
        ],
        compiler_params=pltpu.CompilerParams(vmem_limit_bytes=VMEM),
    )(returned)


def body(latent, latent_grad, row_counts, momentum):
    features = latent.shape[1]
    order = (2, 1, 3)
    tie = lax.optimization_barrier

    early, late = (2,), (1, 3, 0)
    piece_early, mine = column_pieces(latent_grad, [(early, True), (early, False)])
    lat_own, mom_own, mom_other, unit, own_early = first(row_counts, latent, momentum, mine)
    grad_late, own_early = tie((latent_grad, own_early))
    (piece_late,) = column_pieces(grad_late, [(late, True)])
    piece_early, lat_other, mom_other = (
        swap_cores(piece_early), swap_cores(lat_own), swap_cores(mom_other)
    )
    piece_late, piece_early, lat_other, mom_other = tie((piece_late, piece_early, lat_other, mom_other))
    piece_late = swap_cores(piece_late)
    shared = (unit, lat_other, mom_own, mom_other)

    half = features // 2
    upper, lower, whole = (0, half), (half, half), (0, features)
    every, rest, stay = (0, 1, 2, 3), (1, 2, 3), (0,)
    own = {2: own_early}
    two_a, two_b = block(
        own, early, [(2, every, *upper, bf16), (2, every, *lower, bf16)], *shared, piece_early
    )
    lat_late, two_a, two_b = tie((lat_own, two_a, two_b))
    own[1], own[3], own[0] = own_products(lat_late, latent_grad, late)
    (one_a,) = block(own, late, [(1, rest, *upper, bf16)], *shared, piece_late)
    (three_b,) = block(own, late, [(3, rest, *lower, bf16)], *shared, piece_late)
    own[0], one_a, three_b = tie((own[0], one_a, three_b))
    one_b, three_a, one_stay, three_stay, kept_on, kept_stay = block(
        own,
        late,
        [
            (1, rest, *lower, f32),
            (3, rest, *upper, f32),
            (1, stay, *whole, f32),
            (3, stay, *whole, f32),
            (0, rest, *whole, f32),
            (0, stay, *whole, f32),
        ],
        *shared,
        piece_late,
    )
    two_a, two_b = exchange(two_a, 0, 1), exchange(two_b, 0, 3)
    one_a, three_b = exchange(one_a, 0, 1), exchange(three_b, 0, 3)
    three_a = exchange((three_a + two_a[1:].astype(f32)).astype(bf16), 0, 3)
    one_b = exchange((one_b + two_b[1:].astype(f32)).astype(bf16), 0, 1)
    kept_on, one_stay, three_stay = middle(
        kept_on, one_a, three_b, one_stay, three_stay, two_a, two_b
    )
    one_stay, three_stay = exchange(one_stay, 0, 1), exchange(three_stay, 0, 3)

    sums = add_up(kept_on, three_a, one_b)
    got = [exchange(sums[k - 1], 1, k) for k in order]
    head = stay_sum(kept_stay, one_stay, three_stay)
    head = (head + sum(value.astype(f32) for value in got)).astype(bf16)

    pieces = lax.all_to_all(head.reshape(NZ, -1, HD), "z", 0, 0, tiled=True)
    piece = jnp.sum(pieces.astype(f32), axis=0).astype(bf16)
    moment = lax.all_to_all(jnp.broadcast_to(piece, (NZ,) + piece.shape), "z", 0, 0, tiled=True)
    moment = moment.reshape(features, HD)

    outgoing = newton_schulz(moment, NC * NY * NX)
    returned = lax.all_to_all(outgoing, PLANE, 0, 0, tiled=True)
    return tuple(spread(returned))


def solution(mesh):
    fine = Mesh(mesh.devices.reshape(NZ, NY, NX, NC), AXES)
    shard = ("y", "x", "c")
    in_specs = (P(AXES, None), P(AXES, None), P(AXES), P(shard, None))
    out_specs = (P(shard, None), P(shard, None))
    return jax.shard_map(body, mesh=fine, in_specs=in_specs, out_specs=out_specs, check_vma=False)
```

```python
import functools
import math

import jax
import jax.numpy as jnp
from jax import lax
from jax.experimental import pallas as pl
from jax.experimental.pallas import tpu as pltpu
from jax.sharding import Mesh
from jax.sharding import PartitionSpec as P

HD = 256
NS_STEPS = 5
NZ, NY, NX, NC = 8, 4, 4, 2
RING = 4
AXES = ("z", "y", "x", "c")
PLANE = ("c", "y", "x")
COEF_A, COEF_B, COEF_C = 3.4445, -4.775, 2.0315
DECAY = 0.95
VMEM = 16 * 1024 * 1024
MIDDLE = 5 * 10**9
LARGE = 48 * 1024 * 1024
LARGER = 52 * 1024 * 1024
bf16, f32 = jnp.bfloat16, jnp.float32


def device_at(z, y, x, c):
    return ((z * NY + y) * NX + x) * NC + c


def every_device():
    return [(z, y, x, c) for z in range(NZ) for y in range(NY) for x in range(NX) for c in range(NC)]


def exchange(value, axis, distance):
    pairs = []
    for z, y, x, c in every_device():
        if axis == c:
            to = (y, x ^ distance)
        else:
            to = (y ^ distance, x)
        pairs.append((device_at(z, y, x, c), device_at(z, *to, c)))
    return lax.ppermute(value, AXES, pairs)


def swap_cores(value):
    return lax.ppermute(
        value, AXES, [(device_at(z, y, x, c), device_at(z, y, x, 1 - c)) for z, y, x, c in every_device()]
    )


def places():
    core, y, x = lax.axis_index("c"), lax.axis_index("y"), lax.axis_index("x")
    return jnp.where(core == 0, x, y), jnp.where(core == 0, y, x)


def head_columns(near, far, other=False):
    first, second = places()
    if other:
        first, second = second, first
    head = (first ^ near) * RING + (second ^ far)
    return pl.multiple_of(head * HD, HD)


def gather(grad, held, sems, nears, other):
    core = lax.axis_index("c")
    base = (1 - core if other else core) * (grad.shape[1] // NC)
    copies = []
    for near in nears:
        for far in range(RING):
            k = len(copies)
            start = pl.multiple_of(base + head_columns(near, far, other), HD)
            copies.append(
                pltpu.make_async_copy(grad.at[:, pl.ds(start, HD)], held.at[k], sems.at[k])
            )
    return copies


def pieces_kernel(lists, grad, *refs):
    outs, (held, sems_in, sems_out) = refs[: len(lists)], refs[len(lists) :]
    into, onto = [], []
    for (nears, other), out in zip(lists, outs):
        at = len(into)
        count = RING * len(nears)
        into += gather(grad, held.at[pl.ds(at, count)], sems_in.at[pl.ds(at, count)], nears, other)
        for k in range(count):
            onto.append(
                pltpu.make_async_copy(
                    held.at[at + k], out.at[:, k * HD : (k + 1) * HD], sems_out.at[at + k]
                )
            )
    for copy in into:
        copy.start()
    for k in range(len(into)):
        into[k].wait()
        onto[k].start()
    for copy in onto:
        copy.wait()


def column_pieces(grad, lists):
    slots = grad.shape[0]
    widths = [RING * len(nears) for nears, _ in lists]
    hbm = pl.BlockSpec(memory_space=pl.ANY)
    return pl.pallas_call(
        functools.partial(pieces_kernel, lists),
        out_shape=[jax.ShapeDtypeStruct((slots, width * HD), bf16) for width in widths],
        in_specs=[hbm],
        out_specs=[hbm] * len(lists),
        scratch_shapes=[
            pltpu.VMEM((sum(widths), slots, HD), bf16),
            pltpu.SemaphoreType.DMA((sum(widths),)),
            pltpu.SemaphoreType.DMA((sum(widths),)),
        ],
        compiler_params=pltpu.CompilerParams(vmem_limit_bytes=LARGER),
    )(grad)


def first_kernel(counts, latent, momentum, mine, lat, mom_own, mom_other, unit, own):
    core = lax.axis_index("c")
    slots, features = latent.shape
    depth, half = momentum.shape[0], momentum.shape[1] // NC
    live = lax.broadcasted_iota(jnp.int32, (slots, features), 0) < counts[0]
    lat[...] = jnp.where(live, latent[...], jnp.zeros_like(latent)).T
    for out, which in ((mom_own, core), (mom_other, 1 - core)):
        value = (DECAY / NZ) * momentum[:, pl.ds(pl.multiple_of(which * half, half), half)]
        high = value.astype(bf16)
        out[:depth, :] = high
        out[depth:, :] = (value - high.astype(f32)).astype(bf16)
    here = lax.axis_index("y") * NX + lax.axis_index("x")
    row = lax.broadcasted_iota(jnp.int32, unit.shape, 0)
    at = lax.broadcasted_iota(jnp.int32, unit.shape, 1)
    core_of = jnp.where(at < 2 * depth, core, 1 - core)
    unit[...] = (row == (here * NC + core_of) * depth + at % depth).astype(f32).astype(bf16)
    for far in range(RING):
        columns = mine[:, far * HD : (far + 1) * HD]
        own[far] = jnp.dot(lat[...], columns, preferred_element_type=f32).astype(bf16)


def first(counts, latent, momentum, mine):
    slots, features = latent.shape
    depth, columns = momentum.shape
    vmem = pl.BlockSpec(memory_space=pltpu.VMEM)
    mom = jax.ShapeDtypeStruct((2 * depth, columns // NC), bf16)
    return pl.pallas_call(
        first_kernel,
        out_shape=[
            jax.ShapeDtypeStruct((features, slots), bf16),
            mom,
            mom,
            jax.ShapeDtypeStruct((features, 4 * depth), bf16),
            jax.ShapeDtypeStruct((RING, features, HD), bf16),
        ],
        in_specs=[pl.BlockSpec(memory_space=pltpu.SMEM), vmem, vmem, vmem],
        compiler_params=pltpu.CompilerParams(vmem_limit_bytes=VMEM),
    )(counts, latent, momentum, mine)


def own_kernel(nears, lat, grad, *refs):
    outs, (held, sems) = refs[: len(nears)], refs[len(nears) :]
    copies = gather(grad, held, sems, nears, False)
    for copy in copies:
        copy.start()
    for near in range(len(nears)):
        for far in range(RING):
            copies[near * RING + far].wait()
        for far in range(RING):
            value = jnp.dot(lat[...], held[near * RING + far], preferred_element_type=f32)
            outs[near][far] = value.astype(bf16)


def own_products(lat, grad, nears):
    features, tokens = lat.shape
    count = RING * len(nears)
    vmem = pl.BlockSpec(memory_space=pltpu.VMEM)
    return pl.pallas_call(
        functools.partial(own_kernel, nears),
        out_shape=[jax.ShapeDtypeStruct((RING, features, HD), bf16)] * len(nears),
        in_specs=[vmem, pl.BlockSpec(memory_space=pl.ANY)],
        out_specs=[vmem] * len(nears),
        scratch_shapes=[
            pltpu.VMEM((count, tokens, HD), bf16),
            pltpu.SemaphoreType.DMA((count,)),
        ],
        compiler_params=pltpu.CompilerParams(vmem_limit_bytes=LARGE),
        cost_estimate=pl.CostEstimate(
            flops=2 * count * features * HD * tokens,
            bytes_accessed=count * (tokens + features) * HD * 2,
            transcendentals=0,
        ),
    )(lat, grad)


def block_kernel(tiles, unit, lat, mom_own, mom_other, grad, *refs):
    count = 1 + max(t[0] for t in tiles)
    operands, outs = refs[:count], refs[count:]
    for (operand, at_piece, near, fars, row), out in zip(tiles, outs):
        rows = slice(row, row + out.shape[1])
        for place, far in enumerate(fars):
            at = pl.ds(head_columns(near, far), HD)
            in_piece = (at_piece * RING + far) * HD
            mom = jnp.concatenate([mom_own[:, at], mom_other[:, at]], axis=0)
            other = jnp.dot(
                lat[rows, :], grad[:, in_piece : in_piece + HD], preferred_element_type=f32
            )
            added = jnp.dot(unit[rows, :], mom, preferred_element_type=f32)
            total = operands[operand][far, rows].astype(f32) + other.astype(bf16).astype(f32) + added
            out[place] = total.astype(out.dtype)


def block(own, held, which, unit, lat, mom_own, mom_other, grad):
    tokens = lat.shape[1]
    nears = sorted({w[0] for w in which})
    tiles = [(nears.index(w[0]), held.index(w[0]), *w[:3]) for w in which]
    work = sum(len(w[1]) * w[3] for w in which)
    return pl.pallas_call(
        functools.partial(block_kernel, tiles),
        out_shape=[jax.ShapeDtypeStruct((len(w[1]), w[3], HD), w[4]) for w in which],
        compiler_params=pltpu.CompilerParams(vmem_limit_bytes=VMEM),
        cost_estimate=pl.CostEstimate(
            flops=2 * work * HD * (tokens + unit.shape[1]),
            bytes_accessed=work * HD * 4 + len(which) * RING * tokens * HD * 2,
            transcendentals=0,
        ),
    )(unit, lat, mom_own, mom_other, grad, *[own[near] for near in nears])


def middle_kernel(kept, upper, lower, one, three, two_a, two_b, kept_out, one_out, three_out):
    half = upper.shape[1]
    for k in range(kept.shape[0]):
        kept_out[k, :half] = kept[k, :half] + upper[k].astype(f32)
        kept_out[k, half:] = kept[k, half:] + lower[k].astype(f32)
    one_out[...] = (one[0] + two_b[0].astype(f32)).astype(bf16)
    three_out[...] = (three[0] + two_a[0].astype(f32)).astype(bf16)


def middle(kept, upper, *parts):
    stay = jax.ShapeDtypeStruct(upper.shape[1:], bf16)
    return pl.pallas_call(
        middle_kernel,
        out_shape=[jax.ShapeDtypeStruct(kept.shape, f32), stay, stay],
        compiler_params=pltpu.CompilerParams(vmem_limit_bytes=VMEM),
        cost_estimate=pl.CostEstimate(flops=MIDDLE, bytes_accessed=0, transcendentals=0),
    )(kept, upper, *parts)


def stay_kernel(kept, upper, lower, out):
    half = upper.shape[0]
    out[:half, :] = kept[0, :half] + upper[...].astype(f32)
    out[half:, :] = kept[0, half:] + lower[...].astype(f32)


def stay_sum(kept, upper, lower):
    return pl.pallas_call(
        stay_kernel,
        out_shape=jax.ShapeDtypeStruct(kept.shape[1:], f32),
        compiler_params=pltpu.CompilerParams(vmem_limit_bytes=VMEM),
        cost_estimate=pl.CostEstimate(flops=MIDDLE, bytes_accessed=0, transcendentals=0),
    )(kept, upper, lower)


def add_kernel(kept, upper, lower, *outs):
    half = upper.shape[1]
    for k, out in enumerate(outs):
        out[:half, :] = (kept[k + 1, :half] + upper[k].astype(f32)).astype(out.dtype)
        out[half:, :] = (kept[k + 1, half:] + lower[k].astype(f32)).astype(out.dtype)


def add_up(kept, upper, lower):
    heads, rows, columns = kept.shape
    return pl.pallas_call(
        add_kernel,
        out_shape=[jax.ShapeDtypeStruct((rows, columns), bf16)] * (heads - 1),
        compiler_params=pltpu.CompilerParams(vmem_limit_bytes=VMEM),
    )(kept, upper, lower)


def split(value):
    high = value.astype(bf16)
    return high, (value - high.astype(f32)).astype(bf16)


def product(a, b, dims):
    (left,), (right,) = dims
    return lax.dot_general(
        jnp.concatenate([a[0], a[0], a[1]], axis=left),
        jnp.concatenate([b[0], b[1], b[0]], axis=right),
        (dims, ((), ())),
        preferred_element_type=f32,
    )


def newton_schulz_kernel(moment_ref, out_ref):
    moment = moment_ref[...]
    rows, columns = moment.shape
    scale = 0.2 * math.sqrt(max(rows, columns))
    wide = moment.T
    gram = lax.dot_general(wide, wide, (((1,), (1,)), ((), ())), preferred_element_type=f32)
    wide = wide.astype(f32)
    inverse = 1.0 / (jnp.sqrt(jnp.sum(wide * wide)) + 1e-7)
    gram = (gram * inverse) * inverse
    x = wide * inverse
    for step in range(NS_STEPS):
        pair = split(x)
        if step > 0:
            gram = product(pair, pair, ((1,), (1,)))
        gram_pair = split(gram)
        poly = COEF_B * gram + COEF_C * product(gram_pair, gram_pair, ((1,), (0,)))
        x = COEF_A * x + product(split(poly), pair, ((1,), (0,)))
    update = (scale * x).T.astype(bf16)
    owners = out_ref.shape[0]
    depth = rows // owners
    for c in range(NC):
        for chip in range(owners // NC):
            at = slice((chip * NC + c) * depth, (chip * NC + c + 1) * depth)
            out_ref[c * (owners // NC) + chip, 0] = update[at, :]
            out_ref[c * (owners // NC) + chip, 1] = moment[at, :]


def newton_schulz(moment, owners):
    rows, columns = moment.shape
    return pl.pallas_call(
        newton_schulz_kernel,
        out_shape=jax.ShapeDtypeStruct((owners, 2, rows // owners, columns), bf16),
        compiler_params=pltpu.CompilerParams(vmem_limit_bytes=VMEM),
    )(moment)


def spread_kernel(returned, moment, update, moment_held, update_held, sems):
    half = moment_held.shape[1] // NC
    copies = []
    for c in range(NC):
        for y in range(NY):
            for x in range(NX):
                source = (c * NY + y) * NX + x
                head = c * NY * NX + (RING * x + y if c == 0 else RING * y + x)
                at = slice(head * HD, (head + 1) * HD)
                update_held[:, at] = returned[source, 0]
                moment_held[:, at] = returned[source, 1].astype(f32)
        done = pl.ds(c * half, half)
        for k, (held, out) in enumerate(((moment_held, moment), (update_held, update))):
            copies.append(pltpu.make_async_copy(held.at[:, done], out.at[:, done], sems.at[c, k]))
            copies[-1].start()
    for copy in copies:
        copy.wait()


def spread(returned):
    heads, _, rows, columns = returned.shape
    moment = jax.ShapeDtypeStruct((rows, heads * columns), f32)
    update = jax.ShapeDtypeStruct((rows, heads * columns), bf16)
    hbm = pl.BlockSpec(memory_space=pl.ANY)
    return pl.pallas_call(
        spread_kernel,
        out_shape=(moment, update),
        in_specs=[pl.BlockSpec(memory_space=pltpu.VMEM)],
        out_specs=(hbm, hbm),
        scratch_shapes=[
            pltpu.VMEM(moment.shape, f32),
            pltpu.VMEM(update.shape, bf16),
            pltpu.SemaphoreType.DMA((NC, 2)),
        ],
        compiler_params=pltpu.CompilerParams(vmem_limit_bytes=VMEM),
    )(returned)


def body(latent, latent_grad, row_counts, momentum):
    features = latent.shape[1]
    order = (2, 1, 3)
    tie = lax.optimization_barrier

    early, late = (2,), (1, 3, 0)
    piece_early, mine = column_pieces(latent_grad, [(early, True), (early, False)])
    lat_own, mom_own, mom_other, unit, own_early = first(row_counts, latent, momentum, mine)
    grad_late, own_early = tie((latent_grad, own_early))
    (piece_late,) = column_pieces(grad_late, [(late, True)])
    piece_early, lat_other, mom_other = (
        swap_cores(piece_early), swap_cores(lat_own), swap_cores(mom_other)
    )
    piece_late, piece_early, lat_other, mom_other = tie((piece_late, piece_early, lat_other, mom_other))
    piece_late = swap_cores(piece_late)
    shared = (unit, lat_other, mom_own, mom_other)

    half = features // 2
    upper, lower, whole = (0, half), (half, half), (0, features)
    every = (0, 1, 2, 3)
    own = {2: own_early}
    two_a, two_b = block(
        own, early, [(2, every, *upper, bf16), (2, every, *lower, bf16)], *shared, piece_early
    )
    lat_late, two_a, two_b = tie((lat_own, two_a, two_b))
    own[1], own[3], own[0] = own_products(lat_late, latent_grad, late)
    (one_a,) = block(own, late, [(1, every, *upper, bf16)], *shared, piece_late)
    (three_b,) = block(own, late, [(3, every, *lower, bf16)], *shared, piece_late)
    own[0], one_a, three_b = tie((own[0], one_a, three_b))
    one_b, three_a, kept = block(
        own,
        late,
        [(1, every, *lower, f32), (3, every, *upper, f32), (0, every, *whole, f32)],
        *shared,
        piece_late,
    )
    two_a, two_b = exchange(two_a, 0, 1), exchange(two_b, 0, 3)
    one_a, three_b = exchange(one_a, 0, 1), exchange(three_b, 0, 3)
    three_on = exchange((three_a[1:] + two_a[1:].astype(f32)).astype(bf16), 0, 3)
    one_on = exchange((one_b[1:] + two_b[1:].astype(f32)).astype(bf16), 0, 1)
    kept, one_stay, three_stay = middle(kept, one_a, three_b, one_b, three_a, two_a, two_b)
    one_stay, three_stay = exchange(one_stay, 0, 1), exchange(three_stay, 0, 3)

    sums = add_up(kept, three_on, one_on)
    got = [exchange(sums[k - 1], 1, k) for k in order]
    head = stay_sum(kept, three_stay, one_stay)
    head = (head + sum(value.astype(f32) for value in got)).astype(bf16)

    pieces = lax.all_to_all(head.reshape(NZ, -1, HD), "z", 0, 0, tiled=True)
    piece = jnp.sum(pieces.astype(f32), axis=0).astype(bf16)
    moment = lax.all_to_all(jnp.broadcast_to(piece, (NZ,) + piece.shape), "z", 0, 0, tiled=True)
    moment = moment.reshape(features, HD)

    outgoing = newton_schulz(moment, NC * NY * NX)
    returned = lax.all_to_all(outgoing, PLANE, 0, 0, tiled=True)
    return tuple(spread(returned))


def solution(mesh):
    fine = Mesh(mesh.devices.reshape(NZ, NY, NX, NC), AXES)
    shard = ("y", "x", "c")
    in_specs = (P(AXES, None), P(AXES, None), P(AXES), P(shard, None))
    out_specs = (P(shard, None), P(shard, None))
    return jax.shard_map(body, mesh=fine, in_specs=in_specs, out_specs=out_specs, check_vma=False)
```

```python
import functools
import math

import jax
import jax.numpy as jnp
from jax import lax
from jax.experimental import pallas as pl
from jax.experimental.pallas import tpu as pltpu
from jax.sharding import Mesh
from jax.sharding import PartitionSpec as P

HD = 256
NS_STEPS = 5
NZ, NY, NX, NC = 8, 4, 4, 2
RING = 4
AXES = ("z", "y", "x", "c")
PLANE = ("c", "y", "x")
COEF_A, COEF_B, COEF_C = 3.4445, -4.775, 2.0315
DECAY = 0.95
VMEM = 16 * 1024 * 1024
MIDDLE = 5 * 10**9
LARGE = 48 * 1024 * 1024
LARGER = 52 * 1024 * 1024
bf16, f32 = jnp.bfloat16, jnp.float32


def device_at(z, y, x, c):
    return ((z * NY + y) * NX + x) * NC + c


def every_device():
    return [(z, y, x, c) for z in range(NZ) for y in range(NY) for x in range(NX) for c in range(NC)]


def exchange(value, axis, distance):
    pairs = []
    for z, y, x, c in every_device():
        if axis == c:
            to = (y, x ^ distance)
        else:
            to = (y ^ distance, x)
        pairs.append((device_at(z, y, x, c), device_at(z, *to, c)))
    return lax.ppermute(value, AXES, pairs)


def swap_cores(value):
    return lax.ppermute(
        value, AXES, [(device_at(z, y, x, c), device_at(z, y, x, 1 - c)) for z, y, x, c in every_device()]
    )


def places():
    core, y, x = lax.axis_index("c"), lax.axis_index("y"), lax.axis_index("x")
    return jnp.where(core == 0, x, y), jnp.where(core == 0, y, x)


def head_columns(near, far, other=False):
    first, second = places()
    if other:
        first, second = second, first
    head = (first ^ near) * RING + (second ^ far)
    return pl.multiple_of(head * HD, HD)


def gather(grad, held, sems, nears, other):
    core = lax.axis_index("c")
    base = (1 - core if other else core) * (grad.shape[1] // NC)
    copies = []
    for near in nears:
        for far in range(RING):
            k = len(copies)
            start = pl.multiple_of(base + head_columns(near, far, other), HD)
            copies.append(
                pltpu.make_async_copy(grad.at[:, pl.ds(start, HD)], held.at[k], sems.at[k])
            )
    return copies


def pieces_kernel(lists, grad, *refs):
    outs, (held, sems_in, sems_out) = refs[: len(lists)], refs[len(lists) :]
    into, onto = [], []
    for (nears, other), out in zip(lists, outs):
        at = len(into)
        count = RING * len(nears)
        into += gather(grad, held.at[pl.ds(at, count)], sems_in.at[pl.ds(at, count)], nears, other)
        for k in range(count):
            onto.append(
                pltpu.make_async_copy(
                    held.at[at + k], out.at[:, k * HD : (k + 1) * HD], sems_out.at[at + k]
                )
            )
    for copy in into:
        copy.start()
    for k in range(len(into)):
        into[k].wait()
        onto[k].start()
    for copy in onto:
        copy.wait()


def column_pieces(grad, lists):
    slots = grad.shape[0]
    widths = [RING * len(nears) for nears, _ in lists]
    hbm = pl.BlockSpec(memory_space=pl.ANY)
    return pl.pallas_call(
        functools.partial(pieces_kernel, lists),
        out_shape=[jax.ShapeDtypeStruct((slots, width * HD), bf16) for width in widths],
        in_specs=[hbm],
        out_specs=[hbm] * len(lists),
        scratch_shapes=[
            pltpu.VMEM((sum(widths), slots, HD), bf16),
            pltpu.SemaphoreType.DMA((sum(widths),)),
            pltpu.SemaphoreType.DMA((sum(widths),)),
        ],
        compiler_params=pltpu.CompilerParams(vmem_limit_bytes=LARGER),
    )(grad)


def first_kernel(counts, latent, momentum, mine, lat, mom_own, mom_other, unit, own):
    core = lax.axis_index("c")
    slots, features = latent.shape
    depth, half = momentum.shape[0], momentum.shape[1] // NC
    live = lax.broadcasted_iota(jnp.int32, (slots, features), 0) < counts[0]
    lat[...] = jnp.where(live, latent[...], jnp.zeros_like(latent)).T
    for out, which in ((mom_own, core), (mom_other, 1 - core)):
        value = (DECAY / NZ) * momentum[:, pl.ds(pl.multiple_of(which * half, half), half)]
        high = value.astype(bf16)
        out[:depth, :] = high
        out[depth:, :] = (value - high.astype(f32)).astype(bf16)
    here = lax.axis_index("y") * NX + lax.axis_index("x")
    row = lax.broadcasted_iota(jnp.int32, unit.shape, 0)
    at = lax.broadcasted_iota(jnp.int32, unit.shape, 1)
    core_of = jnp.where(at < 2 * depth, core, 1 - core)
    unit[...] = (row == (here * NC + core_of) * depth + at % depth).astype(f32).astype(bf16)
    for far in range(RING):
        columns = mine[:, far * HD : (far + 1) * HD]
        own[far] = jnp.dot(lat[...], columns, preferred_element_type=f32).astype(bf16)


def first(counts, latent, momentum, mine):
    slots, features = latent.shape
    depth, columns = momentum.shape
    vmem = pl.BlockSpec(memory_space=pltpu.VMEM)
    mom = jax.ShapeDtypeStruct((2 * depth, columns // NC), bf16)
    return pl.pallas_call(
        first_kernel,
        out_shape=[
            jax.ShapeDtypeStruct((features, slots), bf16),
            mom,
            mom,
            jax.ShapeDtypeStruct((features, 4 * depth), bf16),
            jax.ShapeDtypeStruct((RING, features, HD), bf16),
        ],
        in_specs=[pl.BlockSpec(memory_space=pltpu.SMEM), vmem, vmem, vmem],
        compiler_params=pltpu.CompilerParams(vmem_limit_bytes=VMEM),
    )(counts, latent, momentum, mine)


def own_kernel(nears, lat, grad, *refs):
    outs, (held, sems) = refs[: len(nears)], refs[len(nears) :]
    copies = gather(grad, held, sems, nears, False)
    for copy in copies:
        copy.start()
    for near in range(len(nears)):
        for far in range(RING):
            copies[near * RING + far].wait()
        for far in range(RING):
            value = jnp.dot(lat[...], held[near * RING + far], preferred_element_type=f32)
            outs[near][far] = value.astype(bf16)


def own_products(lat, grad, nears):
    features, tokens = lat.shape
    count = RING * len(nears)
    vmem = pl.BlockSpec(memory_space=pltpu.VMEM)
    return pl.pallas_call(
        functools.partial(own_kernel, nears),
        out_shape=[jax.ShapeDtypeStruct((RING, features, HD), bf16)] * len(nears),
        in_specs=[vmem, pl.BlockSpec(memory_space=pl.ANY)],
        out_specs=[vmem] * len(nears),
        scratch_shapes=[
            pltpu.VMEM((count, tokens, HD), bf16),
            pltpu.SemaphoreType.DMA((count,)),
        ],
        compiler_params=pltpu.CompilerParams(vmem_limit_bytes=LARGE),
        cost_estimate=pl.CostEstimate(
            flops=2 * count * features * HD * tokens,
            bytes_accessed=count * (tokens + features) * HD * 2,
            transcendentals=0,
        ),
    )(lat, grad)


def block_kernel(tiles, unit, lat, mom_own, mom_other, grad, *refs):
    count = 1 + max(t[0] for t in tiles)
    operands, outs = refs[:count], refs[count:]
    for (operand, at_piece, near, fars, row), out in zip(tiles, outs):
        rows = slice(row, row + out.shape[1])
        for place, far in enumerate(fars):
            at = pl.ds(head_columns(near, far), HD)
            in_piece = (at_piece * RING + far) * HD
            mom = jnp.concatenate([mom_own[:, at], mom_other[:, at]], axis=0)
            other = jnp.dot(
                lat[rows, :], grad[:, in_piece : in_piece + HD], preferred_element_type=f32
            )
            added = jnp.dot(unit[rows, :], mom, preferred_element_type=f32)
            total = operands[operand][far, rows].astype(f32) + other.astype(bf16).astype(f32) + added
            out[place] = total.astype(out.dtype)


def block(own, held, which, unit, lat, mom_own, mom_other, grad):
    tokens = lat.shape[1]
    nears = sorted({w[0] for w in which})
    tiles = [(nears.index(w[0]), held.index(w[0]), *w[:3]) for w in which]
    work = sum(len(w[1]) * w[3] for w in which)
    return pl.pallas_call(
        functools.partial(block_kernel, tiles),
        out_shape=[jax.ShapeDtypeStruct((len(w[1]), w[3], HD), w[4]) for w in which],
        compiler_params=pltpu.CompilerParams(vmem_limit_bytes=VMEM),
        cost_estimate=pl.CostEstimate(
            flops=2 * work * HD * (tokens + unit.shape[1]),
            bytes_accessed=work * HD * 4 + len(which) * RING * tokens * HD * 2,
            transcendentals=0,
        ),
    )(unit, lat, mom_own, mom_other, grad, *[own[near] for near in nears])


def middle_kernel(kept, upper, lower, out):
    half = upper.shape[1]
    for k in range(kept.shape[0]):
        out[k, :half] = kept[k, :half] + upper[k].astype(f32)
        out[k, half:] = kept[k, half:] + lower[k].astype(f32)


def middle(kept, upper, lower):
    return pl.pallas_call(
        middle_kernel,
        out_shape=jax.ShapeDtypeStruct(kept.shape, f32),
        compiler_params=pltpu.CompilerParams(vmem_limit_bytes=VMEM),
        cost_estimate=pl.CostEstimate(flops=MIDDLE, bytes_accessed=0, transcendentals=0),
    )(kept, upper, lower)


def stay_kernel(kept, one, two, three, out):
    out[...] = kept[0] + one[0].astype(f32) + two[0].astype(f32) + three[0].astype(f32)


def stay_sum(kept, *parts):
    return pl.pallas_call(
        stay_kernel,
        out_shape=jax.ShapeDtypeStruct(kept.shape[1:], f32),
        compiler_params=pltpu.CompilerParams(vmem_limit_bytes=VMEM),
        cost_estimate=pl.CostEstimate(flops=MIDDLE, bytes_accessed=0, transcendentals=0),
    )(kept, *parts)


def add_kernel(kept, upper, lower, *outs):
    half = upper.shape[1]
    for k, out in enumerate(outs):
        out[:half, :] = (kept[k, :half] + upper[k].astype(f32)).astype(out.dtype)
        out[half:, :] = (kept[k, half:] + lower[k].astype(f32)).astype(out.dtype)


def add_up(kept, *parts):
    heads, rows, columns = kept.shape
    return pl.pallas_call(
        add_kernel,
        out_shape=[jax.ShapeDtypeStruct((rows, columns), bf16)] * heads,
        compiler_params=pltpu.CompilerParams(vmem_limit_bytes=VMEM),
    )(kept, *parts)


def split(value):
    high = value.astype(bf16)
    return high, (value - high.astype(f32)).astype(bf16)


def product(a, b, dims):
    (left,), (right,) = dims
    return lax.dot_general(
        jnp.concatenate([a[0], a[0], a[1]], axis=left),
        jnp.concatenate([b[0], b[1], b[0]], axis=right),
        (dims, ((), ())),
        preferred_element_type=f32,
    )


def newton_schulz_kernel(moment_ref, out_ref):
    moment = moment_ref[...]
    rows, columns = moment.shape
    scale = 0.2 * math.sqrt(max(rows, columns))
    wide = moment.T
    gram = lax.dot_general(wide, wide, (((1,), (1,)), ((), ())), preferred_element_type=f32)
    wide = wide.astype(f32)
    inverse = 1.0 / (jnp.sqrt(jnp.sum(wide * wide)) + 1e-7)
    gram = (gram * inverse) * inverse
    x = wide * inverse
    for step in range(NS_STEPS):
        pair = split(x)
        if step > 0:
            gram = product(pair, pair, ((1,), (1,)))
        gram_pair = split(gram)
        poly = COEF_B * gram + COEF_C * product(gram_pair, gram_pair, ((1,), (0,)))
        x = COEF_A * x + product(split(poly), pair, ((1,), (0,)))
    update = (scale * x).T.astype(bf16)
    owners = out_ref.shape[0]
    depth = rows // owners
    for c in range(NC):
        for chip in range(owners // NC):
            at = slice((chip * NC + c) * depth, (chip * NC + c + 1) * depth)
            out_ref[c * (owners // NC) + chip, 0] = update[at, :]
            out_ref[c * (owners // NC) + chip, 1] = moment[at, :]


def newton_schulz(moment, owners):
    rows, columns = moment.shape
    return pl.pallas_call(
        newton_schulz_kernel,
        out_shape=jax.ShapeDtypeStruct((owners, 2, rows // owners, columns), bf16),
        compiler_params=pltpu.CompilerParams(vmem_limit_bytes=VMEM),
    )(moment)


def spread_kernel(returned, moment, update, moment_held, update_held, sems):
    half = moment_held.shape[1] // NC
    copies = []
    for c in range(NC):
        for y in range(NY):
            for x in range(NX):
                source = (c * NY + y) * NX + x
                head = c * NY * NX + (RING * x + y if c == 0 else RING * y + x)
                at = slice(head * HD, (head + 1) * HD)
                update_held[:, at] = returned[source, 0]
                moment_held[:, at] = returned[source, 1].astype(f32)
        done = pl.ds(c * half, half)
        for k, (held, out) in enumerate(((moment_held, moment), (update_held, update))):
            copies.append(pltpu.make_async_copy(held.at[:, done], out.at[:, done], sems.at[c, k]))
            copies[-1].start()
    for copy in copies:
        copy.wait()


def spread(returned):
    heads, _, rows, columns = returned.shape
    moment = jax.ShapeDtypeStruct((rows, heads * columns), f32)
    update = jax.ShapeDtypeStruct((rows, heads * columns), bf16)
    hbm = pl.BlockSpec(memory_space=pl.ANY)
    return pl.pallas_call(
        spread_kernel,
        out_shape=(moment, update),
        in_specs=[pl.BlockSpec(memory_space=pltpu.VMEM)],
        out_specs=(hbm, hbm),
        scratch_shapes=[
            pltpu.VMEM(moment.shape, f32),
            pltpu.VMEM(update.shape, bf16),
            pltpu.SemaphoreType.DMA((NC, 2)),
        ],
        compiler_params=pltpu.CompilerParams(vmem_limit_bytes=VMEM),
    )(returned)


def body(latent, latent_grad, row_counts, momentum):
    features = latent.shape[1]
    order = (2, 1, 3)
    tie = lax.optimization_barrier

    early, late = (2,), (1, 3, 0)
    piece_early, mine = column_pieces(latent_grad, [(early, True), (early, False)])
    lat_own, mom_own, mom_other, unit, own_early = first(row_counts, latent, momentum, mine)
    grad_late, own_early = tie((latent_grad, own_early))
    (piece_late,) = column_pieces(grad_late, [(late, True)])
    piece_early, lat_other, mom_other = (
        swap_cores(piece_early), swap_cores(lat_own), swap_cores(mom_other)
    )
    piece_late, piece_early, lat_other, mom_other = tie((piece_late, piece_early, lat_other, mom_other))
    piece_late = swap_cores(piece_late)
    shared = (unit, lat_other, mom_own, mom_other)

    half = features // 2
    upper, lower, whole = (0, half), (half, half), (0, features)
    rest, stay = (1, 2, 3), (0,)
    own = {2: own_early}
    two_a, two_b = block(
        own, early, [(2, rest, *upper, bf16), (2, rest, *lower, bf16)], *shared, piece_early
    )
    lat_late, two_a, two_b = tie((lat_own, two_a, two_b))
    own[1], own[3], own[0] = own_products(lat_late, latent_grad, late)
    (one_a,) = block(own, late, [(1, rest, *upper, bf16)], *shared, piece_late)
    (three_b,) = block(own, late, [(3, rest, *lower, bf16)], *shared, piece_late)
    own[0], own[2], one_a, three_b = tie((own[0], own[2], one_a, three_b))
    one_b, three_a, one_stay, three_stay, kept_on, kept_stay = block(
        own,
        late,
        [
            (1, rest, *lower, f32),
            (3, rest, *upper, f32),
            (1, stay, *whole, bf16),
            (3, stay, *whole, bf16),
            (0, rest, *whole, f32),
            (0, stay, *whole, f32),
        ],
        *shared,
        piece_late,
    )
    (two_stay,) = block(own, early, [(2, stay, *whole, bf16)], *shared, piece_early)
    two_a, two_b = exchange(two_a, 0, 1), exchange(two_b, 0, 3)
    one_a, three_b = exchange(one_a, 0, 1), exchange(three_b, 0, 3)
    three_a = exchange((three_a + two_a.astype(f32)).astype(bf16), 0, 3)
    one_b = exchange((one_b + two_b.astype(f32)).astype(bf16), 0, 1)
    kept_on = middle(kept_on, one_a, three_b)
    one_stay, two_stay, three_stay, kept_on = tie((one_stay, two_stay, three_stay, kept_on))
    one_stay, two_stay, three_stay = (
        exchange(one_stay, 0, 1), exchange(two_stay, 0, 2), exchange(three_stay, 0, 3)
    )

    sums = add_up(kept_on, three_a, one_b)
    got = [exchange(sums[k - 1], 1, k) for k in order]
    head = stay_sum(kept_stay, one_stay, two_stay, three_stay)
    head = (head + sum(value.astype(f32) for value in got)).astype(bf16)

    pieces = lax.all_to_all(head.reshape(NZ, -1, HD), "z", 0, 0, tiled=True)
    piece = jnp.sum(pieces.astype(f32), axis=0).astype(bf16)
    moment = lax.all_to_all(jnp.broadcast_to(piece, (NZ,) + piece.shape), "z", 0, 0, tiled=True)
    moment = moment.reshape(features, HD)

    outgoing = newton_schulz(moment, NC * NY * NX)
    returned = lax.all_to_all(outgoing, PLANE, 0, 0, tiled=True)
    return tuple(spread(returned))


def solution(mesh):
    fine = Mesh(mesh.devices.reshape(NZ, NY, NX, NC), AXES)
    shard = ("y", "x", "c")
    in_specs = (P(AXES, None), P(AXES, None), P(AXES), P(shard, None))
    out_specs = (P(shard, None), P(shard, None))
    return jax.shard_map(body, mesh=fine, in_specs=in_specs, out_specs=out_specs, check_vma=False)
```

```python
import functools
import math

import jax
import jax.numpy as jnp
from jax import lax
from jax.experimental import pallas as pl
from jax.experimental.pallas import tpu as pltpu
from jax.sharding import Mesh
from jax.sharding import PartitionSpec as P

HD = 256
NS_STEPS = 5
NZ, NY, NX, NC = 8, 4, 4, 2
RING = 4
AXES = ("z", "y", "x", "c")
PLANE = ("c", "y", "x")
COEF_A, COEF_B, COEF_C = 3.4445, -4.775, 2.0315
DECAY = 0.95
VMEM = 16 * 1024 * 1024
MIDDLE = 5 * 10**9
LARGE = 48 * 1024 * 1024
LARGER = 52 * 1024 * 1024
bf16, f32 = jnp.bfloat16, jnp.float32


def device_at(z, y, x, c):
    return ((z * NY + y) * NX + x) * NC + c


def every_device():
    return [(z, y, x, c) for z in range(NZ) for y in range(NY) for x in range(NX) for c in range(NC)]


def exchange(value, axis, distance):
    pairs = []
    for z, y, x, c in every_device():
        if axis == c:
            to = (y, x ^ distance)
        else:
            to = (y ^ distance, x)
        pairs.append((device_at(z, y, x, c), device_at(z, *to, c)))
    return lax.ppermute(value, AXES, pairs)


def swap_cores(value):
    return lax.ppermute(
        value, AXES, [(device_at(z, y, x, c), device_at(z, y, x, 1 - c)) for z, y, x, c in every_device()]
    )


def places():
    core, y, x = lax.axis_index("c"), lax.axis_index("y"), lax.axis_index("x")
    return jnp.where(core == 0, x, y), jnp.where(core == 0, y, x)


def head_columns(near, far, other=False):
    first, second = places()
    if other:
        first, second = second, first
    head = (first ^ near) * RING + (second ^ far)
    return pl.multiple_of(head * HD, HD)


def gather(grad, held, sems, nears, other):
    core = lax.axis_index("c")
    base = (1 - core if other else core) * (grad.shape[1] // NC)
    copies = []
    for near in nears:
        for far in range(RING):
            k = len(copies)
            start = pl.multiple_of(base + head_columns(near, far, other), HD)
            copies.append(
                pltpu.make_async_copy(grad.at[:, pl.ds(start, HD)], held.at[k], sems.at[k])
            )
    return copies


def pieces_kernel(lists, grad, *refs):
    outs, (held, sems_in, sems_out) = refs[: len(lists)], refs[len(lists) :]
    into, onto = [], []
    for (nears, other), out in zip(lists, outs):
        at = len(into)
        count = RING * len(nears)
        into += gather(grad, held.at[pl.ds(at, count)], sems_in.at[pl.ds(at, count)], nears, other)
        for k in range(count):
            onto.append(
                pltpu.make_async_copy(
                    held.at[at + k], out.at[:, k * HD : (k + 1) * HD], sems_out.at[at + k]
                )
            )
    for copy in into:
        copy.start()
    for k in range(len(into)):
        into[k].wait()
        onto[k].start()
    for copy in onto:
        copy.wait()


def column_pieces(grad, lists):
    slots = grad.shape[0]
    widths = [RING * len(nears) for nears, _ in lists]
    hbm = pl.BlockSpec(memory_space=pl.ANY)
    return pl.pallas_call(
        functools.partial(pieces_kernel, lists),
        out_shape=[jax.ShapeDtypeStruct((slots, width * HD), bf16) for width in widths],
        in_specs=[hbm],
        out_specs=[hbm] * len(lists),
        scratch_shapes=[
            pltpu.VMEM((sum(widths), slots, HD), bf16),
            pltpu.SemaphoreType.DMA((sum(widths),)),
            pltpu.SemaphoreType.DMA((sum(widths),)),
        ],
        compiler_params=pltpu.CompilerParams(vmem_limit_bytes=LARGER),
    )(grad)


def first_kernel(counts, latent, momentum, mine, lat, mom_own, mom_other, unit, own):
    core = lax.axis_index("c")
    slots, features = latent.shape
    depth, half = momentum.shape[0], momentum.shape[1] // NC
    live = lax.broadcasted_iota(jnp.int32, (slots, features), 0) < counts[0]
    lat[...] = jnp.where(live, latent[...], jnp.zeros_like(latent)).T
    for out, which in ((mom_own, core), (mom_other, 1 - core)):
        value = (DECAY / NZ) * momentum[:, pl.ds(pl.multiple_of(which * half, half), half)]
        high = value.astype(bf16)
        out[:depth, :] = high
        out[depth:, :] = (value - high.astype(f32)).astype(bf16)
    here = lax.axis_index("y") * NX + lax.axis_index("x")
    row = lax.broadcasted_iota(jnp.int32, unit.shape, 0)
    at = lax.broadcasted_iota(jnp.int32, unit.shape, 1)
    core_of = jnp.where(at < 2 * depth, core, 1 - core)
    unit[...] = (row == (here * NC + core_of) * depth + at % depth).astype(f32).astype(bf16)
    for far in range(RING):
        columns = mine[:, far * HD : (far + 1) * HD]
        own[far] = jnp.dot(lat[...], columns, preferred_element_type=f32).astype(bf16)


def first(counts, latent, momentum, mine):
    slots, features = latent.shape
    depth, columns = momentum.shape
    vmem = pl.BlockSpec(memory_space=pltpu.VMEM)
    mom = jax.ShapeDtypeStruct((2 * depth, columns // NC), bf16)
    return pl.pallas_call(
        first_kernel,
        out_shape=[
            jax.ShapeDtypeStruct((features, slots), bf16),
            mom,
            mom,
            jax.ShapeDtypeStruct((features, 4 * depth), bf16),
            jax.ShapeDtypeStruct((RING, features, HD), bf16),
        ],
        in_specs=[pl.BlockSpec(memory_space=pltpu.SMEM), vmem, vmem, vmem],
        compiler_params=pltpu.CompilerParams(vmem_limit_bytes=VMEM),
    )(counts, latent, momentum, mine)


def own_kernel(nears, lat, grad, *refs):
    outs, (held, sems) = refs[: len(nears)], refs[len(nears) :]
    copies = gather(grad, held, sems, nears, False)
    for copy in copies:
        copy.start()
    for near in range(len(nears)):
        for far in range(RING):
            copies[near * RING + far].wait()
        for far in range(RING):
            value = jnp.dot(lat[...], held[near * RING + far], preferred_element_type=f32)
            outs[near][far] = value.astype(bf16)


def own_products(lat, grad, nears):
    features, tokens = lat.shape
    count = RING * len(nears)
    vmem = pl.BlockSpec(memory_space=pltpu.VMEM)
    return pl.pallas_call(
        functools.partial(own_kernel, nears),
        out_shape=[jax.ShapeDtypeStruct((RING, features, HD), bf16)] * len(nears),
        in_specs=[vmem, pl.BlockSpec(memory_space=pl.ANY)],
        out_specs=[vmem] * len(nears),
        scratch_shapes=[
            pltpu.VMEM((count, tokens, HD), bf16),
            pltpu.SemaphoreType.DMA((count,)),
        ],
        compiler_params=pltpu.CompilerParams(vmem_limit_bytes=LARGE),
        cost_estimate=pl.CostEstimate(
            flops=2 * count * features * HD * tokens,
            bytes_accessed=count * (tokens + features) * HD * 2,
            transcendentals=0,
        ),
    )(lat, grad)


def block_kernel(tiles, unit, lat, mom_own, mom_other, grad, *refs):
    count = 1 + max(t[0] for t in tiles)
    operands, outs = refs[:count], refs[count:]
    for (operand, at_piece, near, fars, row), out in zip(tiles, outs):
        rows = slice(row, row + out.shape[1])
        for place, far in enumerate(fars):
            at = pl.ds(head_columns(near, far), HD)
            in_piece = (at_piece * RING + far) * HD
            mom = jnp.concatenate([mom_own[:, at], mom_other[:, at]], axis=0)
            other = jnp.dot(
                lat[rows, :], grad[:, in_piece : in_piece + HD], preferred_element_type=f32
            )
            added = jnp.dot(unit[rows, :], mom, preferred_element_type=f32)
            total = operands[operand][far, rows].astype(f32) + other.astype(bf16).astype(f32) + added
            out[place] = total.astype(out.dtype)


def block(own, held, which, unit, lat, mom_own, mom_other, grad):
    tokens = lat.shape[1]
    nears = sorted({w[0] for w in which})
    tiles = [(nears.index(w[0]), held.index(w[0]), *w[:3]) for w in which]
    work = sum(len(w[1]) * w[3] for w in which)
    return pl.pallas_call(
        functools.partial(block_kernel, tiles),
        out_shape=[jax.ShapeDtypeStruct((len(w[1]), w[3], HD), w[4]) for w in which],
        compiler_params=pltpu.CompilerParams(vmem_limit_bytes=VMEM),
        cost_estimate=pl.CostEstimate(
            flops=2 * work * HD * (tokens + unit.shape[1]),
            bytes_accessed=work * HD * 4 + len(which) * RING * tokens * HD * 2,
            transcendentals=0,
        ),
    )(unit, lat, mom_own, mom_other, grad, *[own[near] for near in nears])


def middle_kernel(kept, upper, lower, one, three, two_a, two_b, kept_out, one_out, three_out):
    half = upper.shape[1]
    for k in range(kept.shape[0]):
        kept_out[k, :half] = kept[k, :half] + upper[k].astype(f32)
        kept_out[k, half:] = kept[k, half:] + lower[k].astype(f32)
    one_out[:half, :] = one[0, :half].astype(bf16)
    one_out[half:, :] = (one[0, half:] + two_b[0].astype(f32)).astype(bf16)
    three_out[:half, :] = (three[0, :half] + two_a[0].astype(f32)).astype(bf16)
    three_out[half:, :] = three[0, half:].astype(bf16)


def middle(kept, *parts):
    stay = jax.ShapeDtypeStruct(kept.shape[1:], bf16)
    return pl.pallas_call(
        middle_kernel,
        out_shape=[jax.ShapeDtypeStruct(kept.shape, f32), stay, stay],
        compiler_params=pltpu.CompilerParams(vmem_limit_bytes=VMEM),
        cost_estimate=pl.CostEstimate(flops=MIDDLE, bytes_accessed=0, transcendentals=0),
    )(kept, *parts)


def stay_kernel(kept, one, three, out):
    out[...] = kept[0] + one[...].astype(f32) + three[...].astype(f32)


def stay_sum(kept, one, three):
    return pl.pallas_call(
        stay_kernel,
        out_shape=jax.ShapeDtypeStruct(kept.shape[1:], f32),
        compiler_params=pltpu.CompilerParams(vmem_limit_bytes=VMEM),
        cost_estimate=pl.CostEstimate(flops=MIDDLE, bytes_accessed=0, transcendentals=0),
    )(kept, one, three)


def add_kernel(kept, upper, lower, *outs):
    half = upper.shape[1]
    for k, out in enumerate(outs):
        out[:half, :] = (kept[k, :half] + upper[k].astype(f32)).astype(out.dtype)
        out[half:, :] = (kept[k, half:] + lower[k].astype(f32)).astype(out.dtype)


def add_up(kept, *parts):
    heads, rows, columns = kept.shape
    return pl.pallas_call(
        add_kernel,
        out_shape=[jax.ShapeDtypeStruct((rows, columns), bf16)] * heads,
        compiler_params=pltpu.CompilerParams(vmem_limit_bytes=VMEM),
    )(kept, *parts)


def split(value):
    high = value.astype(bf16)
    return high, (value - high.astype(f32)).astype(bf16)


def product(a, b, dims):
    (left,), (right,) = dims
    return lax.dot_general(
        jnp.concatenate([a[0], a[0], a[1]], axis=left),
        jnp.concatenate([b[0], b[1], b[0]], axis=right),
        (dims, ((), ())),
        preferred_element_type=f32,
    )


def newton_schulz_kernel(moment_ref, out_ref):
    moment = moment_ref[...]
    rows, columns = moment.shape
    scale = 0.2 * math.sqrt(max(rows, columns))
    wide = moment.T
    gram = lax.dot_general(wide, wide, (((1,), (1,)), ((), ())), preferred_element_type=f32)
    squares = wide.astype(f32) * wide.astype(f32)
    inverse = 1.0 / (jnp.sqrt(jnp.sum(squares)) + 1e-7)
    gram = (gram * inverse) * inverse
    at = [lax.broadcasted_iota(jnp.int32, gram.shape, axis) for axis in range(2)]
    identity = jnp.where(at[0] == at[1], COEF_A, 0.0)
    x = None
    for step in range(NS_STEPS):
        if step > 0:
            pair = split(x)
            gram = product(pair, pair, ((1,), (1,)))
        gram_pair = split(gram)
        poly = identity + COEF_B * gram + COEF_C * product(gram_pair, gram_pair, ((1,), (0,)))
        if step > 0:
            x = product(split(poly), pair, ((1,), (0,)))
        else:
            x = inverse * jnp.dot(
                jnp.concatenate(split(poly), axis=1),
                jnp.concatenate([wide, wide], axis=0),
                preferred_element_type=f32,
            )
    update = (scale * x).T.astype(bf16)
    owners = out_ref.shape[0]
    depth = rows // owners
    for c in range(NC):
        for chip in range(owners // NC):
            at = slice((chip * NC + c) * depth, (chip * NC + c + 1) * depth)
            out_ref[c * (owners // NC) + chip, 0] = update[at, :]
            out_ref[c * (owners // NC) + chip, 1] = moment[at, :]


def newton_schulz(moment, owners):
    rows, columns = moment.shape
    return pl.pallas_call(
        newton_schulz_kernel,
        out_shape=jax.ShapeDtypeStruct((owners, 2, rows // owners, columns), bf16),
        compiler_params=pltpu.CompilerParams(vmem_limit_bytes=VMEM),
    )(moment)


def spread_kernel(returned, moment, update, moment_held, update_held, sems):
    half = moment_held.shape[1] // NC
    copies = []
    for c in range(NC):
        for y in range(NY):
            for x in range(NX):
                source = (c * NY + y) * NX + x
                head = c * NY * NX + (RING * x + y if c == 0 else RING * y + x)
                at = slice(head * HD, (head + 1) * HD)
                update_held[:, at] = returned[source, 0]
                moment_held[:, at] = returned[source, 1].astype(f32)
        done = pl.ds(c * half, half)
        for k, (held, out) in enumerate(((moment_held, moment), (update_held, update))):
            copies.append(pltpu.make_async_copy(held.at[:, done], out.at[:, done], sems.at[c, k]))
            copies[-1].start()
    for copy in copies:
        copy.wait()


def spread(returned):
    heads, _, rows, columns = returned.shape
    moment = jax.ShapeDtypeStruct((rows, heads * columns), f32)
    update = jax.ShapeDtypeStruct((rows, heads * columns), bf16)
    hbm = pl.BlockSpec(memory_space=pl.ANY)
    return pl.pallas_call(
        spread_kernel,
        out_shape=(moment, update),
        in_specs=[pl.BlockSpec(memory_space=pltpu.VMEM)],
        out_specs=(hbm, hbm),
        scratch_shapes=[
            pltpu.VMEM(moment.shape, f32),
            pltpu.VMEM(update.shape, bf16),
            pltpu.SemaphoreType.DMA((NC, 2)),
        ],
        compiler_params=pltpu.CompilerParams(vmem_limit_bytes=VMEM),
    )(returned)


def body(latent, latent_grad, row_counts, momentum):
    features = latent.shape[1]
    order = (2, 1, 3)
    tie = lax.optimization_barrier

    early, late = (2,), (1, 3, 0)
    piece_early, mine = column_pieces(latent_grad, [(early, True), (early, False)])
    lat_own, mom_own, mom_other, unit, own_early = first(row_counts, latent, momentum, mine)
    grad_late, own_early = tie((latent_grad, own_early))
    (piece_late,) = column_pieces(grad_late, [(late, True)])
    piece_early, lat_other, mom_other = (
        swap_cores(piece_early), swap_cores(lat_own), swap_cores(mom_other)
    )
    piece_late, piece_early, lat_other, mom_other = tie((piece_late, piece_early, lat_other, mom_other))
    piece_late = swap_cores(piece_late)
    shared = (unit, lat_other, mom_own, mom_other)

    half = features // 2
    upper, lower, whole = (0, half), (half, half), (0, features)
    every, rest, stay = (0, 1, 2, 3), (1, 2, 3), (0,)
    own = {2: own_early}
    two_a, two_b = block(
        own, early, [(2, every, *upper, bf16), (2, every, *lower, bf16)], *shared, piece_early
    )
    lat_late, two_a, two_b = tie((lat_own, two_a, two_b))
    own[1], own[3] = own_products(lat_late, grad_late, late[:2])
    (one_a,) = block(own, late, [(1, rest, *upper, bf16)], *shared, piece_late)
    (three_b,) = block(own, late, [(3, rest, *lower, bf16)], *shared, piece_late)
    own[1], own[3], one_a, three_b = tie((own[1], own[3], one_a, three_b))
    one_b, three_a = block(
        own, late, [(1, rest, *lower, f32), (3, rest, *upper, f32)], *shared, piece_late
    )
    two_a, two_b = exchange(two_a, 0, 1), exchange(two_b, 0, 3)
    one_a, three_b = exchange(one_a, 0, 1), exchange(three_b, 0, 3)
    three_a = (three_a + two_a[1:].astype(f32)).astype(bf16)
    one_b = (one_b + two_b[1:].astype(f32)).astype(bf16)
    lat_last, own[1], one_b = tie((lat_late, own[1], one_b))
    three_a, one_b = exchange(three_a, 0, 3), exchange(one_b, 0, 1)
    (own[0],) = own_products(lat_last, grad_late, late[2:])
    one_stay, three_stay, kept_on, kept_stay = block(
        own,
        late,
        [
            (1, stay, *whole, f32),
            (3, stay, *whole, f32),
            (0, rest, *whole, f32),
            (0, stay, *whole, f32),
        ],
        *shared,
        piece_late,
    )
    kept_on, one_stay, three_stay = middle(
        kept_on, one_a, three_b, one_stay, three_stay, two_a, two_b
    )
    one_stay, three_stay = exchange(one_stay, 0, 1), exchange(three_stay, 0, 3)

    sums = add_up(kept_on, three_a, one_b)
    got = [exchange(sums[k - 1], 1, k) for k in order]
    head = stay_sum(kept_stay, one_stay, three_stay)
    head = (head + sum(value.astype(f32) for value in got)).astype(bf16)

    pieces = lax.all_to_all(head.reshape(NZ, -1, HD), "z", 0, 0, tiled=True)
    piece = jnp.sum(pieces.astype(f32), axis=0).astype(bf16)
    moment = lax.all_to_all(jnp.broadcast_to(piece, (NZ,) + piece.shape), "z", 0, 0, tiled=True)
    moment = moment.reshape(features, HD)

    outgoing = newton_schulz(moment, NC * NY * NX)
    returned = lax.all_to_all(outgoing, PLANE, 0, 0, tiled=True)
    return tuple(spread(returned))


def solution(mesh):
    fine = Mesh(mesh.devices.reshape(NZ, NY, NX, NC), AXES)
    shard = ("y", "x", "c")
    in_specs = (P(AXES, None), P(AXES, None), P(AXES), P(shard, None))
    out_specs = (P(shard, None), P(shard, None))
    return jax.shard_map(body, mesh=fine, in_specs=in_specs, out_specs=out_specs, check_vma=False)
```

```python
import functools
import math

import jax
import jax.numpy as jnp
from jax import lax
from jax.experimental import pallas as pl
from jax.experimental.pallas import tpu as pltpu
from jax.sharding import Mesh
from jax.sharding import PartitionSpec as P

HD = 256
NS_STEPS = 5
NZ, NY, NX, NC = 8, 4, 4, 2
RING = 4
AXES = ("z", "y", "x", "c")
PLANE = ("c", "y", "x")
COEF_A, COEF_B, COEF_C = 3.4445, -4.775, 2.0315
DECAY = 0.95
VMEM = 16 * 1024 * 1024
MIDDLE = 5 * 10**9
LARGE = 48 * 1024 * 1024
LARGER = 52 * 1024 * 1024
bf16, f32 = jnp.bfloat16, jnp.float32


def device_at(z, y, x, c):
    return ((z * NY + y) * NX + x) * NC + c


def every_device():
    return [(z, y, x, c) for z in range(NZ) for y in range(NY) for x in range(NX) for c in range(NC)]


def exchange(value, axis, distance):
    pairs = []
    for z, y, x, c in every_device():
        if axis == c:
            to = (y, x ^ distance)
        else:
            to = (y ^ distance, x)
        pairs.append((device_at(z, y, x, c), device_at(z, *to, c)))
    return lax.ppermute(value, AXES, pairs)


def swap_cores(value):
    return lax.ppermute(
        value, AXES, [(device_at(z, y, x, c), device_at(z, y, x, 1 - c)) for z, y, x, c in every_device()]
    )


def places():
    core, y, x = lax.axis_index("c"), lax.axis_index("y"), lax.axis_index("x")
    return jnp.where(core == 0, x, y), jnp.where(core == 0, y, x)


def head_columns(near, far, other=False):
    first, second = places()
    if other:
        first, second = second, first
    head = (first ^ near) * RING + (second ^ far)
    return pl.multiple_of(head * HD, HD)


def gather(grad, held, sems, nears, other):
    core = lax.axis_index("c")
    base = (1 - core if other else core) * (grad.shape[1] // NC)
    copies = []
    for near in nears:
        for far in range(RING):
            k = len(copies)
            start = pl.multiple_of(base + head_columns(near, far, other), HD)
            copies.append(
                pltpu.make_async_copy(grad.at[:, pl.ds(start, HD)], held.at[k], sems.at[k])
            )
    return copies


def pieces_kernel(lists, grad, *refs):
    outs, (held, sems_in, sems_out) = refs[: len(lists)], refs[len(lists) :]
    into, onto = [], []
    for (nears, other), out in zip(lists, outs):
        at = len(into)
        count = RING * len(nears)
        into += gather(grad, held.at[pl.ds(at, count)], sems_in.at[pl.ds(at, count)], nears, other)
        for k in range(count):
            onto.append(
                pltpu.make_async_copy(
                    held.at[at + k], out.at[:, k * HD : (k + 1) * HD], sems_out.at[at + k]
                )
            )
    for copy in into:
        copy.start()
    for k in range(len(into)):
        into[k].wait()
        onto[k].start()
    for copy in onto:
        copy.wait()


def column_pieces(grad, lists):
    slots = grad.shape[0]
    widths = [RING * len(nears) for nears, _ in lists]
    hbm = pl.BlockSpec(memory_space=pl.ANY)
    return pl.pallas_call(
        functools.partial(pieces_kernel, lists),
        out_shape=[jax.ShapeDtypeStruct((slots, width * HD), bf16) for width in widths],
        in_specs=[hbm],
        out_specs=[hbm] * len(lists),
        scratch_shapes=[
            pltpu.VMEM((sum(widths), slots, HD), bf16),
            pltpu.SemaphoreType.DMA((sum(widths),)),
            pltpu.SemaphoreType.DMA((sum(widths),)),
        ],
        compiler_params=pltpu.CompilerParams(vmem_limit_bytes=LARGER),
    )(grad)


def first_kernel(counts, latent, momentum, mine, lat, mom_own, mom_other, unit, own):
    core = lax.axis_index("c")
    slots, features = latent.shape
    depth, half = momentum.shape[0], momentum.shape[1] // NC
    live = lax.broadcasted_iota(jnp.int32, (slots, features), 0) < counts[0]
    lat[...] = jnp.where(live, latent[...], jnp.zeros_like(latent)).T
    for out, which in ((mom_own, core), (mom_other, 1 - core)):
        value = (DECAY / NZ) * momentum[:, pl.ds(pl.multiple_of(which * half, half), half)]
        high = value.astype(bf16)
        out[:depth, :] = high
        out[depth:, :] = (value - high.astype(f32)).astype(bf16)
    here = lax.axis_index("y") * NX + lax.axis_index("x")
    row = lax.broadcasted_iota(jnp.int32, unit.shape, 0)
    at = lax.broadcasted_iota(jnp.int32, unit.shape, 1)
    core_of = jnp.where(at < 2 * depth, core, 1 - core)
    unit[...] = (row == (here * NC + core_of) * depth + at % depth).astype(f32).astype(bf16)
    for far in range(RING):
        columns = mine[:, far * HD : (far + 1) * HD]
        own[far] = jnp.dot(lat[...], columns, preferred_element_type=f32).astype(bf16)


def first(counts, latent, momentum, mine):
    slots, features = latent.shape
    depth, columns = momentum.shape
    vmem = pl.BlockSpec(memory_space=pltpu.VMEM)
    mom = jax.ShapeDtypeStruct((2 * depth, columns // NC), bf16)
    return pl.pallas_call(
        first_kernel,
        out_shape=[
            jax.ShapeDtypeStruct((features, slots), bf16),
            mom,
            mom,
            jax.ShapeDtypeStruct((features, 4 * depth), bf16),
            jax.ShapeDtypeStruct((RING, features, HD), bf16),
        ],
        in_specs=[pl.BlockSpec(memory_space=pltpu.SMEM), vmem, vmem, vmem],
        compiler_params=pltpu.CompilerParams(vmem_limit_bytes=VMEM),
    )(counts, latent, momentum, mine)


def own_kernel(nears, lat, grad, *refs):
    outs, (held, sems) = refs[: len(nears)], refs[len(nears) :]
    copies = gather(grad, held, sems, nears, False)
    for copy in copies:
        copy.start()
    for near in range(len(nears)):
        for far in range(RING):
            copies[near * RING + far].wait()
        for far in range(RING):
            value = jnp.dot(lat[...], held[near * RING + far], preferred_element_type=f32)
            outs[near][far] = value.astype(bf16)


def own_products(lat, grad, nears):
    features, tokens = lat.shape
    count = RING * len(nears)
    vmem = pl.BlockSpec(memory_space=pltpu.VMEM)
    return pl.pallas_call(
        functools.partial(own_kernel, nears),
        out_shape=[jax.ShapeDtypeStruct((RING, features, HD), bf16)] * len(nears),
        in_specs=[vmem, pl.BlockSpec(memory_space=pl.ANY)],
        out_specs=[vmem] * len(nears),
        scratch_shapes=[
            pltpu.VMEM((count, tokens, HD), bf16),
            pltpu.SemaphoreType.DMA((count,)),
        ],
        compiler_params=pltpu.CompilerParams(vmem_limit_bytes=LARGE),
        cost_estimate=pl.CostEstimate(
            flops=2 * count * features * HD * tokens,
            bytes_accessed=count * (tokens + features) * HD * 2,
            transcendentals=0,
        ),
    )(lat, grad)


def block_kernel(tiles, unit, lat, mom_own, mom_other, grad, *refs):
    count = 1 + max(t[0] for t in tiles)
    operands, outs = refs[:count], refs[count:]
    for (operand, at_piece, near, fars, row), out in zip(tiles, outs):
        rows = slice(row, row + out.shape[1])
        for place, far in enumerate(fars):
            at = pl.ds(head_columns(near, far), HD)
            in_piece = (at_piece * RING + far) * HD
            mom = jnp.concatenate([mom_own[:, at], mom_other[:, at]], axis=0)
            other = jnp.dot(
                lat[rows, :], grad[:, in_piece : in_piece + HD], preferred_element_type=f32
            )
            added = jnp.dot(unit[rows, :], mom, preferred_element_type=f32)
            total = operands[operand][far, rows].astype(f32) + other.astype(bf16).astype(f32) + added
            out[place] = total.astype(out.dtype)


def block(own, held, which, unit, lat, mom_own, mom_other, grad):
    tokens = lat.shape[1]
    nears = sorted({w[0] for w in which})
    tiles = [(nears.index(w[0]), held.index(w[0]), *w[:3]) for w in which]
    work = sum(len(w[1]) * w[3] for w in which)
    return pl.pallas_call(
        functools.partial(block_kernel, tiles),
        out_shape=[jax.ShapeDtypeStruct((len(w[1]), w[3], HD), w[4]) for w in which],
        compiler_params=pltpu.CompilerParams(vmem_limit_bytes=VMEM),
        cost_estimate=pl.CostEstimate(
            flops=2 * work * HD * (tokens + unit.shape[1]),
            bytes_accessed=work * HD * 4 + len(which) * RING * tokens * HD * 2,
            transcendentals=0,
        ),
    )(unit, lat, mom_own, mom_other, grad, *[own[near] for near in nears])


def middle_kernel(kept, upper, lower, one, three, two_a, two_b, kept_out, one_out, three_out):
    half = upper.shape[1]
    for k in range(kept.shape[0]):
        kept_out[k, :half] = kept[k, :half] + upper[k].astype(f32)
        kept_out[k, half:] = kept[k, half:] + lower[k].astype(f32)
    one_out[:half, :] = one[0, :half].astype(bf16)
    one_out[half:, :] = (one[0, half:] + two_b[0].astype(f32)).astype(bf16)
    three_out[:half, :] = (three[0, :half] + two_a[0].astype(f32)).astype(bf16)
    three_out[half:, :] = three[0, half:].astype(bf16)


def middle(kept, *parts):
    stay = jax.ShapeDtypeStruct(kept.shape[1:], bf16)
    return pl.pallas_call(
        middle_kernel,
        out_shape=[jax.ShapeDtypeStruct(kept.shape, f32), stay, stay],
        compiler_params=pltpu.CompilerParams(vmem_limit_bytes=VMEM),
        cost_estimate=pl.CostEstimate(flops=MIDDLE, bytes_accessed=0, transcendentals=0),
    )(kept, *parts)


def stay_kernel(kept, one, three, out):
    out[...] = kept[0] + one[...].astype(f32) + three[...].astype(f32)


def stay_sum(kept, one, three):
    return pl.pallas_call(
        stay_kernel,
        out_shape=jax.ShapeDtypeStruct(kept.shape[1:], f32),
        compiler_params=pltpu.CompilerParams(vmem_limit_bytes=VMEM),
        cost_estimate=pl.CostEstimate(flops=MIDDLE, bytes_accessed=0, transcendentals=0),
    )(kept, one, three)


def add_kernel(kept, upper, lower, *outs):
    half = upper.shape[1]
    for k, out in enumerate(outs):
        out[:half, :] = (kept[k, :half] + upper[k].astype(f32)).astype(out.dtype)
        out[half:, :] = (kept[k, half:] + lower[k].astype(f32)).astype(out.dtype)


def add_up(kept, *parts):
    heads, rows, columns = kept.shape
    return pl.pallas_call(
        add_kernel,
        out_shape=[jax.ShapeDtypeStruct((rows, columns), bf16)] * heads,
        compiler_params=pltpu.CompilerParams(vmem_limit_bytes=VMEM),
    )(kept, *parts)


def split(value):
    high = value.astype(bf16)
    return high, (value - high.astype(f32)).astype(bf16)


def product(a, b, dims):
    (left,), (right,) = dims
    return lax.dot_general(
        jnp.concatenate([a[0], a[0], a[1]], axis=left),
        jnp.concatenate([b[0], b[1], b[0]], axis=right),
        (dims, ((), ())),
        preferred_element_type=f32,
    )


def newton_schulz_kernel(moment_ref, out_ref):
    moment = moment_ref[...]
    rows, columns = moment.shape
    scale = 0.2 * math.sqrt(max(rows, columns))
    wide = moment.T
    gram = lax.dot_general(wide, wide, (((1,), (1,)), ((), ())), preferred_element_type=f32)
    squares = wide.astype(f32) * wide.astype(f32)
    inverse = 1.0 / (jnp.sqrt(jnp.sum(squares)) + 1e-7)
    gram = (gram * inverse) * inverse
    at = [lax.broadcasted_iota(jnp.int32, gram.shape, axis) for axis in range(2)]
    identity = jnp.where(at[0] == at[1], COEF_A, 0.0)
    x = None
    for step in range(NS_STEPS):
        if step > 0:
            pair = split(x)
            gram = product(pair, pair, ((1,), (1,)))
        gram_pair = split(gram)
        poly = identity + COEF_B * gram + COEF_C * product(gram_pair, gram_pair, ((1,), (0,)))
        if step > 0:
            x = product(split(poly), pair, ((1,), (0,)))
        else:
            x = inverse * jnp.dot(
                jnp.concatenate(split(poly), axis=1),
                jnp.concatenate([wide, wide], axis=0),
                preferred_element_type=f32,
            )
    update = (scale * x).T.astype(bf16)
    owners = out_ref.shape[0]
    depth = rows // owners
    for c in range(NC):
        for chip in range(owners // NC):
            at = slice((chip * NC + c) * depth, (chip * NC + c + 1) * depth)
            out_ref[c * (owners // NC) + chip, 0] = update[at, :]
            out_ref[c * (owners // NC) + chip, 1] = moment[at, :]


def newton_schulz(moment, owners):
    rows, columns = moment.shape
    return pl.pallas_call(
        newton_schulz_kernel,
        out_shape=jax.ShapeDtypeStruct((owners, 2, rows // owners, columns), bf16),
        compiler_params=pltpu.CompilerParams(vmem_limit_bytes=VMEM),
    )(moment)


def spread_kernel(returned, moment, update, moment_held, update_held, sems):
    half = moment_held.shape[1] // NC
    copies = []
    for c in range(NC):
        for y in range(NY):
            for x in range(NX):
                source = (c * NY + y) * NX + x
                head = c * NY * NX + (RING * x + y if c == 0 else RING * y + x)
                at = slice(head * HD, (head + 1) * HD)
                update_held[:, at] = returned[source, 0]
                moment_held[:, at] = returned[source, 1].astype(f32)
        done = pl.ds(c * half, half)
        for k, (held, out) in enumerate(((moment_held, moment), (update_held, update))):
            copies.append(pltpu.make_async_copy(held.at[:, done], out.at[:, done], sems.at[c, k]))
            copies[-1].start()
    for copy in copies:
        copy.wait()


def spread(returned):
    heads, _, rows, columns = returned.shape
    moment = jax.ShapeDtypeStruct((rows, heads * columns), f32)
    update = jax.ShapeDtypeStruct((rows, heads * columns), bf16)
    hbm = pl.BlockSpec(memory_space=pl.ANY)
    return pl.pallas_call(
        spread_kernel,
        out_shape=(moment, update),
        in_specs=[pl.BlockSpec(memory_space=pltpu.VMEM)],
        out_specs=(hbm, hbm),
        scratch_shapes=[
            pltpu.VMEM(moment.shape, f32),
            pltpu.VMEM(update.shape, bf16),
            pltpu.SemaphoreType.DMA((NC, 2)),
        ],
        compiler_params=pltpu.CompilerParams(vmem_limit_bytes=VMEM),
    )(returned)


def body(latent, latent_grad, row_counts, momentum):
    features = latent.shape[1]
    order = (1, 3, 2)
    tie = lax.optimization_barrier

    early, late = (2,), (1, 3, 0)
    piece_early, mine = column_pieces(latent_grad, [(early, True), (early, False)])
    lat_own, mom_own, mom_other, unit, own_early = first(row_counts, latent, momentum, mine)
    grad_late, own_early = tie((latent_grad, own_early))
    (piece_late,) = column_pieces(grad_late, [(late, True)])
    piece_early, lat_other, mom_other = (
        swap_cores(piece_early), swap_cores(lat_own), swap_cores(mom_other)
    )
    piece_late, piece_early, lat_other, mom_other = tie((piece_late, piece_early, lat_other, mom_other))
    piece_late = swap_cores(piece_late)
    shared = (unit, lat_other, mom_own, mom_other)

    half = features // 2
    upper, lower, whole = (0, half), (half, half), (0, features)
    every, rest, stay = (0, 1, 2, 3), (1, 2, 3), (0,)
    own = {2: own_early}
    two_a, two_b = block(
        own, early, [(2, every, *upper, bf16), (2, every, *lower, bf16)], *shared, piece_early
    )
    lat_late, two_a, two_b = tie((lat_own, two_a, two_b))
    own[1], own[3] = own_products(lat_late, grad_late, late[:2])
    (one_a,) = block(own, late, [(1, rest, *upper, bf16)], *shared, piece_late)
    (three_b,) = block(own, late, [(3, rest, *lower, bf16)], *shared, piece_late)
    own[1], own[3], one_a, three_b = tie((own[1], own[3], one_a, three_b))
    one_b, three_a = block(
        own, late, [(1, rest, *lower, f32), (3, rest, *upper, f32)], *shared, piece_late
    )
    two_a, two_b = exchange(two_a, 0, 1), exchange(two_b, 0, 3)
    one_a, three_b = exchange(one_a, 0, 1), exchange(three_b, 0, 3)
    three_a = (three_a + two_a[1:].astype(f32)).astype(bf16)
    one_b = (one_b + two_b[1:].astype(f32)).astype(bf16)
    lat_last, own[1], one_b = tie((lat_late, own[1], one_b))
    three_a, one_b = exchange(three_a, 0, 3), exchange(one_b, 0, 1)
    (own[0],) = own_products(lat_last, grad_late, late[2:])
    one_stay, three_stay, kept_on, kept_stay = block(
        own,
        late,
        [
            (1, stay, *whole, f32),
            (3, stay, *whole, f32),
            (0, rest, *whole, f32),
            (0, stay, *whole, f32),
        ],
        *shared,
        piece_late,
    )
    kept_on, one_stay, three_stay = middle(
        kept_on, one_a, three_b, one_stay, three_stay, two_a, two_b
    )
    one_stay, three_stay = exchange(one_stay, 0, 1), exchange(three_stay, 0, 3)

    sums = add_up(kept_on, three_a, one_b)
    got = [exchange(sums[k - 1], 1, k) for k in order]
    head = stay_sum(kept_stay, one_stay, three_stay)
    head = (head + sum(value.astype(f32) for value in got)).astype(bf16)

    pieces = lax.all_to_all(head.reshape(NZ, -1, HD), "z", 0, 0, tiled=True)
    piece = jnp.sum(pieces.astype(f32), axis=0).astype(bf16)
    moment = lax.all_to_all(jnp.broadcast_to(piece, (NZ,) + piece.shape), "z", 0, 0, tiled=True)
    moment = moment.reshape(features, HD)

    outgoing = newton_schulz(moment, NC * NY * NX)
    returned = lax.all_to_all(outgoing, PLANE, 0, 0, tiled=True)
    return tuple(spread(returned))


def solution(mesh):
    fine = Mesh(mesh.devices.reshape(NZ, NY, NX, NC), AXES)
    shard = ("y", "x", "c")
    in_specs = (P(AXES, None), P(AXES, None), P(AXES), P(shard, None))
    out_specs = (P(shard, None), P(shard, None))
    return jax.shard_map(body, mesh=fine, in_specs=in_specs, out_specs=out_specs, check_vma=False)
```

```python
import functools
import math

import jax
import jax.numpy as jnp
from jax import lax
from jax.experimental import pallas as pl
from jax.experimental.pallas import tpu as pltpu
from jax.sharding import Mesh
from jax.sharding import PartitionSpec as P

HD = 256
NS_STEPS = 5
NZ, NY, NX, NC = 8, 4, 4, 2
RING = 4
AXES = ("z", "y", "x", "c")
PLANE = ("c", "y", "x")
COEF_A, COEF_B, COEF_C = 3.4445, -4.775, 2.0315
DECAY = 0.95
VMEM = 16 * 1024 * 1024
MIDDLE = 5 * 10**9
LARGE = 48 * 1024 * 1024
LARGER = 52 * 1024 * 1024
bf16, f32 = jnp.bfloat16, jnp.float32


def device_at(z, y, x, c):
    return ((z * NY + y) * NX + x) * NC + c


def every_device():
    return [(z, y, x, c) for z in range(NZ) for y in range(NY) for x in range(NX) for c in range(NC)]


def exchange(value, axis, distance):
    pairs = []
    for z, y, x, c in every_device():
        if axis == c:
            to = (y, x ^ distance)
        else:
            to = (y ^ distance, x)
        pairs.append((device_at(z, y, x, c), device_at(z, *to, c)))
    return lax.ppermute(value, AXES, pairs)


def swap_cores(value):
    return lax.ppermute(
        value, AXES, [(device_at(z, y, x, c), device_at(z, y, x, 1 - c)) for z, y, x, c in every_device()]
    )


def places():
    core, y, x = lax.axis_index("c"), lax.axis_index("y"), lax.axis_index("x")
    return jnp.where(core == 0, x, y), jnp.where(core == 0, y, x)


def head_columns(near, far, other=False):
    first, second = places()
    if other:
        first, second = second, first
    head = (first ^ near) * RING + (second ^ far)
    return pl.multiple_of(head * HD, HD)


def gather(grad, held, sems, nears, other):
    core = lax.axis_index("c")
    base = (1 - core if other else core) * (grad.shape[1] // NC)
    copies = []
    for near in nears:
        for far in range(RING):
            k = len(copies)
            start = pl.multiple_of(base + head_columns(near, far, other), HD)
            copies.append(
                pltpu.make_async_copy(grad.at[:, pl.ds(start, HD)], held.at[k], sems.at[k])
            )
    return copies


def pieces_kernel(lists, grad, *refs):
    outs, (held, sems_in, sems_out) = refs[: len(lists)], refs[len(lists) :]
    into, onto = [], []
    for (nears, other), out in zip(lists, outs):
        at = len(into)
        count = RING * len(nears)
        into += gather(grad, held.at[pl.ds(at, count)], sems_in.at[pl.ds(at, count)], nears, other)
        for k in range(count):
            onto.append(
                pltpu.make_async_copy(
                    held.at[at + k], out.at[:, k * HD : (k + 1) * HD], sems_out.at[at + k]
                )
            )
    for copy in into:
        copy.start()
    for k in range(len(into)):
        into[k].wait()
        onto[k].start()
    for copy in onto:
        copy.wait()


def column_pieces(grad, lists):
    slots = grad.shape[0]
    widths = [RING * len(nears) for nears, _ in lists]
    hbm = pl.BlockSpec(memory_space=pl.ANY)
    return pl.pallas_call(
        functools.partial(pieces_kernel, lists),
        out_shape=[jax.ShapeDtypeStruct((slots, width * HD), bf16) for width in widths],
        in_specs=[hbm],
        out_specs=[hbm] * len(lists),
        scratch_shapes=[
            pltpu.VMEM((sum(widths), slots, HD), bf16),
            pltpu.SemaphoreType.DMA((sum(widths),)),
            pltpu.SemaphoreType.DMA((sum(widths),)),
        ],
        compiler_params=pltpu.CompilerParams(vmem_limit_bytes=LARGER),
    )(grad)


def first_kernel(counts, latent, momentum, mine, lat, mom_own, mom_other, unit, own):
    core = lax.axis_index("c")
    slots, features = latent.shape
    depth, half = momentum.shape[0], momentum.shape[1] // NC
    live = lax.broadcasted_iota(jnp.int32, (slots, features), 0) < counts[0]
    lat[...] = jnp.where(live, latent[...], jnp.zeros_like(latent)).T
    for out, which in ((mom_own, core), (mom_other, 1 - core)):
        value = (DECAY / NZ) * momentum[:, pl.ds(pl.multiple_of(which * half, half), half)]
        high = value.astype(bf16)
        out[:depth, :] = high
        out[depth:, :] = (value - high.astype(f32)).astype(bf16)
    here = lax.axis_index("y") * NX + lax.axis_index("x")
    row = lax.broadcasted_iota(jnp.int32, unit.shape, 0)
    at = lax.broadcasted_iota(jnp.int32, unit.shape, 1)
    core_of = jnp.where(at < 2 * depth, core, 1 - core)
    unit[...] = (row == (here * NC + core_of) * depth + at % depth).astype(f32).astype(bf16)
    for far in range(RING):
        columns = mine[:, far * HD : (far + 1) * HD]
        own[far] = jnp.dot(lat[...], columns, preferred_element_type=f32).astype(bf16)


def first(counts, latent, momentum, mine):
    slots, features = latent.shape
    depth, columns = momentum.shape
    vmem = pl.BlockSpec(memory_space=pltpu.VMEM)
    mom = jax.ShapeDtypeStruct((2 * depth, columns // NC), bf16)
    return pl.pallas_call(
        first_kernel,
        out_shape=[
            jax.ShapeDtypeStruct((features, slots), bf16),
            mom,
            mom,
            jax.ShapeDtypeStruct((features, 4 * depth), bf16),
            jax.ShapeDtypeStruct((RING, features, HD), bf16),
        ],
        in_specs=[pl.BlockSpec(memory_space=pltpu.SMEM), vmem, vmem, vmem],
        compiler_params=pltpu.CompilerParams(vmem_limit_bytes=VMEM),
    )(counts, latent, momentum, mine)


def own_kernel(nears, lat, grad, *refs):
    outs, (held, sems) = refs[: len(nears)], refs[len(nears) :]
    copies = gather(grad, held, sems, nears, False)
    for copy in copies:
        copy.start()
    for near in range(len(nears)):
        for far in range(RING):
            copies[near * RING + far].wait()
        for far in range(RING):
            value = jnp.dot(lat[...], held[near * RING + far], preferred_element_type=f32)
            outs[near][far] = value.astype(bf16)


def own_products(lat, grad, nears):
    features, tokens = lat.shape
    count = RING * len(nears)
    vmem = pl.BlockSpec(memory_space=pltpu.VMEM)
    return pl.pallas_call(
        functools.partial(own_kernel, nears),
        out_shape=[jax.ShapeDtypeStruct((RING, features, HD), bf16)] * len(nears),
        in_specs=[vmem, pl.BlockSpec(memory_space=pl.ANY)],
        out_specs=[vmem] * len(nears),
        scratch_shapes=[
            pltpu.VMEM((count, tokens, HD), bf16),
            pltpu.SemaphoreType.DMA((count,)),
        ],
        compiler_params=pltpu.CompilerParams(vmem_limit_bytes=LARGE),
        cost_estimate=pl.CostEstimate(
            flops=2 * count * features * HD * tokens,
            bytes_accessed=count * (tokens + features) * HD * 2,
            transcendentals=0,
        ),
    )(lat, grad)


def block_kernel(tiles, unit, lat, mom_own, mom_other, grad, *refs):
    count = 1 + max(t[0] for t in tiles)
    operands, outs = refs[:count], refs[count:]
    for (operand, at_piece, near, fars, row), out in zip(tiles, outs):
        rows = slice(row, row + out.shape[1])
        for place, far in enumerate(fars):
            at = pl.ds(head_columns(near, far), HD)
            in_piece = (at_piece * RING + far) * HD
            mom = jnp.concatenate([mom_own[:, at], mom_other[:, at]], axis=0)
            other = jnp.dot(
                lat[rows, :], grad[:, in_piece : in_piece + HD], preferred_element_type=f32
            )
            added = jnp.dot(unit[rows, :], mom, preferred_element_type=f32)
            total = operands[operand][far, rows].astype(f32) + other.astype(bf16).astype(f32) + added
            out[place] = total.astype(out.dtype)


def block(own, held, which, unit, lat, mom_own, mom_other, grad):
    tokens = lat.shape[1]
    nears = sorted({w[0] for w in which})
    tiles = [(nears.index(w[0]), held.index(w[0]), *w[:3]) for w in which]
    work = sum(len(w[1]) * w[3] for w in which)
    return pl.pallas_call(
        functools.partial(block_kernel, tiles),
        out_shape=[jax.ShapeDtypeStruct((len(w[1]), w[3], HD), w[4]) for w in which],
        compiler_params=pltpu.CompilerParams(vmem_limit_bytes=VMEM),
        cost_estimate=pl.CostEstimate(
            flops=2 * work * HD * (tokens + unit.shape[1]),
            bytes_accessed=work * HD * 4 + len(which) * RING * tokens * HD * 2,
            transcendentals=0,
        ),
    )(unit, lat, mom_own, mom_other, grad, *[own[near] for near in nears])


def middle_kernel(kept, upper, lower, one, three, two_a, two_b, kept_out, one_out, three_out):
    half = upper.shape[1]
    for k in range(kept.shape[0]):
        kept_out[k, :half] = kept[k, :half] + upper[k].astype(f32)
        kept_out[k, half:] = kept[k, half:] + lower[k].astype(f32)
    one_out[:half, :] = one[0, :half].astype(bf16)
    one_out[half:, :] = (one[0, half:] + two_b[0].astype(f32)).astype(bf16)
    three_out[:half, :] = (three[0, :half] + two_a[0].astype(f32)).astype(bf16)
    three_out[half:, :] = three[0, half:].astype(bf16)


def middle(kept, *parts):
    stay = jax.ShapeDtypeStruct(kept.shape[1:], bf16)
    return pl.pallas_call(
        middle_kernel,
        out_shape=[jax.ShapeDtypeStruct(kept.shape, f32), stay, stay],
        compiler_params=pltpu.CompilerParams(vmem_limit_bytes=VMEM),
        cost_estimate=pl.CostEstimate(flops=MIDDLE, bytes_accessed=0, transcendentals=0),
    )(kept, *parts)


def stay_kernel(kept, one, three, out):
    out[...] = kept[0] + one[...].astype(f32) + three[...].astype(f32)


def stay_sum(kept, one, three):
    return pl.pallas_call(
        stay_kernel,
        out_shape=jax.ShapeDtypeStruct(kept.shape[1:], f32),
        compiler_params=pltpu.CompilerParams(vmem_limit_bytes=VMEM),
        cost_estimate=pl.CostEstimate(flops=MIDDLE, bytes_accessed=0, transcendentals=0),
    )(kept, one, three)


def add_kernel(kept, upper, lower, *outs):
    half = upper.shape[1]
    for k, out in enumerate(outs):
        out[:half, :] = (kept[k, :half] + upper[k].astype(f32)).astype(out.dtype)
        out[half:, :] = (kept[k, half:] + lower[k].astype(f32)).astype(out.dtype)


def add_up(kept, *parts):
    heads, rows, columns = kept.shape
    return pl.pallas_call(
        add_kernel,
        out_shape=[jax.ShapeDtypeStruct((rows, columns), bf16)] * heads,
        compiler_params=pltpu.CompilerParams(vmem_limit_bytes=VMEM),
    )(kept, *parts)


def split(value):
    high = value.astype(bf16)
    return high, (value - high.astype(f32)).astype(bf16)


def product(a, b, dims):
    (left,), (right,) = dims
    return lax.dot_general(
        jnp.concatenate([a[0], a[0], a[1]], axis=left),
        jnp.concatenate([b[0], b[1], b[0]], axis=right),
        (dims, ((), ())),
        preferred_element_type=f32,
    )


def newton_schulz_kernel(moment_ref, out_ref):
    moment = moment_ref[...]
    rows, columns = moment.shape
    scale = 0.2 * math.sqrt(max(rows, columns))
    wide = moment.T
    gram = lax.dot_general(wide, wide, (((1,), (1,)), ((), ())), preferred_element_type=f32)
    squares = wide.astype(f32) * wide.astype(f32)
    inverse = 1.0 / (jnp.sqrt(jnp.sum(squares)) + 1e-7)
    gram = (gram * inverse) * inverse
    at = [lax.broadcasted_iota(jnp.int32, gram.shape, axis) for axis in range(2)]
    identity = jnp.where(at[0] == at[1], COEF_A, 0.0)
    x = None
    for step in range(NS_STEPS):
        if step > 0:
            pair = split(x)
            gram = product(pair, pair, ((1,), (1,)))
        gram_pair = split(gram)
        poly = identity + COEF_B * gram + COEF_C * product(gram_pair, gram_pair, ((1,), (0,)))
        if step > 0:
            x = product(split(poly), pair, ((1,), (0,)))
        else:
            x = inverse * jnp.dot(
                jnp.concatenate(split(poly), axis=1),
                jnp.concatenate([wide, wide], axis=0),
                preferred_element_type=f32,
            )
    update = (scale * x).T.astype(bf16)
    owners = out_ref.shape[0]
    depth = rows // owners
    for c in range(NC):
        for chip in range(owners // NC):
            at = slice((chip * NC + c) * depth, (chip * NC + c + 1) * depth)
            out_ref[c * (owners // NC) + chip, 0] = update[at, :]
            out_ref[c * (owners // NC) + chip, 1] = moment[at, :]


def newton_schulz(moment, owners):
    rows, columns = moment.shape
    return pl.pallas_call(
        newton_schulz_kernel,
        out_shape=jax.ShapeDtypeStruct((owners, 2, rows // owners, columns), bf16),
        compiler_params=pltpu.CompilerParams(vmem_limit_bytes=VMEM),
    )(moment)


def spread_kernel(returned, moment, update, moment_held, update_held, sems):
    half = moment_held.shape[1] // NC
    copies = []
    for c in range(NC):
        for y in range(NY):
            for x in range(NX):
                source = (c * NY + y) * NX + x
                head = c * NY * NX + (RING * x + y if c == 0 else RING * y + x)
                at = slice(head * HD, (head + 1) * HD)
                update_held[:, at] = returned[source, 0]
                moment_held[:, at] = returned[source, 1].astype(f32)
        done = pl.ds(c * half, half)
        for k, (held, out) in enumerate(((moment_held, moment), (update_held, update))):
            copies.append(pltpu.make_async_copy(held.at[:, done], out.at[:, done], sems.at[c, k]))
            copies[-1].start()
    for copy in copies:
        copy.wait()


def spread(returned):
    heads, _, rows, columns = returned.shape
    moment = jax.ShapeDtypeStruct((rows, heads * columns), f32)
    update = jax.ShapeDtypeStruct((rows, heads * columns), bf16)
    hbm = pl.BlockSpec(memory_space=pl.ANY)
    return pl.pallas_call(
        spread_kernel,
        out_shape=(moment, update),
        in_specs=[pl.BlockSpec(memory_space=pltpu.VMEM)],
        out_specs=(hbm, hbm),
        scratch_shapes=[
            pltpu.VMEM(moment.shape, f32),
            pltpu.VMEM(update.shape, bf16),
            pltpu.SemaphoreType.DMA((NC, 2)),
        ],
        compiler_params=pltpu.CompilerParams(vmem_limit_bytes=VMEM),
    )(returned)


def body(latent, latent_grad, row_counts, momentum):
    features = latent.shape[1]
    order = (2, 1, 3)
    tie = lax.optimization_barrier

    early, late = (2,), (1, 3, 0)
    piece_early, mine = column_pieces(latent_grad, [(early, True), (early, False)])
    lat_own, mom_own, mom_other, unit, own_early = first(row_counts, latent, momentum, mine)
    grad_late, own_early = tie((latent_grad, own_early))
    (piece_late,) = column_pieces(grad_late, [(late, True)])
    piece_early, lat_other, mom_other = (
        swap_cores(piece_early), swap_cores(lat_own), swap_cores(mom_other)
    )
    piece_late, piece_early, lat_other, mom_other = tie((piece_late, piece_early, lat_other, mom_other))
    piece_late = swap_cores(piece_late)
    shared = (unit, lat_other, mom_own, mom_other)

    half = features // 2
    upper, lower, whole = (0, half), (half, half), (0, features)
    every, rest, stay = (0, 1, 2, 3), (1, 2, 3), (0,)
    own = {2: own_early}
    two_a, two_b = block(
        own, early, [(2, every, *upper, bf16), (2, every, *lower, bf16)], *shared, piece_early
    )
    lat_late, two_a, two_b = tie((lat_own, two_a, two_b))
    own[1], own[3], own[0] = own_products(lat_late, latent_grad, late)
    (one_a,) = block(own, late, [(1, rest, *upper, bf16)], *shared, piece_late)
    (three_b,) = block(own, late, [(3, rest, *lower, bf16)], *shared, piece_late)
    own[0], one_a, three_b = tie((own[0], one_a, three_b))
    one_b, three_a, one_stay, three_stay, kept_on, kept_stay = block(
        own,
        late,
        [
            (1, rest, *lower, f32),
            (3, rest, *upper, f32),
            (1, stay, *whole, f32),
            (3, stay, *whole, f32),
            (0, rest, *whole, f32),
            (0, stay, *whole, f32),
        ],
        *shared,
        piece_late,
    )
    two_a, two_b = exchange(two_a, 0, 1), exchange(two_b, 0, 3)
    one_a, three_b = exchange(one_a, 0, 1), exchange(three_b, 0, 3)
    three_a = exchange((three_a + two_a[1:].astype(f32)).astype(bf16), 0, 3)
    one_b = exchange((one_b + two_b[1:].astype(f32)).astype(bf16), 0, 1)
    kept_on, one_stay, three_stay = middle(
        kept_on, one_a, three_b, one_stay, three_stay, two_a, two_b
    )
    one_stay, three_stay = exchange(one_stay, 0, 1), exchange(three_stay, 0, 3)

    sums = add_up(kept_on, three_a, one_b)
    got = [exchange(sums[k - 1], 1, k) for k in order]
    head = stay_sum(kept_stay, one_stay, three_stay)
    head = (head + sum(value.astype(f32) for value in got)).astype(bf16)

    pieces = lax.all_to_all(head.reshape(NZ, -1, HD), "z", 0, 0, tiled=True)
    piece = jnp.sum(pieces.astype(f32), axis=0).astype(bf16)
    moment = lax.all_to_all(jnp.broadcast_to(piece, (NZ,) + piece.shape), "z", 0, 0, tiled=True)
    moment = moment.reshape(features, HD)

    outgoing = newton_schulz(moment, NC * NY * NX)
    returned = lax.all_to_all(outgoing, PLANE, 0, 0, tiled=True)
    return tuple(spread(returned))


def solution(mesh):
    fine = Mesh(mesh.devices.reshape(NZ, NY, NX, NC), AXES)
    shard = ("y", "x", "c")
    in_specs = (P(AXES, None), P(AXES, None), P(AXES), P(shard, None))
    out_specs = (P(shard, None), P(shard, None))
    return jax.shard_map(body, mesh=fine, in_specs=in_specs, out_specs=out_specs, check_vma=False)
```

```python
import functools
import math

import jax
import jax.numpy as jnp
from jax import lax
from jax.experimental import pallas as pl
from jax.experimental.pallas import tpu as pltpu
from jax.sharding import Mesh
from jax.sharding import PartitionSpec as P

HD = 256
NS_STEPS = 5
NZ, NY, NX, NC = 8, 4, 4, 2
RING = 4
AXES = ("z", "y", "x", "c")
PLANE = ("c", "y", "x")
COEF_A, COEF_B, COEF_C = 3.4445, -4.775, 2.0315
DECAY = 0.95
VMEM = 16 * 1024 * 1024
MIDDLE = 5 * 10**9
LARGE = 48 * 1024 * 1024
LARGER = 52 * 1024 * 1024
bf16, f32 = jnp.bfloat16, jnp.float32


def device_at(z, y, x, c):
    return ((z * NY + y) * NX + x) * NC + c


def every_device():
    return [(z, y, x, c) for z in range(NZ) for y in range(NY) for x in range(NX) for c in range(NC)]


def exchange(value, axis, distance):
    pairs = []
    for z, y, x, c in every_device():
        if axis == c:
            to = (y, x ^ distance)
        else:
            to = (y ^ distance, x)
        pairs.append((device_at(z, y, x, c), device_at(z, *to, c)))
    return lax.ppermute(value, AXES, pairs)


def swap_cores(value):
    return lax.ppermute(
        value, AXES, [(device_at(z, y, x, c), device_at(z, y, x, 1 - c)) for z, y, x, c in every_device()]
    )


def places():
    core, y, x = lax.axis_index("c"), lax.axis_index("y"), lax.axis_index("x")
    return jnp.where(core == 0, x, y), jnp.where(core == 0, y, x)


def head_columns(near, far, other=False):
    first, second = places()
    if other:
        first, second = second, first
    head = (first ^ near) * RING + (second ^ far)
    return pl.multiple_of(head * HD, HD)


def gather(grad, held, sems, nears, other):
    core = lax.axis_index("c")
    base = (1 - core if other else core) * (grad.shape[1] // NC)
    copies = []
    for near in nears:
        for far in range(RING):
            k = len(copies)
            start = pl.multiple_of(base + head_columns(near, far, other), HD)
            copies.append(
                pltpu.make_async_copy(grad.at[:, pl.ds(start, HD)], held.at[k], sems.at[k])
            )
    return copies


def pieces_kernel(lists, grad, *refs):
    outs, (held, sems_in, sems_out) = refs[: len(lists)], refs[len(lists) :]
    into, onto = [], []
    for (nears, other), out in zip(lists, outs):
        at = len(into)
        count = RING * len(nears)
        into += gather(grad, held.at[pl.ds(at, count)], sems_in.at[pl.ds(at, count)], nears, other)
        for k in range(count):
            onto.append(
                pltpu.make_async_copy(
                    held.at[at + k], out.at[:, k * HD : (k + 1) * HD], sems_out.at[at + k]
                )
            )
    for copy in into:
        copy.start()
    for k in range(len(into)):
        into[k].wait()
        onto[k].start()
    for copy in onto:
        copy.wait()


def column_pieces(grad, lists):
    slots = grad.shape[0]
    widths = [RING * len(nears) for nears, _ in lists]
    hbm = pl.BlockSpec(memory_space=pl.ANY)
    return pl.pallas_call(
        functools.partial(pieces_kernel, lists),
        out_shape=[jax.ShapeDtypeStruct((slots, width * HD), bf16) for width in widths],
        in_specs=[hbm],
        out_specs=[hbm] * len(lists),
        scratch_shapes=[
            pltpu.VMEM((sum(widths), slots, HD), bf16),
            pltpu.SemaphoreType.DMA((sum(widths),)),
            pltpu.SemaphoreType.DMA((sum(widths),)),
        ],
        compiler_params=pltpu.CompilerParams(vmem_limit_bytes=LARGER),
    )(grad)


def first_kernel(counts, latent, momentum, mine, lat, mom_own, mom_other, unit, own):
    core = lax.axis_index("c")
    slots, features = latent.shape
    depth, half = momentum.shape[0], momentum.shape[1] // NC
    live = lax.broadcasted_iota(jnp.int32, (slots, features), 0) < counts[0]
    lat[...] = jnp.where(live, latent[...], jnp.zeros_like(latent)).T
    for out, which in ((mom_own, core), (mom_other, 1 - core)):
        value = (DECAY / NZ) * momentum[:, pl.ds(pl.multiple_of(which * half, half), half)]
        high = value.astype(bf16)
        out[:depth, :] = high
        out[depth:, :] = (value - high.astype(f32)).astype(bf16)
    here = lax.axis_index("y") * NX + lax.axis_index("x")
    row = lax.broadcasted_iota(jnp.int32, unit.shape, 0)
    at = lax.broadcasted_iota(jnp.int32, unit.shape, 1)
    core_of = jnp.where(at < 2 * depth, core, 1 - core)
    unit[...] = (row == (here * NC + core_of) * depth + at % depth).astype(f32).astype(bf16)
    for far in range(RING):
        columns = mine[:, far * HD : (far + 1) * HD]
        own[far] = jnp.dot(lat[...], columns, preferred_element_type=f32).astype(bf16)


def first(counts, latent, momentum, mine):
    slots, features = latent.shape
    depth, columns = momentum.shape
    vmem = pl.BlockSpec(memory_space=pltpu.VMEM)
    mom = jax.ShapeDtypeStruct((2 * depth, columns // NC), bf16)
    return pl.pallas_call(
        first_kernel,
        out_shape=[
            jax.ShapeDtypeStruct((features, slots), bf16),
            mom,
            mom,
            jax.ShapeDtypeStruct((features, 4 * depth), bf16),
            jax.ShapeDtypeStruct((RING, features, HD), bf16),
        ],
        in_specs=[pl.BlockSpec(memory_space=pltpu.SMEM), vmem, vmem, vmem],
        compiler_params=pltpu.CompilerParams(vmem_limit_bytes=VMEM),
    )(counts, latent, momentum, mine)


def own_kernel(nears, lat, grad, *refs):
    outs, (held, sems) = refs[: len(nears)], refs[len(nears) :]
    copies = gather(grad, held, sems, nears, False)
    for copy in copies:
        copy.start()
    for near in range(len(nears)):
        for far in range(RING):
            copies[near * RING + far].wait()
        for far in range(RING):
            value = jnp.dot(lat[...], held[near * RING + far], preferred_element_type=f32)
            outs[near][far] = value.astype(bf16)


def own_products(lat, grad, nears):
    features, tokens = lat.shape
    count = RING * len(nears)
    vmem = pl.BlockSpec(memory_space=pltpu.VMEM)
    return pl.pallas_call(
        functools.partial(own_kernel, nears),
        out_shape=[jax.ShapeDtypeStruct((RING, features, HD), bf16)] * len(nears),
        in_specs=[vmem, pl.BlockSpec(memory_space=pl.ANY)],
        out_specs=[vmem] * len(nears),
        scratch_shapes=[
            pltpu.VMEM((count, tokens, HD), bf16),
            pltpu.SemaphoreType.DMA((count,)),
        ],
        compiler_params=pltpu.CompilerParams(vmem_limit_bytes=LARGE),
        cost_estimate=pl.CostEstimate(
            flops=2 * count * features * HD * tokens,
            bytes_accessed=count * (tokens + features) * HD * 2,
            transcendentals=0,
        ),
    )(lat, grad)


def block_kernel(tiles, unit, lat, mom_own, mom_other, grad, *refs):
    count = 1 + max(t[0] for t in tiles)
    operands, outs = refs[:count], refs[count:]
    for (operand, at_piece, near, fars, row), out in zip(tiles, outs):
        rows = slice(row, row + out.shape[1])
        for place, far in enumerate(fars):
            at = pl.ds(head_columns(near, far), HD)
            in_piece = (at_piece * RING + far) * HD
            mom = jnp.concatenate([mom_own[:, at], mom_other[:, at]], axis=0)
            other = jnp.dot(
                lat[rows, :], grad[:, in_piece : in_piece + HD], preferred_element_type=f32
            )
            added = jnp.dot(unit[rows, :], mom, preferred_element_type=f32)
            total = operands[operand][far, rows].astype(f32) + other.astype(bf16).astype(f32) + added
            out[place] = total.astype(out.dtype)


def block(own, held, which, unit, lat, mom_own, mom_other, grad):
    tokens = lat.shape[1]
    nears = sorted({w[0] for w in which})
    tiles = [(nears.index(w[0]), held.index(w[0]), *w[:3]) for w in which]
    work = sum(len(w[1]) * w[3] for w in which)
    return pl.pallas_call(
        functools.partial(block_kernel, tiles),
        out_shape=[jax.ShapeDtypeStruct((len(w[1]), w[3], HD), w[4]) for w in which],
        compiler_params=pltpu.CompilerParams(vmem_limit_bytes=VMEM),
        cost_estimate=pl.CostEstimate(
            flops=2 * work * HD * (tokens + unit.shape[1]),
            bytes_accessed=work * HD * 4 + len(which) * RING * tokens * HD * 2,
            transcendentals=0,
        ),
    )(unit, lat, mom_own, mom_other, grad, *[own[near] for near in nears])


def middle_kernel(kept, upper, lower, one, three, two_a, two_b, kept_out, one_out, three_out):
    half = upper.shape[1]
    for k in range(kept.shape[0]):
        kept_out[k, :half] = kept[k, :half] + upper[k].astype(f32)
        kept_out[k, half:] = kept[k, half:] + lower[k].astype(f32)
    one_out[:half, :] = one[0, :half].astype(bf16)
    one_out[half:, :] = (one[0, half:] + two_b[0].astype(f32)).astype(bf16)
    three_out[:half, :] = (three[0, :half] + two_a[0].astype(f32)).astype(bf16)
    three_out[half:, :] = three[0, half:].astype(bf16)


def middle(kept, *parts):
    stay = jax.ShapeDtypeStruct(kept.shape[1:], bf16)
    return pl.pallas_call(
        middle_kernel,
        out_shape=[jax.ShapeDtypeStruct(kept.shape, f32), stay, stay],
        compiler_params=pltpu.CompilerParams(vmem_limit_bytes=VMEM),
        cost_estimate=pl.CostEstimate(flops=MIDDLE, bytes_accessed=0, transcendentals=0),
    )(kept, *parts)


def stay_kernel(kept, one, three, out):
    out[...] = kept[0] + one[...].astype(f32) + three[...].astype(f32)


def stay_sum(kept, one, three):
    return pl.pallas_call(
        stay_kernel,
        out_shape=jax.ShapeDtypeStruct(kept.shape[1:], f32),
        compiler_params=pltpu.CompilerParams(vmem_limit_bytes=VMEM),
        cost_estimate=pl.CostEstimate(flops=MIDDLE, bytes_accessed=0, transcendentals=0),
    )(kept, one, three)


def add_kernel(kept, upper, lower, *outs):
    half = upper.shape[1]
    for k, out in enumerate(outs):
        out[:half, :] = (kept[k, :half] + upper[k].astype(f32)).astype(out.dtype)
        out[half:, :] = (kept[k, half:] + lower[k].astype(f32)).astype(out.dtype)


def add_up(kept, *parts):
    heads, rows, columns = kept.shape
    return pl.pallas_call(
        add_kernel,
        out_shape=[jax.ShapeDtypeStruct((rows, columns), bf16)] * heads,
        compiler_params=pltpu.CompilerParams(vmem_limit_bytes=VMEM),
    )(kept, *parts)


def split(value):
    high = value.astype(bf16)
    return high, (value - high.astype(f32)).astype(bf16)


def product(a, b, dims):
    (left,), (right,) = dims
    return lax.dot_general(
        jnp.concatenate([a[0], a[0], a[1]], axis=left),
        jnp.concatenate([b[0], b[1], b[0]], axis=right),
        (dims, ((), ())),
        preferred_element_type=f32,
    )


def newton_schulz_kernel(moment_ref, out_ref):
    moment = moment_ref[...]
    rows, columns = moment.shape
    scale = 0.2 * math.sqrt(max(rows, columns))
    wide = moment.T
    gram = lax.dot_general(wide, wide, (((1,), (1,)), ((), ())), preferred_element_type=f32)
    wide = wide.astype(f32)
    inverse = 1.0 / (jnp.sqrt(jnp.sum(wide * wide)) + 1e-7)
    gram = (gram * inverse) * inverse
    x = wide * inverse
    for step in range(NS_STEPS):
        pair = split(x)
        if step > 0:
            gram = product(pair, pair, ((1,), (1,)))
        gram_pair = split(gram)
        poly = COEF_B * gram + COEF_C * product(gram_pair, gram_pair, ((1,), (0,)))
        x = COEF_A * x + product(split(poly), pair, ((1,), (0,)))
    update = (scale * x).T.astype(bf16)
    owners = out_ref.shape[0]
    depth = rows // owners
    for c in range(NC):
        for chip in range(owners // NC):
            at = slice((chip * NC + c) * depth, (chip * NC + c + 1) * depth)
            out_ref[c * (owners // NC) + chip, 0] = update[at, :]
            out_ref[c * (owners // NC) + chip, 1] = moment[at, :]


def newton_schulz(moment, owners):
    rows, columns = moment.shape
    return pl.pallas_call(
        newton_schulz_kernel,
        out_shape=jax.ShapeDtypeStruct((owners, 2, rows // owners, columns), bf16),
        compiler_params=pltpu.CompilerParams(vmem_limit_bytes=VMEM),
    )(moment)


def spread_kernel(returned, moment, update, moment_held, update_held, sems):
    half = moment_held.shape[1] // NC
    copies = []
    for c in range(NC):
        for y in range(NY):
            for x in range(NX):
                source = (c * NY + y) * NX + x
                head = c * NY * NX + (RING * x + y if c == 0 else RING * y + x)
                at = slice(head * HD, (head + 1) * HD)
                update_held[:, at] = returned[source, 0]
                moment_held[:, at] = returned[source, 1].astype(f32)
        done = pl.ds(c * half, half)
        for k, (held, out) in enumerate(((moment_held, moment), (update_held, update))):
            copies.append(pltpu.make_async_copy(held.at[:, done], out.at[:, done], sems.at[c, k]))
            copies[-1].start()
    for copy in copies:
        copy.wait()


def spread(returned):
    heads, _, rows, columns = returned.shape
    moment = jax.ShapeDtypeStruct((rows, heads * columns), f32)
    update = jax.ShapeDtypeStruct((rows, heads * columns), bf16)
    hbm = pl.BlockSpec(memory_space=pl.ANY)
    return pl.pallas_call(
        spread_kernel,
        out_shape=(moment, update),
        in_specs=[pl.BlockSpec(memory_space=pltpu.VMEM)],
        out_specs=(hbm, hbm),
        scratch_shapes=[
            pltpu.VMEM(moment.shape, f32),
            pltpu.VMEM(update.shape, bf16),
            pltpu.SemaphoreType.DMA((NC, 2)),
        ],
        compiler_params=pltpu.CompilerParams(vmem_limit_bytes=VMEM),
    )(returned)


def body(latent, latent_grad, row_counts, momentum):
    features = latent.shape[1]
    order = (2, 1, 3)
    tie = lax.optimization_barrier

    early, late = (2,), (1, 3, 0)
    piece_early, mine = column_pieces(latent_grad, [(early, True), (early, False)])
    lat_own, mom_own, mom_other, unit, own_early = first(row_counts, latent, momentum, mine)
    grad_late, own_early = tie((latent_grad, own_early))
    (piece_late,) = column_pieces(grad_late, [(late, True)])
    piece_early, lat_other, mom_other = (
        swap_cores(piece_early), swap_cores(lat_own), swap_cores(mom_other)
    )
    piece_late, piece_early, lat_other, mom_other = tie((piece_late, piece_early, lat_other, mom_other))
    piece_late = swap_cores(piece_late)
    shared = (unit, lat_other, mom_own, mom_other)

    half = features // 2
    upper, lower, whole = (0, half), (half, half), (0, features)
    every, rest, stay = (0, 1, 2, 3), (1, 2, 3), (0,)
    own = {2: own_early}
    two_a, two_b = block(
        own, early, [(2, every, *upper, bf16), (2, every, *lower, bf16)], *shared, piece_early
    )
    lat_late, two_a, two_b = tie((lat_own, two_a, two_b))
    own[1], own[3], own[0] = own_products(lat_late, latent_grad, late)
    one_a, three_b = block(
        own, late, [(1, rest, *upper, bf16), (3, rest, *lower, bf16)], *shared, piece_late
    )
    own[0], one_a, three_b = tie((own[0], one_a, three_b))
    one_b, three_a, one_stay, three_stay, kept_on, kept_stay = block(
        own,
        late,
        [
            (1, rest, *lower, f32),
            (3, rest, *upper, f32),
            (1, stay, *whole, f32),
            (3, stay, *whole, f32),
            (0, rest, *whole, f32),
            (0, stay, *whole, f32),
        ],
        *shared,
        piece_late,
    )
    two_a, two_b = exchange(two_a, 0, 1), exchange(two_b, 0, 3)
    one_a, three_b = exchange(one_a, 0, 1), exchange(three_b, 0, 3)
    three_a = exchange((three_a + two_a[1:].astype(f32)).astype(bf16), 0, 3)
    one_b = exchange((one_b + two_b[1:].astype(f32)).astype(bf16), 0, 1)
    kept_on, one_stay, three_stay = middle(
        kept_on, one_a, three_b, one_stay, three_stay, two_a, two_b
    )
    one_stay, three_stay = exchange(one_stay, 0, 1), exchange(three_stay, 0, 3)

    sums = add_up(kept_on, three_a, one_b)
    got = [exchange(sums[k - 1], 1, k) for k in order]
    head = stay_sum(kept_stay, one_stay, three_stay)
    head = (head + sum(value.astype(f32) for value in got)).astype(bf16)

    pieces = lax.all_to_all(head.reshape(NZ, -1, HD), "z", 0, 0, tiled=True)
    piece = jnp.sum(pieces.astype(f32), axis=0).astype(bf16)
    moment = lax.all_to_all(jnp.broadcast_to(piece, (NZ,) + piece.shape), "z", 0, 0, tiled=True)
    moment = moment.reshape(features, HD)

    outgoing = newton_schulz(moment, NC * NY * NX)
    returned = lax.all_to_all(outgoing, PLANE, 0, 0, tiled=True)
    return tuple(spread(returned))


def solution(mesh):
    fine = Mesh(mesh.devices.reshape(NZ, NY, NX, NC), AXES)
    shard = ("y", "x", "c")
    in_specs = (P(AXES, None), P(AXES, None), P(AXES), P(shard, None))
    out_specs = (P(shard, None), P(shard, None))
    return jax.shard_map(body, mesh=fine, in_specs=in_specs, out_specs=out_specs, check_vma=False)
```
